32 devices in a mesh: fsdp: 4 (over z), ctx: 2 (over x), tp: 4 (over y, core).
Axes of the slice: x: 2, y: 2, z: 4, core: 2. Of those that a mesh axis runs over, the one named last changes fastest.
Arguments:
- hidden_in: bfloat16 [4, 1024, 1024], P('fsdp', 'ctx'), may hold values from -6 to 6
- lengths: int32 [4], P('fsdp'), may hold values from 513 to 1024, as said below
- positions: int32 [4, 1024], P('fsdp', 'ctx'), may hold values from 0 to 4092, as said below
- query_weight: bfloat16 [1024, 1024], P('fsdp', 'tp'), may hold values from -0.1875 to 0.1875
- key_weight: bfloat16 [1024, 512], P('fsdp', 'tp'), may hold values from -0.1875 to 0.1875
- value_weight: bfloat16 [1024, 512], P('fsdp', 'tp'), may hold values from -0.1875 to 0.1875
- output_weight: bfloat16 [1024, 1024], P('tp', 'fsdp'), may hold values from -3 to 3
- gate_weight: bfloat16 [1024, 4608], P('fsdp', 'tp'), may hold values from -0.1875 to 0.1875
- up_weight: bfloat16 [1024, 4608], P('fsdp', 'tp'), may hold values from -0.1875 to 0.1875
- down_weight: bfloat16 [4608, 1024], P('tp', 'fsdp'), may hold values from -0.09375 to 0.09375
- attention_gain: bfloat16 [1024], P('fsdp'), may hold values from 0.099609375 to 1.8984375
- feedforward_gain: bfloat16 [1024], P('fsdp'), may hold values from 0.099609375 to 1.8984375
- query_gain: bfloat16 [64], replicated, may hold values from 0.099609375 to 1.8984375
- key_gain: bfloat16 [64], replicated, may hold values from 0.099609375 to 1.8984375
- cotangent: bfloat16 [4, 1024, 1024], P('fsdp', 'ctx'), may hold values from -6 to 6
Outputs:
- block_out: bfloat16 [4, 1024, 1024], P('fsdp', 'ctx')
- input_grad: float32 [4, 1024, 1024], P('fsdp', 'ctx')
- query_weight_grad: float32 [1024, 1024], P('fsdp', 'tp')
- key_weight_grad: float32 [1024, 512], P('fsdp', 'tp')
- value_weight_grad: float32 [1024, 512], P('fsdp', 'tp')
- output_weight_grad: float32 [1024, 1024], P('tp', 'fsdp')
- gate_weight_grad: float32 [1024, 4608], P('fsdp', 'tp')
- up_weight_grad: float32 [1024, 4608], P('fsdp', 'tp')
- down_weight_grad: float32 [4608, 1024], P('tp', 'fsdp')
- attention_gain_grad: float32 [1024], P('fsdp')
- feedforward_gain_grad: float32 [1024], P('fsdp')
- query_gain_grad: float32 [64], replicated
- key_gain_grad: float32 [64], replicated
- rms_stats: float32 [4], replicated
The draws below stay inside these ranges and needn't reach their ends.
Inputs may be any that keep to these rules, and one draw needn't show every extreme that they name: `lengths`: slots at and after a sequence's length are padding. In every draw one sequence has 1024 valid slots and another 1024 // 2 + 1. Along a sequence positions rise by 1 to 3 from slot to slot; the first lies below 1024.
All inputs are finite; a program needn't handle non-finite values.
Results may differ from the reference program's by a relative error of at most 0.013.
Values may be sent and summed in bfloat16 or wider, within the bound.
No kernel may reach another device: no remote copies, remote signals or barrier semaphores. Data moves between devices by JAX's collectives and lax.ppermute only.
A program may use at most 128 MiB of HBM per device.

```python
import jax
import jax.numpy as jnp
from jax import lax

D = 1024
HEADS = 16
KV_HEADS = 8
HD = 64
FF = 4608
SLOTS = 1024
SEQS = 4


def draw_lengths(key, part):
    key = jax.random.fold_in(key, 11)
    first, second = jax.random.split(key)
    values = jax.random.randint(first, (SEQS,), SLOTS // 2 + 1, SLOTS + 1)
    order = jax.random.permutation(second, SEQS)
    values = values.at[order[0]].set(SLOTS)
    values = values.at[order[1]].set(SLOTS // 2 + 1)
    return values.astype(jnp.int32)


def draw_positions(key, part):
    key = jax.random.fold_in(key, 23)
    first, second, third = jax.random.split(key, 3)
    steps = jax.random.randint(first, (SEQS, SLOTS), 1, 4)
    starts = jax.random.randint(second, (SEQS, 1), 0, SLOTS)
    order = jax.random.permutation(third, SEQS)
    starts = starts.at[order[0], 0].set(0)
    starts = starts.at[order[1], 0].set(SLOTS - 1)
    steps = steps.at[order[1]].set(3)
    return (starts + jnp.cumsum(steps, axis=1) - steps[:, :1]).astype(jnp.int32)


def levels(own_key, extent, cuts, least, largest):
    level = 1.0
    for axis_at, shards_of in cuts:
        heights = jax.random.uniform(jax.random.fold_in(jax.random.fold_in(own_key, 6), axis_at), (shards_of,), jnp.float32, least / len(cuts), largest / len(cuts))
        level = level * jnp.repeat(jnp.exp(heights), extent[axis_at] // shards_of).reshape((-1,) + (1,) * (len(extent) - 1 - axis_at))
    return level


def centred(key, shape, spread, bound, pieces=(), held_as=jnp.bfloat16):
    drawn = jax.random.normal(key, shape, jnp.float32) * spread
    if len(pieces) > 0:
        drawn = levels(key, shape, pieces, -0.22, 0.18) * drawn
    return jnp.clip(drawn, min=-bound, max=bound).astype(held_as)


def setup_inputs(seed: int = 0) -> dict:
    seeds = jax.random.split(jax.random.key(seed), 16)
    return {
        "hidden_in": centred(seeds[0], (SEQS, SLOTS, D), 1.0, 6.0, ((0, 4), (1, 2))),
        "lengths": draw_lengths(jax.random.fold_in(seeds[15], 71), 0),
        "positions": draw_positions(jax.random.fold_in(seeds[15], 71), 0),
        "query_weight": centred(seeds[3], (D, HEADS * HD), D ** -0.5, 0.1875, ((0, 4), (1, 4))),
        "key_weight": centred(seeds[4], (D, KV_HEADS * HD), D ** -0.5, 0.1875, ((0, 4), (1, 4))),
        "value_weight": centred(seeds[5], (D, KV_HEADS * HD), D ** -0.5, 0.1875, ((0, 4), (1, 4))),
        "output_weight": centred(seeds[6], (HEADS * HD, D), (max(D // 256, 1)) ** -0.5, 3.0, ((0, 4), (1, 4))),
        "gate_weight": centred(seeds[7], (D, FF), D ** -0.5, 0.1875, ((0, 4), (1, 4))),
        "up_weight": centred(seeds[8], (D, FF), D ** -0.5, 0.1875, ((0, 4), (1, 4))),
        "down_weight": centred(seeds[9], (FF, D), FF ** -0.5, 0.09375, ((0, 4), (1, 4))),
        "attention_gain": jnp.clip(1.0 + 0.18 * jax.random.normal(seeds[10], (D,), jnp.float32), 0.099609375, 1.8984375).astype(jnp.bfloat16),
        "feedforward_gain": jnp.clip(1.0 + 0.18 * jax.random.normal(seeds[11], (D,), jnp.float32), 0.099609375, 1.8984375).astype(jnp.bfloat16),
        "query_gain": jnp.clip(1.0 + 0.18 * jax.random.normal(seeds[12], (HD,), jnp.float32), 0.099609375, 1.8984375).astype(jnp.bfloat16),
        "key_gain": jnp.clip(1.0 + 0.18 * jax.random.normal(seeds[13], (HD,), jnp.float32), 0.099609375, 1.8984375).astype(jnp.bfloat16),
        "cotangent": centred(seeds[14], (SEQS, SLOTS, D), 1.0, 6.0, ((0, 4), (1, 2))),
    }


@jax.custom_vjp
def low(v):
    return lax.optimization_barrier(v.astype(jnp.bfloat16)).astype(jnp.float32)

@jax.custom_vjp
def low_back(v):
    return v

def low_keep(v):
    return (low(v), None)

def low_pass(kept, grad):
    return (grad,)

def back_keep(v):
    return (v, None)

def back_low(kept, grad):
    return (low(grad),)
low.defvjp(low_keep, low_pass)
low_back.defvjp(back_keep, back_low)
epsilon = 1e-05
rope_base = 1000000.0
highest = lax.Precision.HIGHEST

def product(left, right):
    return jnp.dot(left, right, precision=highest, preferred_element_type=jnp.float32)

def normalize(values, gain):
    inverse = lax.rsqrt(lax.optimization_barrier(jnp.mean(values * values, axis=-1, keepdims=True)) + epsilon)
    return values * inverse * gain

def rotate(values, cosine, sine):
    half = values.shape[-1] // 2
    first = values[..., :half]
    second = values[..., half:]
    return jnp.concatenate([first * cosine - second * sine, second * cosine + first * sine], axis=-1)

def rope_tables(places, head_size):
    freqs = rope_base ** (-2.0 * jnp.arange(head_size // 2, dtype=jnp.float32) / head_size)
    angles = places.astype(jnp.float32)[:, None] * freqs[None, :]
    return (jnp.cos(angles)[:, None, :], jnp.sin(angles)[:, None, :])

def block(inputs, params, valid, cosine, sine):
    query_weight, key_weight, value_weight, output_weight, gate_weight, up_weight, down_weight, attention_gain, feedforward_gain, query_gain, key_gain = params
    slots = inputs.shape[0]
    group = HEADS // KV_HEADS
    normed = low(normalize(inputs, attention_gain))
    query_raw = low_back(product(normed, query_weight)).reshape(slots, HEADS, HD)
    key_raw = low_back(product(normed, key_weight)).reshape(slots, KV_HEADS, HD)
    value_all = low(low_back(product(normed, value_weight))).reshape(slots, KV_HEADS, HD)
    query_all = low(rotate(normalize(query_raw, query_gain), cosine, sine))
    key_all = low(rotate(normalize(key_raw, key_gain), cosine, sine))
    query_grouped = query_all.reshape(slots, KV_HEADS, group, HD)
    scores = jnp.einsum('qkgd,skd->kgqs', query_grouped, key_all, precision=highest) * HD ** (-0.5)
    scores = low_back(scores)
    index = jnp.arange(slots)
    allowed = (index[None, :] <= index[:, None]) & (valid[None, :] > 0)
    probs = low(jax.nn.softmax(jnp.where(allowed, scores, -1e+30), axis=-1))
    mixed = jnp.einsum('kgqs,skd->qkgd', probs, value_all, precision=highest).reshape(slots, HEADS * HD)
    mixed = low(low_back(mixed))
    attention_branch = low_back(product(mixed, output_weight))
    middle = inputs + attention_branch
    normed_two = low(normalize(middle, feedforward_gain))
    gate = low_back(product(normed_two, gate_weight))
    upper = low_back(product(normed_two, up_weight))
    activated = low(jax.nn.silu(gate) * upper)
    feedforward_branch = low_back(product(activated, down_weight))
    output = (middle + feedforward_branch) * valid[:, None]
    return (output, (attention_branch, middle, feedforward_branch))

def reference(hidden_in, lengths, positions, query_weight, key_weight, value_weight, output_weight, gate_weight, up_weight, down_weight, attention_gain, feedforward_gain, query_gain, key_gain, cotangent):
    params = tuple((item.astype(jnp.float32) for item in (query_weight, key_weight, value_weight, output_weight, gate_weight, up_weight, down_weight, attention_gain, feedforward_gain, query_gain, key_gain)))
    zeros = tuple((jnp.zeros_like(item) for item in params))

    def one_sequence(carry, inputs):
        totals, squares = carry
        sequence, length, places, upstream = inputs
        valid = (jnp.arange(SLOTS) < length).astype(jnp.float32)
        cosine, sine = rope_tables(places, HD)
        start = sequence.astype(jnp.float32)

        def run(values, weights):
            return block(values, weights, valid, cosine, sine)
        output, pullback, parts = jax.vjp(run, start, params, has_aux=True)
        input_grad, weight_grads = pullback(upstream.astype(jnp.float32))
        totals = jax.tree.map(lambda left, right: left + right, totals, weight_grads)
        attention_branch, middle, feedforward_branch = parts
        masked = valid[:, None]
        found = jnp.stack([jnp.sum(item * item * masked) for item in (start, attention_branch, middle, feedforward_branch)])
        return ((totals, squares + found), (output.astype(jnp.bfloat16), input_grad))
    (totals, squares), (outputs, input_grads) = lax.scan(one_sequence, (zeros, jnp.zeros((4,), jnp.float32)), (hidden_in, lengths, positions, cotangent))
    count = jnp.sum(lengths).astype(jnp.float32) * D
    stats = jnp.sqrt(squares / count)
    return (outputs, input_grads, totals[0], totals[1], totals[2], totals[3], totals[4], totals[5], totals[6], totals[7], totals[8], totals[9], totals[10], stats)
```

```python
import jax
import jax.numpy as jnp
from jax import lax
from jax.sharding import Mesh, PartitionSpec as P

HD = 64
epsilon = 1e-05
rope_base = 1000000.0
F32 = jnp.float32
BF16 = jnp.bfloat16
PLANE = ("ctx", "y", "core")


def product(left, right):
    return jnp.dot(left, right, preferred_element_type=F32)


def rows_product(left, right):
    return lax.dot_general(left, right, (((0,), (0,)), ((), ())), preferred_element_type=F32)


def cols_product(left, right):
    return lax.dot_general(left, right, (((1,), (1,)), ((), ())), preferred_element_type=F32)


def swap(value, axis):
    return lax.ppermute(value, axis, [(0, 1), (1, 0)])


def halve(value, index, axis):
    size = value.shape[axis] // 2
    return lax.dynamic_slice_in_dim(value, index * size, size, axis)


def in_order(mine, other, index, axis):
    first = jnp.where(index == 0, mine, other)
    second = jnp.where(index == 0, other, mine)
    return jnp.concatenate([first, second], axis)


def sum_scatter(parts):
    width = parts.shape[-1] // 2
    total = parts[0].astype(F32) + swap(parts[1], "core").astype(F32)
    low = total.astype(BF16)
    from_x = swap(low[1, :, :, :width], "ctx").astype(F32)
    from_y = swap(low[:, 1, :, width:], "y").astype(F32)
    left = total[0, :, :, :width] + from_x
    right = total[:, 0, :, width:] + from_y
    left = left[0] + swap(left[1].astype(BF16), "y").astype(F32)
    right = right[0] + swap(right[1].astype(BF16), "ctx").astype(F32)
    return jnp.concatenate([left, right], -1)


def gather_plane(block):
    width = block.shape[-1] // 2
    left, right = block[:, :width], block[:, width:]
    left = jnp.stack([left, swap(left, "ctx")])
    right = jnp.stack([right, swap(right, "y")])
    left = jnp.stack([left, swap(left, "y")], 1)
    right = jnp.stack([right, swap(right, "ctx")], 0)
    here = jnp.concatenate([left, right], -1)
    return jnp.stack([here, swap(here, "core")])


def sum_all(value):
    for axis in ("core", "y", "ctx"):
        value = value + swap(value, axis)
    size = lax.axis_size("fsdp")
    step = 1
    while step < size:
        value = value + lax.ppermute(value, "fsdp", [(i, i ^ step) for i in range(size)])
        step *= 2
    return value


def rotate(values, cosine, sine):
    half = values.shape[-1] // 2
    first = values[..., :half]
    second = values[..., half:]
    return jnp.concatenate([first * cosine - second * sine, second * cosine + first * sine], axis=-1)


def normalize(values, gain):
    inverse = lax.rsqrt(jnp.mean(values * values, axis=-1, keepdims=True) + epsilon)
    return values * inverse * gain


def shards(
    hidden_in,
    lengths,
    positions,
    query_weight,
    key_weight,
    value_weight,
    output_weight,
    gate_weight,
    up_weight,
    down_weight,
    attention_gain,
    feedforward_gain,
    query_gain,
    key_gain,
    cotangent,
):
    ctx, why, core = lax.axis_index("ctx"), lax.axis_index("y"), lax.axis_index("core")
    local, width = hidden_in.shape[1:]
    block = local // 4
    every = 2 * local
    length = lengths[0]

    attention_scale = attention_gain.astype(F32)[:, None]
    feedforward_scale = feedforward_gain.astype(F32)[:, None]
    qkv_own = jnp.concatenate(
        [halve(query_weight, ctx, 1), halve(key_weight, ctx, 1), halve(value_weight, ctx, 1)], 1
    )
    heads = query_weight.shape[1] // 2 // HD
    groups = key_weight.shape[1] // 2 // HD
    group = heads // groups
    wide = qkv_own.shape[1]
    qkv_own = (qkv_own.astype(F32) * attention_scale).astype(BF16)
    attn_own = jnp.concatenate([qkv_own, halve(output_weight, ctx, 0).T], 1)
    hidden = gate_weight.shape[1] // 2
    gu_own = jnp.concatenate([halve(gate_weight, ctx, 1), halve(up_weight, ctx, 1)], 1)
    gu_own = (gu_own.astype(F32) * feedforward_scale).astype(BF16)
    ff_own = jnp.concatenate([gu_own, halve(down_weight, ctx, 0).T], 1)
    attn_full = lax.all_gather(attn_own, "fsdp", axis=0, tiled=True)
    ff_own, attn_full = lax.optimization_barrier((ff_own, attn_full))
    ff_full = lax.all_gather(ff_own, "fsdp", axis=0, tiled=True)
    qkv_w, out_w = attn_full[:, :wide], attn_full[:, wide:]
    gate_w, up_w, down_w = ff_full[:, :hidden], ff_full[:, hidden : 2 * hidden], ff_full[:, 2 * hidden :]

    def relative(array):
        pieces = [
            lax.dynamic_slice_in_dim(array, (2 * (why ^ yy) + (core ^ kk)) * block, block)
            for kk in range(2)
            for yy in range(2)
        ]
        return jnp.concatenate(pieces)

    def both_halves(own):
        near, far = own[:local // 2], own[local // 2 :]
        other = swap(near, "ctx")
        return jnp.concatenate([near, other, far, swap(other, "core")])

    inputs = relative(hidden_in[0]).astype(F32)
    inverse = lax.rsqrt(jnp.mean(inputs * inputs, axis=-1, keepdims=True) + epsilon)
    unit = both_halves((inputs * inverse).astype(BF16))
    inputs, inverse = inputs[:block], inverse[:block]

    def slots_of(xx):
        steps = jnp.arange(block, dtype=jnp.int32)
        return [
            ((ctx ^ xx) * 4 + 2 * (why ^ yy) + (core ^ kk)) * block + steps for kk in range(2) for yy in range(2)
        ]

    near_slots, far_slots = slots_of(0), slots_of(1)
    slots = jnp.concatenate(near_slots[:2] + far_slots[:2] + near_slots[2:] + far_slots[2:])
    places = relative(positions[0])
    other_places = swap(places, "ctx")
    places = jnp.concatenate(
        [places[: local // 2], other_places[: local // 2], places[local // 2 :], other_places[local // 2 :]]
    )
    freqs = rope_base ** (-2.0 * jnp.arange(HD // 2, dtype=F32) / HD)
    angles = places.astype(F32)[:, None] * freqs[None, :]
    cosine, sine = jnp.cos(angles)[:, None, :], jnp.sin(angles)[:, None, :]
    allowed = (slots[None, :] <= slots[:, None]) & (slots[None, :] < length)
    valid = (slots[:block] < length).astype(F32)[:, None]
    upstream_rel = relative(cotangent[0])
    upstream = upstream_rel[:block].astype(F32) * valid
    branch_low = both_halves(upstream_rel)
    branch_low = jnp.where((slots < length)[:, None], branch_low, jnp.zeros_like(branch_low))

    qkv_raw = product(unit, qkv_w)
    scale = HD ** (-0.5)

    def shape_heads(query_lin, key_lin, query_scale, key_scale):
        query_rot = rotate(normalize(query_lin.reshape(every, heads, HD), query_scale), cosine, sine)
        key_rot = rotate(normalize(key_lin.reshape(every, groups, HD), key_scale), cosine, sine)
        return (query_rot, key_rot)

    (query_rot, key_rot), heads_pull = jax.vjp(
        shape_heads,
        qkv_raw[:, : heads * HD],
        qkv_raw[:, heads * HD : (heads + groups) * HD],
        query_gain.astype(F32),
        key_gain.astype(F32),
    )
    query_low = query_rot.astype(BF16).reshape(every, groups, group, HD)
    key_low = key_rot.astype(BF16)
    value_low = qkv_raw[:, (heads + groups) * HD :].astype(BF16).reshape(every, groups, HD)
    scores = jnp.einsum("qkgd,skd->kgqs", query_low, key_low, preferred_element_type=F32) * scale
    probs = jax.nn.softmax(jnp.where(allowed, scores, -1e30), axis=-1)
    probs_low = probs.astype(BF16)
    mixed = jnp.einsum("kgqs,skd->qkgd", probs_low, value_low, preferred_element_type=F32)
    mixed_low = mixed.reshape(every, heads * HD).astype(BF16)

    def split(array):
        return array.astype(BF16).reshape(2, 2, 2, block, width)

    attention_branch = sum_scatter(split(cols_product(mixed_low, out_w)))
    middle = inputs + attention_branch
    inverse_two = lax.rsqrt(jnp.mean(middle * middle, axis=-1, keepdims=True) + epsilon)
    unit_two_own = middle * inverse_two
    unit_two = gather_plane(unit_two_own.astype(BF16)).reshape(every, width)

    gate = product(unit_two, gate_w)
    upper = product(unit_two, up_w)
    sigmoid = 1.0 / (1.0 + jnp.exp(-gate))
    silu = gate * sigmoid
    activated = (silu * upper).astype(BF16)
    activated_grad = product(branch_low, down_w)
    gate_low = (activated_grad * upper * (sigmoid * (1.0 + gate * (1.0 - sigmoid)))).astype(BF16)
    upper_low = (activated_grad * silu).astype(BF16)
    second = sum_scatter(split(cols_product(gate_low, gate_w) + cols_product(upper_low, up_w)))
    ff_grad = jnp.concatenate(
        [
            rows_product(unit_two, gate_low).astype(BF16),
            rows_product(unit_two, upper_low).astype(BF16),
            rows_product(branch_low, activated).astype(BF16),
        ],
        1,
    )
    ff_share = lax.psum_scatter(ff_grad, "fsdp", scatter_dimension=0, tiled=True)
    middle_grad = upstream + inverse_two * (
        second - unit_two_own * jnp.mean(second * unit_two_own, axis=-1, keepdims=True)
    )
    feedforward_gain_part = jnp.sum(second * unit_two_own, axis=0)
    attention_low = gather_plane(middle_grad.astype(BF16)).reshape(every, width)
    feedforward_branch = sum_scatter(split(cols_product(activated, down_w)))
    output = ((middle + feedforward_branch) * valid).astype(BF16)
    block_rows = lax.all_gather(output, ("y", "core"), axis=0, tiled=True)

    output_grad = rows_product(attention_low, mixed_low)
    mixed_grad = product(attention_low, out_w).astype(BF16).reshape(every, groups, group, HD)
    value_grad = jnp.einsum("kgqs,qkgd->skd", probs_low, mixed_grad, preferred_element_type=F32)
    probs_grad = jnp.einsum("qkgd,skd->kgqs", mixed_grad, value_low, preferred_element_type=F32)
    score_grad = (probs * (probs_grad - jnp.sum(probs * probs_grad, axis=-1, keepdims=True))).astype(BF16)
    query_rot_grad = jnp.einsum("kgqs,skd->qkgd", score_grad, key_low, preferred_element_type=F32) * scale
    key_rot_grad = jnp.einsum("kgqs,qkgd->skd", score_grad, query_low, preferred_element_type=F32) * scale
    query_back, key_back, query_gain_part, key_gain_part = heads_pull(
        (query_rot_grad.reshape(every, heads, HD), key_rot_grad)
    )
    qkv_grad = jnp.concatenate([query_back, key_back, value_grad.reshape(every, groups * HD)], 1).astype(BF16)
    first = sum_scatter(split(cols_product(qkv_grad, qkv_w)))
    attn_grad = jnp.concatenate([rows_product(unit, qkv_grad), output_grad], 1).astype(BF16)
    attn_share = lax.psum_scatter(attn_grad, "fsdp", scatter_dimension=0, tiled=True)
    unit_own = inputs * inverse
    input_grad = middle_grad + inverse * (first - unit_own * jnp.mean(first * unit_own, axis=-1, keepdims=True))
    attention_gain_part = jnp.sum(first * unit_own, axis=0)
    input_rows = lax.all_gather(input_grad.astype(BF16), ("y", "core"), axis=0, tiled=True).astype(F32)

    squares = jnp.stack(
        [jnp.sum(item * item * valid) for item in (inputs, attention_branch, middle, feedforward_branch)]
    )
    small = jnp.concatenate(
        [
            attention_gain_part,
            feedforward_gain_part,
            query_gain_part,
            key_gain_part,
            squares,
            jnp.sum(valid)[None],
            jnp.zeros((123,), F32),
        ]
    )
    small = sum_all(small.reshape(-1, 128)).reshape(-1)
    own_gain = attention_gain.shape[0]
    shard = lax.axis_index("fsdp") * own_gain
    attention_share = lax.dynamic_slice_in_dim(small, shard, own_gain) / attention_scale[:, 0]
    feedforward_share = lax.dynamic_slice_in_dim(small, width + shard, own_gain) / feedforward_scale[:, 0]
    rest = small[2 * width :]
    query_gain_total, key_gain_total = rest[:HD], rest[HD : 2 * HD]
    stats = jnp.sqrt(rest[2 * HD : 2 * HD + 4] / (rest[2 * HD + 4] * width))

    attn_other = swap(attn_share, "ctx")
    ff_other = swap(ff_share, "ctx")

    def whole(mine, other, start, size, axis, gain):
        mine = mine[:, start : start + size].astype(F32)
        other = other[:, start : start + size].astype(F32)
        if gain is not None:
            mine, other = mine * gain, other * gain
        if axis == 0:
            mine, other = mine.T, other.T
        return in_order(mine, other, ctx, axis)

    query_cols, key_cols = heads * HD, groups * HD
    return (
        block_rows[None],
        input_rows[None],
        whole(attn_share, attn_other, 0, query_cols, 1, attention_scale),
        whole(attn_share, attn_other, query_cols, key_cols, 1, attention_scale),
        whole(attn_share, attn_other, query_cols + key_cols, key_cols, 1, attention_scale),
        whole(attn_share, attn_other, wide, query_cols, 0, None),
        whole(ff_share, ff_other, 0, hidden, 1, feedforward_scale),
        whole(ff_share, ff_other, hidden, hidden, 1, feedforward_scale),
        whole(ff_share, ff_other, 2 * hidden, hidden, 0, None),
        attention_share,
        feedforward_share,
        query_gain_total,
        key_gain_total,
        stats,
    )


def solution(mesh):
    fsdp, ctx, tp = (mesh.shape[axis] for axis in ("fsdp", "ctx", "tp"))
    assert ctx == 2 and tp == 4
    plane = Mesh(mesh.devices.reshape(fsdp, 2, 2, 2), ("fsdp", "ctx", "y", "core"))
    tp = ("y", "core")
    in_specs = (
        P("fsdp", "ctx", None),
        P("fsdp"),
        P("fsdp", "ctx"),
        P("fsdp", tp),
        P("fsdp", tp),
        P("fsdp", tp),
        P(tp, "fsdp"),
        P("fsdp", tp),
        P("fsdp", tp),
        P(tp, "fsdp"),
        P("fsdp"),
        P("fsdp"),
        P(),
        P(),
        P("fsdp", "ctx", None),
    )
    out_specs = (
        P("fsdp", "ctx", None),
        P("fsdp", "ctx", None),
        P("fsdp", tp),
        P("fsdp", tp),
        P("fsdp", tp),
        P(tp, "fsdp"),
        P("fsdp", tp),
        P("fsdp", tp),
        P(tp, "fsdp"),
        P("fsdp"),
        P("fsdp"),
        P(),
        P(),
        P(),
    )
    return jax.shard_map(shards, mesh=plane, in_specs=in_specs, out_specs=out_specs, check_vma=False)
```

```python
import jax
import jax.numpy as jnp
from jax import lax
from jax.experimental import pallas as pl
from jax.experimental.pallas import tpu as pltpu
from jax.sharding import Mesh, PartitionSpec as P

HD = 64
epsilon = 1e-05
rope_base = 1000000.0
F32 = jnp.float32
BF16 = jnp.bfloat16
PLANE = ("ctx", "y", "core")


def swap(value, axis):
    return lax.ppermute(value, axis, [(0, 1), (1, 0)])


def halve(value, index, axis):
    size = value.shape[axis] // 2
    return lax.dynamic_slice_in_dim(value, index * size, size, axis)


def in_order(mine, other, index, axis):
    first = jnp.where(index == 0, mine, other)
    second = jnp.where(index == 0, other, mine)
    return jnp.concatenate([first, second], axis)


def sum_scatter(near, far):
    block, width = near.shape[0] // 4, near.shape[1] // 2
    total = near.astype(F32) + swap(far, "core").astype(F32)
    total = total.reshape(2, 2, block, -1)
    low = total.astype(BF16)
    from_x = swap(low[1, :, :, :width], "ctx").astype(F32)
    from_y = swap(low[:, 1, :, width:], "y").astype(F32)
    left = total[0, :, :, :width] + from_x
    right = total[:, 0, :, width:] + from_y
    left = left[0] + swap(left[1].astype(BF16), "y").astype(F32)
    right = right[0] + swap(right[1].astype(BF16), "ctx").astype(F32)
    return jnp.concatenate([left, right], -1)


def gather_plane(block):
    width = block.shape[-1] // 2
    left, right = block[:, :width], block[:, width:]
    left = jnp.stack([left, swap(left, "ctx")])
    right = jnp.stack([right, swap(right, "y")])
    left = jnp.stack([left, swap(left, "y")], 1)
    right = jnp.stack([right, swap(right, "ctx")], 0)
    near = jnp.concatenate([left, right], -1).reshape(-1, 2 * width)
    return near, swap(near, "core")


def gather_shards(own):
    size = lax.axis_size("fsdp")
    parts = [own]
    for step in range(1, size):
        parts.append(lax.ppermute(own, "fsdp", [(i, i ^ step) for i in range(size)]))
    return parts


def region(flag, work, *args):
    shapes = jax.eval_shape(work, *args)
    return lax.cond(flag, work, lambda *_: jax.tree.map(lambda x: jnp.zeros(x.shape, x.dtype), shapes), *args)


def gather_rows(block, why, core):
    pair = jnp.stack([block, swap(block, "y")])
    four = jnp.concatenate([pair, swap(pair, "core")])
    pieces = [lax.dynamic_slice_in_dim(four, 2 * (core ^ (i % 2)) + (why ^ (i // 2)), 1)[0] for i in range(4)]
    return jnp.concatenate(pieces)


def sum_all(value):
    for axis in ("core", "y", "ctx"):
        value = value + swap(value, axis)
    size = lax.axis_size("fsdp")
    step = 1
    while step < size:
        value = value + lax.ppermute(value, "fsdp", [(i, i ^ step) for i in range(size)])
        step *= 2
    return value


def lanes(shape):
    return lax.broadcasted_iota(jnp.int32, shape, len(shape) - 1)


def nt(left, right):
    return lax.dot_general(left, right, (((1,), (1,)), ((), ())), preferred_element_type=F32)


def tn(left, right):
    return lax.dot_general(left, right, (((0,), (0,)), ((), ())), preferred_element_type=F32)


def nn(left, right):
    return lax.dot_general(left, right, (((1,), (0,)), ((), ())), preferred_element_type=F32)


def half_sums(values, low):
    first = jnp.sum(jnp.where(low, values, 0.0), axis=-1, keepdims=True)
    second = jnp.sum(jnp.where(low, 0.0, values), axis=-1, keepdims=True)
    return first, second


def turned(values):
    return jnp.where(lanes(values.shape) % HD < HD // 2, pltpu.roll(values, 96, 1), pltpu.roll(values, 32, 1))


def rows_of(own, kk, xx, yy, block):
    return pl.multiple_of((own ^ (xx * 4 + yy * 2 + kk)) * block, block)


def attention_forward(
    index, h0, h1, h2, h3, cosine, sine, query_gain, key_gain, *rest
):
    *parts, w, gains, part_low, part_high, unit, query, key, value, raw, mixed, mixed_rel, inverse = rest
    own, length = index[0], index[1]
    if len(parts) > 2:
        rows = w.shape[0] // len(parts)
        for at, part in enumerate(parts):
            to = pl.multiple_of((index[2] ^ at) * rows, rows)
            w[pl.ds(to, rows), :] = part[:rows, :]
            gains[:, pl.ds(to, rows)] = part[rows : rows + 16, :rows].astype(F32)[:8]
    else:
        w[...] = parts[0][...]
        gains[...] = parts[1][...]
    gain = gains[0:1, :]
    pair = h0.shape[0]
    block = pair // 2
    low = lanes((pair, 2 * HD)) < HD
    for at, h in enumerate((h0, h1, h2, h3)):
        kk, xx = divmod(at, 2)
        here = slice(at * pair, (at + 1) * pair)
        x = h[...].astype(F32)
        r = lax.rsqrt(jnp.mean(x * x, axis=-1, keepdims=True) + epsilon)
        u = (x * r * gain).astype(BF16)
        unit[here, :] = u
        lin = nn(u, w[:, : 4 * HD])
        raw[here, :] = lin
        q, kv = lin[:, : 2 * HD], lin[:, 2 * HD :]
        one, two = half_sums(q * q, low)
        r = jnp.where(low, lax.rsqrt(one / HD + epsilon), lax.rsqrt(two / HD + epsilon))
        y = q * r * query_gain[...]
        c, s = cosine[here, :], sine[here, :]
        q = (y * c + turned(y) * s).astype(BF16).astype(F32) * HD**-0.5
        one, _ = half_sums(kv * kv, low)
        y = kv * lax.rsqrt(one / HD + epsilon) * key_gain[...]
        kv = jnp.where(low, y * c + turned(y) * s, kv)
        other = pltpu.roll(kv, HD, 1)
        k, v = jnp.where(low, kv, other), jnp.where(low, other, kv)
        for yy in range(2):
            to = rows_of(own, kk, xx, yy, block)
            some = slice(yy * block, (yy + 1) * block)
            query[pl.ds(to, block), :] = q[some].astype(BF16)
            key[pl.ds(to, block), :] = k[some].astype(BF16)
            value[pl.ds(to, block), :] = v[some].astype(BF16)
    for at in range(4):
        here = slice(at * pair, (at + 1) * pair)
        n = (at + 1) * pair
        q = query[here, :]
        q = jnp.concatenate([jnp.where(low, q, jnp.zeros_like(q)), jnp.where(low, jnp.zeros_like(q), q)])
        e = masked_exp(nt(q, key[:n, :]), at, pair, length)
        total = 1.0 / jnp.sum(e, axis=-1, keepdims=True)
        o = nn((e * total).astype(BF16), value[:n, :])
        mixed[here, :] = jnp.where(low, o[:pair], o[pair:])
        inverse[here, :] = jnp.where(low, total[:pair], total[pair:])
    for at in range(4):
        kk, xx = divmod(at, 2)
        pieces = [mixed[pl.ds(rows_of(own, kk, xx, yy, block), block), :] for yy in range(2)]
        m = jnp.concatenate(pieces).astype(BF16)
        mixed_rel[at * pair : (at + 1) * pair, :] = m
        part = nt(m, w[:, 4 * HD :]).astype(BF16)
        to = part_high if kk else part_low
        to[xx * pair : (xx + 1) * pair, :] = part


def masked_exp(scores, at, pair, length):
    n = scores.shape[1]
    columns = lax.broadcasted_iota(jnp.int32, scores.shape, 1)
    rows = lax.broadcasted_iota(jnp.int32, scores.shape, 0) % pair + at * pair
    return jnp.where((columns <= rows) & (columns < length), jnp.exp(scores), 0.0)


def attention_backward(
    index, a_low, a_high, w, query, key, value, raw, mixed, inverse, cosine, sine, query_gain, key_gain,
    first_low, first_high, back, gains, down, dq, dk, dv,
):
    own, length = index[0], index[1]
    pair = a_low.shape[0] // 2
    block = pair // 2
    low = lanes((pair, 2 * HD)) < HD
    for at in range(4):
        kk, xx = divmod(at, 2)
        a = a_high if kk else a_low
        m = nn(a[xx * pair : (xx + 1) * pair, :], w[:, 4 * HD :]).astype(BF16)
        for yy in range(2):
            down[pl.ds(rows_of(own, kk, xx, yy, block), block), :] = m[yy * block : (yy + 1) * block]
    dk[...] = jnp.zeros_like(dk)
    dv[...] = jnp.zeros_like(dv)
    for at in range(4):
        here = slice(at * pair, (at + 1) * pair)
        n = (at + 1) * pair
        q, m = query[here, :], down[here, :]
        zero = jnp.zeros_like(q)
        q = jnp.concatenate([jnp.where(low, q, zero), jnp.where(low, zero, q)])
        one, two = half_sums(m.astype(F32) * mixed[here, :], low)
        drop = jnp.concatenate([one, two])
        m = jnp.concatenate([jnp.where(low, m, zero), jnp.where(low, zero, m)])
        total = jnp.concatenate([inverse[here, 0:1], inverse[here, HD : HD + 1]])
        p = masked_exp(nt(q, key[:n, :]), at, pair, length) * total
        g = (p * (nt(m, value[:n, :]) - drop)).astype(BF16)
        dv[:n, :] += tn(p.astype(BF16), m)
        dk[:n, :] += tn(g, q)
        o = nn(g, key[:n, :])
        dq[here, :] = jnp.where(low, o[:pair], o[pair:]) * HD**-0.5
    query_sum = jnp.zeros((1, 2 * HD), F32)
    key_sum = jnp.zeros((1, 2 * HD), F32)
    for at in range(4):
        kk, xx = divmod(at, 2)
        here = slice(at * pair, (at + 1) * pair)
        spots = [pl.ds(rows_of(own, kk, xx, yy, block), block) for yy in range(2)]
        c, s = cosine[here, :], sine[here, :]
        x, kv = raw[here, : 2 * HD], raw[here, 2 * HD :]
        one, two = half_sums(x * x, low)
        r = jnp.where(low, lax.rsqrt(one / HD + epsilon), lax.rsqrt(two / HD + epsilon))
        z = x * r
        y = jnp.concatenate([dq[spot, :] for spot in spots])
        y = y * c - turned(y) * s
        query_sum += jnp.sum(y * z, axis=0, keepdims=True)
        y = y * query_gain[...]
        one, two = half_sums(y * z, low)
        x = r * (y - z * jnp.where(low, one / HD, two / HD))
        one, _ = half_sums(kv * kv, low)
        r = lax.rsqrt(one / HD + epsilon)
        z = kv * r
        y = jnp.concatenate([dk[spot, :] for spot in spots])
        y = y + pltpu.roll(y, HD, 1)
        y = y * c - turned(y) * s
        key_sum += jnp.sum(y * z, axis=0, keepdims=True)
        y = y * key_gain[...]
        one, _ = half_sums(y * z, low)
        v = jnp.concatenate([dv[spot, :] for spot in spots])
        kv = jnp.where(low, r * (y - z * (one / HD)), v + pltpu.roll(v, HD, 1))
        lin = jnp.concatenate([x, kv], axis=1).astype(BF16)
        back[here, :] = lin
        part = nt(lin, w[:, : 4 * HD]).astype(BF16)
        to = first_high if kk else first_low
        to[xx * pair : (xx + 1) * pair, :] = part
    gains[0:1, :] = query_sum
    gains[1:2, :] = key_sum


def feed_forward(
    index, x_low, x_high, b0, b1, b2, b3, f, second_low, second_high, gate_up, activated, branch, unit
):
    own, length = index[0], index[1]
    pair = b0.shape[0]
    block, four = pair // 2, 2 * pair
    main = gate_up.shape[1] // 2 // 128 * 128
    both = 2 * main
    wide = both + 128
    low = lanes((four, 128)) < HD
    rows = lax.broadcasted_iota(jnp.int32, (pair, 1), 0)
    for kk, (x, bs, to) in enumerate(((x_low, (b0, b1), second_low), (x_high, (b2, b3), second_high))):
        here = slice(kk * four, (kk + 1) * four)
        x = x[...]
        unit[here, :] = x
        for xx, b in enumerate(bs):
            starts = jnp.where(rows < block, own ^ (xx * 4 + kk), own ^ (xx * 4 + 2 + kk)) * block
            b = b[...]
            b = jnp.where(starts + rows % block < length, b, jnp.zeros_like(b))
            branch[kk * four + xx * pair : kk * four + (xx + 1) * pair, :] = b
        gu = nn(x, f[:, :wide])
        back = nn(branch[here, :], f[:, wide:])
        tail = gu[:, both:]
        gate = jnp.concatenate([gu[:, :main], tail], 1)
        upper = jnp.concatenate([gu[:, main:both], pltpu.roll(tail, HD, 1)], 1)
        sigmoid = 1.0 / (1.0 + jnp.exp(-gate))
        silu = gate * sigmoid
        act = silu * upper
        gate_back = back * upper * (sigmoid + silu * (1.0 - sigmoid))
        upper_back = back * silu
        activated[here, :main] = act[:, :main].astype(BF16)
        activated[here, main:] = jnp.where(low, act[:, main:], 0.0).astype(BF16)
        mix = jnp.where(low, gate_back[:, main:], pltpu.roll(upper_back[:, main:], HD, 1))
        gu = jnp.concatenate([gate_back[:, :main], upper_back[:, :main], mix], 1).astype(BF16)
        gate_up[here, :] = gu
        to[...] = nt(gu, f[:, :wide]).astype(BF16)


def pack_attention(index, query, key, value, output, gains, out):
    rows = query.shape[0]
    wide = query.shape[1] // 2
    for half in range(2):

        @pl.when(index[3] == half)
        def _():
            out[:rows, :wide] = query[:, half * wide : (half + 1) * wide]
            low = lanes((rows, 2 * HD)) < HD
            k, v = key[...].astype(F32), value[...].astype(F32)
            if half:
                kv = jnp.where(low, pltpu.roll(k, HD, 1), v)
            else:
                kv = jnp.where(low, k, pltpu.roll(v, HD, 1))
            out[:rows, wide : wide + 2 * HD] = kv.astype(BF16)
            out[:rows, wide + 2 * HD :] = output[half * wide : (half + 1) * wide, :].astype(F32).T.astype(BF16)

    out[rows:, :rows] = gains[...]


def unpack_attention(index, mine, other, query, key, value, output):
    wide = query.shape[1] // 2
    low = lanes((mine.shape[0], 2 * HD)) < HD
    for half in range(2):

        @pl.when(index[3] == half)
        def _():
            first, second = (other, mine) if half else (mine, other)
            for at, part in enumerate((first, second)):
                query[:, at * wide : (at + 1) * wide] = part[:, :wide].astype(F32)
                output[at * wide : (at + 1) * wide, :] = part[:, wide + 2 * HD :].astype(F32).T
            one = first[:, wide : wide + 2 * HD].astype(F32)
            two = second[:, wide : wide + 2 * HD].astype(F32)
            key[...] = jnp.where(low, one, pltpu.roll(two, HD, 1))
            value[...] = jnp.where(low, pltpu.roll(one, HD, 1), two)


def unpack_feed_forward(index, mine, other, gate, upper, down):
    rows, hidden = mine.shape[0], gate.shape[1] // 2
    main = hidden // 128 * 128
    both, wide = 2 * main, 2 * hidden
    low = lanes((rows, 128)) < HD
    for half in range(2):

        @pl.when(index[3] == half)
        def _():
            first, second = (other, mine) if half else (mine, other)
            for at, to in enumerate((gate, upper)):
                to[:, :main] = first[:, at * main : (at + 1) * main].astype(F32)
                one = first[:, both : both + 128].astype(F32)
                two = second[:, both : both + 128].astype(F32)
                if at:
                    one = pltpu.roll(one, HD, 1)
                else:
                    two = pltpu.roll(two, HD, 1)
                end = second[:, at * main : (at + 1) * main].astype(F32)
                end = pltpu.roll(jnp.concatenate([end, jnp.zeros((rows, 128), F32)], 1), HD, 1)
                to[:, main : main + 128] = jnp.where(low, one, end[:, :128])
                to[:, main + 128 : 2 * main] = end[:, 128:main]
                to[:, 2 * main :] = jnp.where(low, end[:, main:], two)
            for at, part in enumerate((first, second)):
                turned = part[:, wide:].astype(F32).T
                down[at * hidden : (at + 1) * hidden, :] = turned[:hidden]


def call(kernel, outs, args, scratch=()):
    vmem = pl.BlockSpec(memory_space=pltpu.VMEM)
    return pl.pallas_call(
        kernel,
        out_shape=[jax.ShapeDtypeStruct(shape, kind) for shape, kind in outs],
        in_specs=[pl.BlockSpec(memory_space=pltpu.SMEM) if arg.dtype == jnp.int32 else vmem for arg in args],
        out_specs=[vmem] * len(outs),
        scratch_shapes=[pltpu.VMEM(shape, kind) for shape, kind in scratch],
        compiler_params=pltpu.CompilerParams(vmem_limit_bytes=48 * 2**20),
        cost_estimate=pl.CostEstimate(flops=1000, bytes_accessed=1000, transcendentals=0),
    )(*args)


def down_product(activated, f, part_low, part_high):
    wide = f.shape[1] - activated.shape[1]
    half = part_low.shape[0]
    part_low[...] = nt(activated[:half, :], f[:, wide:]).astype(BF16)
    part_high[...] = nt(activated[half:, :], f[:, wide:]).astype(BF16)


def feed_forward_weights(unit, branch, gate_up, activated, out):
    wide = gate_up.shape[1]
    step = out.shape[0] // 2
    for row in range(0, out.shape[0], step):
        here = slice(row, row + step)
        out[here, :wide] = tn(unit[:, here], gate_up[...]).astype(BF16)
        out[here, wide:] = tn(branch[:, here], activated[...]).astype(BF16)


def attention_weights(unit, back, a_low, a_high, mixed_rel, w, gains, out, gain_out):
    wide = back.shape[1]
    half = a_low.shape[0]
    step = 256
    for row in range(0, out.shape[0], step):
        here = slice(row, row + step)
        grad = tn(unit[:, here], back[...])
        out[here, :wide] = grad.astype(BF16)
        grad = jnp.sum(grad * w[here, :wide].astype(F32), axis=1, keepdims=True)
        gain_out[:, here] = jnp.broadcast_to(grad, (step, 128)).T[:8] / gains[0:1, here]
        o = tn(a_low[:, here], mixed_rel[:half, :]) + tn(a_high[:, here], mixed_rel[half:, :])
        out[here, wide:] = o.astype(BF16)


def shards(
    hidden_in,
    lengths,
    positions,
    query_weight,
    key_weight,
    value_weight,
    output_weight,
    gate_weight,
    up_weight,
    down_weight,
    attention_gain,
    feedforward_gain,
    query_gain,
    key_gain,
    cotangent,
):
    ctx, why, core = lax.axis_index("ctx"), lax.axis_index("y"), lax.axis_index("core")
    local, width = hidden_in.shape[1:]
    block = local // 4
    every = 2 * local
    length = lengths[0]

    heads = query_weight.shape[1] // 2 // HD
    groups = key_weight.shape[1] // 2 // HD
    group = heads // groups
    wide = (heads + 2 * groups) * HD
    rows = query_weight.shape[0]
    gains = jnp.pad(jnp.stack([attention_gain, feedforward_gain]), ((0, 14), (0, 0)))
    own = ctx * 4 + why * 2 + core
    shard = lax.axis_index("fsdp")
    index = jnp.stack([own, length, shard, ctx]).astype(jnp.int32)
    (attn_parts,) = call(
        pack_attention,
        [((rows + 16, wide + heads * HD), BF16)],
        (index, query_weight, key_weight, value_weight, output_weight, gains),
    )
    size = lax.axis_size("fsdp")
    if size > 4:
        attn_parts = lax.all_gather(attn_parts, "fsdp")
        gains = attn_parts[:, rows : rows + 8, :rows].astype(F32).transpose(1, 0, 2).reshape(8, -1)
        attn_parts = [attn_parts[:, :rows].reshape(-1, wide + heads * HD), gains]
    else:
        attn_parts = gather_shards(attn_parts)
    hidden = gate_weight.shape[1] // 2
    main = hidden // 128 * 128
    assert hidden - main == HD and 2 * heads * HD == 256 and groups == 1
    gate_own, up_own = halve(gate_weight, ctx, 1), halve(up_weight, ctx, 1)
    gu_own = jnp.concatenate([gate_own[:, :main], up_own[:, :main], gate_own[:, main:], up_own[:, main:]], 1)
    down_own = jnp.concatenate([halve(down_weight, ctx, 0).T, jnp.zeros((rows, HD), BF16)], 1)

    def relative(array, kk):
        pieces = [
            lax.dynamic_slice_in_dim(array, (2 * (why ^ yy) + (core ^ kk)) * block, block) for yy in range(2)
        ]
        return jnp.concatenate(pieces)

    def both_halves(array):
        near = relative(array, 0)
        other = swap(near, "ctx")
        return near, other, relative(array, 1), swap(other, "core")

    flag = length > 0

    def prepare(hidden_in, positions):
        hidden_rel = both_halves(hidden_in[0])
        places = jnp.stack([relative(positions[0], kk) for kk in range(2)])
        places = jnp.stack([places, swap(places, "ctx")], 1).reshape(-1)
        freqs = rope_base ** (-2.0 * jnp.arange(HD // 2, dtype=F32) / HD)
        angles = places.astype(F32)[:, None] * jnp.tile(freqs, 4)[None, :]
        cosine = jnp.cos(angles)
        sine = jnp.sin(angles) * jnp.where(jnp.arange(2 * HD) % HD < HD // 2, -1.0, 1.0)[None, :]
        return hidden_rel, cosine, sine

    hidden_rel, cosine, sine = region(flag, prepare, hidden_in, positions)
    attn_parts, hidden_rel = lax.optimization_barrier((attn_parts, hidden_rel))
    cotangent_rel, _ = lax.optimization_barrier((relative(cotangent[0], 0), hidden_rel[1]))
    cotangent_x = swap(cotangent_rel, "ctx")
    ff_own, _ = lax.optimization_barrier((jnp.concatenate([gu_own, down_own], 1), hidden_rel[1]))
    ff_full = lax.all_gather(ff_own, "fsdp", axis=0, tiled=True)
    inputs = hidden_rel[0][:block].astype(F32)
    inverse = lax.rsqrt(jnp.mean(inputs * inputs, axis=-1, keepdims=True) + epsilon)

    valid = (own * block + jnp.arange(block, dtype=jnp.int32) < length).astype(F32)[:, None]
    upstream = cotangent_rel[:block].astype(F32) * valid

    query_row = jnp.tile(query_gain.astype(F32), 2)[None]
    key_row = jnp.concatenate([key_gain.astype(F32), jnp.ones((HD,), F32)])[None]
    lane = 2 * HD
    attn_full, gains, near, far, unit, query, key, value, raw, mixed, mixed_rel, total = call(
        attention_forward,
        [((width, wide + 2 * HD), BF16), ((8, width), F32)]
        + [((every // 2, width), BF16)] * 2
        + [((every, width), BF16)]
        + [((every, lane), BF16)] * 3
        + [((every, 2 * lane), F32), ((every, lane), F32), ((every, lane), BF16), ((every, lane), F32)],
        (index, *hidden_rel, cosine, sine, query_row, key_row, *attn_parts),
    )
    attention_scale, feedforward_scale = gains[0:1], gains[1:2]
    kept = (attn_full, query, key, value, raw, mixed, total, cosine, sine, query_row, key_row)
    near, cotangent_x = lax.optimization_barrier((near, cotangent_x))

    def middle_of(near, far, inputs, feedforward_scale, cotangent_x, cotangent_in):
        attention_branch = sum_scatter(near, far)
        middle = inputs + attention_branch
        inverse_two = lax.rsqrt(jnp.mean(middle * middle, axis=-1, keepdims=True) + epsilon)
        unit_two_own = middle * inverse_two
        unit_near, unit_far = gather_plane((unit_two_own * feedforward_scale).astype(BF16))
        cotangent_far = relative(cotangent_in[0], 1), swap(cotangent_x, "core")
        return attention_branch, middle, inverse_two, unit_near, unit_far, cotangent_far

    attention_branch, middle, inverse_two, unit_near, unit_far, cotangent_far = region(
        flag, middle_of, near, far, inputs, feedforward_scale, cotangent_x, cotangent
    )
    unit_two_own = middle * inverse_two

    tail = main + 2 * HD
    near, far, gate_up, activated, branch_low, unit_two = call(
        feed_forward,
        [((every // 2, width), BF16)] * 2
        + [((every, 2 * hidden), BF16), ((every, tail), BF16), ((every, width), BF16), ((every, width), BF16)],
        (index, unit_near, unit_far, cotangent_rel, cotangent_x, *cotangent_far, ff_full),
    )
    (ff_grad,) = call(
        feed_forward_weights, [((width, 2 * hidden + tail), BF16)], (unit_two, branch_low, gate_up, activated)
    )
    ff_grad, near = lax.optimization_barrier((ff_grad, near))
    ff_share = lax.psum_scatter(ff_grad, "fsdp", scatter_dimension=0, tiled=True)

    def turn(near, far, activated, ff_full, unit_two_own, inverse_two, upstream, middle, kept, unit, mixed_rel):
        second = sum_scatter(near, far)
        feedforward_gain_part = jnp.sum(second * unit_two_own, axis=0)
        second = second * feedforward_scale
        middle_grad = upstream + inverse_two * (
            second - unit_two_own * jnp.mean(second * unit_two_own, axis=-1, keepdims=True)
        )
        attention_near, attention_far = gather_plane(middle_grad.astype(BF16))
        near, far = call(down_product, [((every // 2, width), BF16)] * 2, (activated, ff_full))
        feedforward_branch = sum_scatter(near, far)
        output = ((middle + feedforward_branch) * valid).astype(BF16)
        block_rows = gather_rows(output, why, core)
        near, far, back, gain_sums = call(
            attention_backward,
            [((every // 2, width), BF16)] * 2 + [((every, 2 * lane), BF16), ((8, lane), F32)],
            (index, attention_near, attention_far, *kept),
            [((every, lane), BF16)] + [((every, lane), F32)] * 3,
        )
        attn_grad, attention_gain_part = call(
            attention_weights,
            [((width, 3 * lane), BF16), ((8, width), F32)],
            (unit, back, attention_near, attention_far, mixed_rel, kept[0], gains),
        )
        feedforward_gain_part = jnp.stack([feedforward_gain_part, attention_gain_part[0]])
        return near, far, attn_grad, gain_sums, block_rows, feedforward_branch, middle_grad, feedforward_gain_part

    near, far, attn_grad, gain_sums, block_rows, feedforward_branch, middle_grad, gain_parts = region(
        flag,
        turn,
        near,
        far,
        activated,
        ff_full,
        unit_two_own,
        inverse_two,
        upstream,
        middle,
        kept,
        unit,
        mixed_rel,
    )
    attn_share = lax.psum_scatter(attn_grad, "fsdp", scatter_dimension=0, tiled=True)
    ff_share, near = lax.optimization_barrier((ff_share, near))
    ff_other = swap(ff_share, "ctx")

    def sums(near, far, inputs, gain_parts, gain_sums, branches):
        squares = jnp.stack([jnp.sum(item * item * valid) for item in (inputs, *branches)])
        small = jnp.concatenate(
            [
                gain_parts.reshape(-1),
                gain_sums[0, :HD] + gain_sums[0, HD:],
                gain_sums[1, :HD],
                squares,
                jnp.sum(valid)[None],
                jnp.zeros((123,), F32),
            ]
        )
        return sum_scatter(near, far), sum_all(small.reshape(-1, 128)).reshape(-1)

    first, small = region(
        flag, sums, near, far, inputs, gain_parts, gain_sums, (attention_branch, middle, feedforward_branch)
    )
    first, attn_share, ff_other = lax.optimization_barrier((first, attn_share, ff_other))
    attn_other = swap(attn_share, "ctx")

    def finish(first, middle_grad, inputs, inverse, attention_scale, index, ff_share, ff_other):
        unit_own = inputs * inverse
        first = first * attention_scale
        input_grad = middle_grad + inverse * (
            first - unit_own * jnp.mean(first * unit_own, axis=-1, keepdims=True)
        )
        ff_grads = call(
            unpack_feed_forward,
            [((rows, 2 * hidden), F32)] * 2 + [((2 * hidden, rows), F32)],
            (index, ff_share, ff_other),
        )
        return gather_rows(input_grad.astype(BF16), why, core).astype(F32), ff_grads

    input_rows, ff_grads = region(
        flag, finish, first, middle_grad, inputs, inverse, attention_scale, index, ff_share, ff_other
    )
    attn_other, input_rows = lax.optimization_barrier((attn_other, input_rows))
    attn_grads = call(
        unpack_attention,
        [((rows, 2 * heads * HD), F32)] + [((rows, 2 * groups * HD), F32)] * 2 + [((2 * heads * HD, rows), F32)],
        (index, attn_share, attn_other),
    )
    own_gain = attention_gain.shape[0]
    shard = shard * own_gain
    feedforward_share = lax.dynamic_slice_in_dim(small, shard, own_gain)
    attention_share = lax.dynamic_slice_in_dim(small, width + shard, own_gain)
    rest = small[2 * width :]
    query_gain_total, key_gain_total = rest[:HD], rest[HD : 2 * HD]
    stats = jnp.sqrt(rest[2 * HD : 2 * HD + 4] / (rest[2 * HD + 4] * width))

    return (
        block_rows[None],
        input_rows[None],
        *attn_grads,
        *ff_grads,
        attention_share,
        feedforward_share,
        query_gain_total,
        key_gain_total,
        stats,
    )


def solution(mesh):
    fsdp, ctx, tp = (mesh.shape[axis] for axis in ("fsdp", "ctx", "tp"))
    assert ctx == 2 and tp == 4
    plane = Mesh(mesh.devices.reshape(fsdp, 2, 2, 2), ("fsdp", "ctx", "y", "core"))
    tp = ("y", "core")
    in_specs = (
        P("fsdp", "ctx", None),
        P("fsdp"),
        P("fsdp", "ctx"),
        P("fsdp", tp),
        P("fsdp", tp),
        P("fsdp", tp),
        P(tp, "fsdp"),
        P("fsdp", tp),
        P("fsdp", tp),
        P(tp, "fsdp"),
        P("fsdp"),
        P("fsdp"),
        P(),
        P(),
        P("fsdp", "ctx", None),
    )
    out_specs = (
        P("fsdp", "ctx", None),
        P("fsdp", "ctx", None),
        P("fsdp", tp),
        P("fsdp", tp),
        P("fsdp", tp),
        P(tp, "fsdp"),
        P("fsdp", tp),
        P("fsdp", tp),
        P(tp, "fsdp"),
        P("fsdp"),
        P("fsdp"),
        P(),
        P(),
        P(),
    )
    return jax.shard_map(shards, mesh=plane, in_specs=in_specs, out_specs=out_specs, check_vma=False)
```

```python
import jax
import jax.numpy as jnp
from jax import lax
from jax.experimental import pallas as pl
from jax.experimental.pallas import tpu as pltpu
from jax.sharding import Mesh, PartitionSpec as P

HD = 64
epsilon = 1e-05
rope_base = 1000000.0
F32 = jnp.float32
BF16 = jnp.bfloat16
PLANE = ("ctx", "y", "core")


def swap(value, axis):
    return lax.ppermute(value, axis, [(0, 1), (1, 0)])


def halve(value, index, axis):
    size = value.shape[axis] // 2
    return lax.dynamic_slice_in_dim(value, index * size, size, axis)


def in_order(mine, other, index, axis):
    first = jnp.where(index == 0, mine, other)
    second = jnp.where(index == 0, other, mine)
    return jnp.concatenate([first, second], axis)


def sum_scatter(near, far):
    block, width = near.shape[0] // 4, near.shape[1] // 2
    total = near.astype(F32) + swap(far, "core").astype(F32)
    total = total.reshape(2, 2, block, -1)
    low = total.astype(BF16)
    from_x = swap(low[1, :, :, :width], "ctx").astype(F32)
    from_y = swap(low[:, 1, :, width:], "y").astype(F32)
    left = total[0, :, :, :width] + from_x
    right = total[:, 0, :, width:] + from_y
    left = left[0] + swap(left[1].astype(BF16), "y").astype(F32)
    right = right[0] + swap(right[1].astype(BF16), "ctx").astype(F32)
    return jnp.concatenate([left, right], -1)


def hop(value, axis, step=1):
    size = lax.axis_size(axis)
    return lax.ppermute(value, axis, [(i, i ^ step) for i in range(size)])


def last_sums(near, far, small):
    block, width = near.shape[0] // 4, near.shape[1] // 2
    far, more = together(swap(far, "core"), hop(small, "core"))
    total = (near.astype(F32) + far.astype(F32)).reshape(2, 2, block, -1)
    small = small + more
    low = total.astype(BF16)
    from_x = swap(low[1, :, :, :width], "ctx")
    from_y = swap(low[:, 1, :, width:], "y")
    from_x, from_y, more = together(from_x, from_y, hop(small, "ctx"))
    left = total[0, :, :, :width] + from_x.astype(F32)
    right = total[:, 0, :, width:] + from_y.astype(F32)
    small = small + more
    from_y = swap(left[1].astype(BF16), "y")
    from_x = swap(right[1].astype(BF16), "ctx")
    from_x, from_y, more = together(from_x, from_y, hop(small, "y"))
    return jnp.concatenate([left[0] + from_y.astype(F32), right[0] + from_x.astype(F32)], -1), small + more


def gather_plane(block, beside=None):
    width = block.shape[-1] // 2
    left, right = block[:, :width], block[:, width:]
    left_x, right_y = swap(left, "ctx"), swap(right, "y")
    if beside is not None:
        beside, left_x, right_y = together(swap(beside, "core"), left_x, right_y)
    left = jnp.stack([left, left_x])
    right = jnp.stack([right, right_y])
    left = jnp.stack([left, swap(left, "y")], 1)
    right = jnp.stack([right, swap(right, "ctx")], 0)
    near = jnp.concatenate([left, right], -1).reshape(-1, 2 * width)
    return near, swap(near, "core"), beside


def near_shards():
    return lax.axis_size("fsdp") <= 4


def direct(pieces):
    size = lax.axis_size("fsdp")
    return [
        piece if step == 0 else lax.ppermute(piece, "fsdp", [(i, i ^ step) for i in range(size)])
        for step, piece in enumerate(pieces)
    ]


def onward(value):
    size = lax.axis_size("fsdp")
    return lax.ppermute(value, "fsdp", [(i, (i + 1) % size) for i in range(size)])


def together(*values):
    return lax.optimization_barrier(values)


def region(flag, work, *args):
    shapes = jax.eval_shape(work, *args)
    return lax.cond(flag, work, lambda *_: jax.tree.map(lambda x: jnp.zeros(x.shape, x.dtype), shapes), *args)


def lanes(shape):
    return lax.broadcasted_iota(jnp.int32, shape, len(shape) - 1)


def nt(left, right):
    return lax.dot_general(left, right, (((1,), (1,)), ((), ())), preferred_element_type=F32)


def tn(left, right):
    return lax.dot_general(left, right, (((0,), (0,)), ((), ())), preferred_element_type=F32)


def nn(left, right):
    return lax.dot_general(left, right, (((1,), (0,)), ((), ())), preferred_element_type=F32)


def half_sums(values, low):
    first = jnp.sum(jnp.where(low, values, 0.0), axis=-1, keepdims=True)
    second = jnp.sum(jnp.where(low, 0.0, values), axis=-1, keepdims=True)
    return first, second


def turned(values):
    return jnp.where(lanes(values.shape) % HD < HD // 2, pltpu.roll(values, 96, 1), pltpu.roll(values, 32, 1))


def rows_of(own, kk, xx, yy, block):
    return pl.multiple_of((own ^ (xx * 4 + yy * 2 + kk)) * block, block)


def attention_forward(
    index, h0, h1, h2, h3, cosine, sine, query_gain, key_gain, *rest
):
    *parts, w, gains, part_low, part_high, unit, query, key, value, raw, mixed, mixed_rel, inverse = rest
    own, length = index[0], index[1]
    if len(parts) > 2:
        rows = w.shape[0] // len(parts)
        for at, part in enumerate(parts):
            to = pl.multiple_of((index[2] ^ at) * rows, rows)
            w[pl.ds(to, rows), :] = part[:rows, :]
            gains[:, pl.ds(to, rows)] = part[rows : rows + 16, :rows].astype(F32)[:8]
    else:
        w[...] = parts[0][...]
        gains[...] = parts[1][...]
    gain = gains[0:1, :]
    pair = h0.shape[0]
    block = pair // 2
    low = lanes((pair, 2 * HD)) < HD
    for at, h in enumerate((h0, h1, h2, h3)):
        kk, xx = divmod(at, 2)
        here = slice(at * pair, (at + 1) * pair)
        x = h[...].astype(F32)
        r = lax.rsqrt(jnp.mean(x * x, axis=-1, keepdims=True) + epsilon)
        u = (x * r * gain).astype(BF16)
        unit[here, :] = u
        lin = nn(u, w[:, : 4 * HD])
        raw[here, :] = lin
        q, kv = lin[:, : 2 * HD], lin[:, 2 * HD :]
        one, two = half_sums(q * q, low)
        r = jnp.where(low, lax.rsqrt(one / HD + epsilon), lax.rsqrt(two / HD + epsilon))
        y = q * r * query_gain[...]
        c, s = cosine[here, :], sine[here, :]
        q = (y * c + turned(y) * s).astype(BF16).astype(F32) * HD**-0.5
        one, _ = half_sums(kv * kv, low)
        y = kv * lax.rsqrt(one / HD + epsilon) * key_gain[...]
        kv = jnp.where(low, y * c + turned(y) * s, kv)
        other = pltpu.roll(kv, HD, 1)
        k, v = jnp.where(low, kv, other), jnp.where(low, other, kv)
        for yy in range(2):
            to = rows_of(own, kk, xx, yy, block)
            some = slice(yy * block, (yy + 1) * block)
            query[pl.ds(to, block), :] = q[some].astype(BF16)
            key[pl.ds(to, block), :] = k[some].astype(BF16)
            value[pl.ds(to, block), :] = v[some].astype(BF16)
    for at in range(4):
        here = slice(at * pair, (at + 1) * pair)
        n = (at + 1) * pair
        q = query[here, :]
        q = jnp.concatenate([jnp.where(low, q, jnp.zeros_like(q)), jnp.where(low, jnp.zeros_like(q), q)])
        e = masked_exp(nt(q, key[:n, :]), at, pair, length)
        total = 1.0 / jnp.sum(e, axis=-1, keepdims=True)
        o = nn((e * total).astype(BF16), value[:n, :])
        mixed[here, :] = jnp.where(low, o[:pair], o[pair:])
        inverse[here, :] = jnp.where(low, total[:pair], total[pair:])
    for at in range(4):
        kk, xx = divmod(at, 2)
        pieces = [mixed[pl.ds(rows_of(own, kk, xx, yy, block), block), :] for yy in range(2)]
        m = jnp.concatenate(pieces).astype(BF16)
        mixed_rel[at * pair : (at + 1) * pair, :] = m
        part = nt(m, w[:, 4 * HD :]).astype(BF16)
        to = part_high if kk else part_low
        to[xx * pair : (xx + 1) * pair, :] = part


def masked_exp(scores, at, pair, length):
    n = scores.shape[1]
    columns = lax.broadcasted_iota(jnp.int32, scores.shape, 1)
    rows = lax.broadcasted_iota(jnp.int32, scores.shape, 0) % pair + at * pair
    return jnp.where((columns <= rows) & (columns < length), jnp.exp(scores), 0.0)


def attention_backward(
    index, a_low, a_high, w, query, key, value, raw, mixed, inverse, cosine, sine, query_gain, key_gain,
    first_low, first_high, back, gains, down, dq, dk, dv,
):
    own, length = index[0], index[1]
    pair = a_low.shape[0] // 2
    block = pair // 2
    low = lanes((pair, 2 * HD)) < HD
    for at in range(4):
        kk, xx = divmod(at, 2)
        a = a_high if kk else a_low
        m = nn(a[xx * pair : (xx + 1) * pair, :], w[:, 4 * HD :]).astype(BF16)
        for yy in range(2):
            down[pl.ds(rows_of(own, kk, xx, yy, block), block), :] = m[yy * block : (yy + 1) * block]
    dk[...] = jnp.zeros_like(dk)
    dv[...] = jnp.zeros_like(dv)
    for at in range(4):
        here = slice(at * pair, (at + 1) * pair)
        n = (at + 1) * pair
        q, m = query[here, :], down[here, :]
        zero = jnp.zeros_like(q)
        q = jnp.concatenate([jnp.where(low, q, zero), jnp.where(low, zero, q)])
        one, two = half_sums(m.astype(F32) * mixed[here, :], low)
        drop = jnp.concatenate([one, two])
        m = jnp.concatenate([jnp.where(low, m, zero), jnp.where(low, zero, m)])
        total = jnp.concatenate([inverse[here, 0:1], inverse[here, HD : HD + 1]])
        p = masked_exp(nt(q, key[:n, :]), at, pair, length) * total
        g = (p * (nt(m, value[:n, :]) - drop)).astype(BF16)
        dv[:n, :] += tn(p.astype(BF16), m)
        dk[:n, :] += tn(g, q)
        o = nn(g, key[:n, :])
        dq[here, :] = jnp.where(low, o[:pair], o[pair:]) * HD**-0.5
    query_sum = jnp.zeros((1, 2 * HD), F32)
    key_sum = jnp.zeros((1, 2 * HD), F32)
    for at in range(4):
        kk, xx = divmod(at, 2)
        here = slice(at * pair, (at + 1) * pair)
        spots = [pl.ds(rows_of(own, kk, xx, yy, block), block) for yy in range(2)]
        c, s = cosine[here, :], sine[here, :]
        x, kv = raw[here, : 2 * HD], raw[here, 2 * HD :]
        one, two = half_sums(x * x, low)
        r = jnp.where(low, lax.rsqrt(one / HD + epsilon), lax.rsqrt(two / HD + epsilon))
        z = x * r
        y = jnp.concatenate([dq[spot, :] for spot in spots])
        y = y * c - turned(y) * s
        query_sum += jnp.sum(y * z, axis=0, keepdims=True)
        y = y * query_gain[...]
        one, two = half_sums(y * z, low)
        x = r * (y - z * jnp.where(low, one / HD, two / HD))
        one, _ = half_sums(kv * kv, low)
        r = lax.rsqrt(one / HD + epsilon)
        z = kv * r
        y = jnp.concatenate([dk[spot, :] for spot in spots])
        y = y + pltpu.roll(y, HD, 1)
        y = y * c - turned(y) * s
        key_sum += jnp.sum(y * z, axis=0, keepdims=True)
        y = y * key_gain[...]
        one, _ = half_sums(y * z, low)
        v = jnp.concatenate([dv[spot, :] for spot in spots])
        kv = jnp.where(low, r * (y - z * (one / HD)), v + pltpu.roll(v, HD, 1))
        lin = jnp.concatenate([x, kv], axis=1).astype(BF16)
        back[here, :] = lin
        part = nt(lin, w[:, : 4 * HD]).astype(BF16)
        to = first_high if kk else first_low
        to[xx * pair : (xx + 1) * pair, :] = part
    gains[0:1, :] = query_sum
    gains[1:2, :] = key_sum


def activated_gradient(index, b0, b1, b2, b3, *rest):
    *parts, down_w, back = rest
    own, length = index[0], index[1]
    count, rows = len(parts), parts[0].shape[0]
    for at, part in enumerate(parts):
        to = pl.multiple_of((index[2] + count - at) % count * rows, rows)
        down_w[pl.ds(to, rows), :] = part[...]
    pair = b0.shape[0]
    block = pair // 2
    row = lax.broadcasted_iota(jnp.int32, (pair, 1), 0)
    for at, b in enumerate((b0, b1, b2, b3)):
        kk, xx = divmod(at, 2)
        ok = (own ^ (kk + 4 * xx + jnp.where(row >= block, 2, 0))) * block + row % block < length
        back[at * pair : (at + 1) * pair, :] = jnp.where(ok, nn(b[...], down_w[...]), 0.0)


def feed_forward(index, x_low, x_high, b0, b1, b2, b3, back_all, gu_w, second_low, second_high, grad, activated, gate_up):
    own, length = index[0], index[1]
    width = x_low.shape[1]
    pair = b0.shape[0]
    block, four = pair // 2, 2 * pair
    main = gate_up.shape[1] // 2 // 128 * 128
    both = 2 * main
    wide = both + 128
    low = lanes((four, 128)) < HD
    row = lax.broadcasted_iota(jnp.int32, (four, 1), 0)
    bs = (b0, b1, b2, b3)
    for kk, (x, to) in enumerate(((x_low, second_low), (x_high, second_high))):
        here = slice(kk * four, (kk + 1) * four)
        start = own ^ (kk + jnp.where(row >= pair, 4, 0) + jnp.where(row % pair >= block, 2, 0))
        ok = start * block + row % block < length
        gu = nn(x[...], gu_w[...])
        back = back_all[here, :]
        tail = gu[:, both:]
        gate = jnp.concatenate([gu[:, :main], tail], 1)
        upper = jnp.concatenate([gu[:, main:both], pltpu.roll(tail, HD, 1)], 1)
        sigmoid = 1.0 / (1.0 + jnp.exp(-gate))
        silu = gate * sigmoid
        act = jnp.where(ok, silu * upper, 0.0)
        gate_back = back * upper * (sigmoid + silu * (1.0 - sigmoid))
        upper_back = back * silu
        activated[here, :main] = act[:, :main].astype(BF16)
        activated[here, main:] = jnp.where(low, act[:, main:], 0.0).astype(BF16)
        mix = jnp.where(low, gate_back[:, main:], pltpu.roll(upper_back[:, main:], HD, 1))
        gate_up[here, :main] = gate_back[:, :main].astype(BF16)
        gate_up[here, main:both] = upper_back[:, :main].astype(BF16)
        gate_up[here, both:] = mix.astype(BF16)
        to[...] = nt(gate_up[here, :], gu_w[...]).astype(BF16)
    step = width // 2
    for row in range(0, width, step):
        here = slice(row, row + step)
        out = tn(x_low[:, here], gate_up[:four, :]) + tn(x_high[:, here], gate_up[four:, :])
        grad[here, :wide] = out.astype(BF16)
        out = tn(b0[:, here], activated[:pair, :])
        for piece in range(1, 4):
            out += tn(bs[piece][:, here], activated[piece * pair : (piece + 1) * pair, :])
        grad[here, wide:] = out.astype(BF16)


def down_product(index, activated, down_w, branch_low, branch_high):
    four = branch_low.shape[0]
    branch_low[...] = nt(activated[:four, :], down_w[...]).astype(BF16)
    branch_high[...] = nt(activated[four:, :], down_w[...]).astype(BF16)


def small_sums(index, inputs, middle, branch, second, inverse, gain, attention_sums, head_sums, out):
    own, length = index[0], index[1]
    block, width = inputs.shape
    row = lax.broadcasted_iota(jnp.int32, (block, 1), 0)
    valid = (own * block + row < length).astype(F32)
    x, m = inputs[...], middle[...]
    feedforward_sums = jnp.sum(second[...] * (m * inverse[...]), axis=0, keepdims=True)
    for at in range(width // 128):
        here = slice(at * 128, (at + 1) * 128)
        out[at : at + 1, :] = feedforward_sums[:, here]
        out[width // 128 + at : width // 128 + at + 1, :] = attention_sums[0:1, here]
    lane = lanes((1, 128))
    q = head_sums[0:1, :] + pltpu.roll(head_sums[0:1, :], HD, 1)
    out[16:17, :] = jnp.where(lane < HD, q, pltpu.roll(head_sums[1:2, :], HD, 1))
    line = jnp.where(lane == 4, jnp.sum(valid), 0.0)
    for at, item in enumerate((x, m - x, m, branch[...])):
        line = jnp.where(lane == at, jnp.sum(item * item * valid), line)
    out[17:18, :] = line
    out[18:, :] = jnp.zeros((out.shape[0] - 18, 128), F32)


def attention_weights(index, unit, back, a_low, a_high, mixed_rel, w, gains, out, gain_out):
    wide = back.shape[1]
    half = a_low.shape[0]
    step = 256
    for row in range(0, out.shape[0], step):
        here = slice(row, row + step)
        grad = tn(unit[:, here], back[...])
        out[here, :wide] = grad.astype(BF16)
        grad = jnp.sum(grad * w[here, :wide].astype(F32), axis=1, keepdims=True)
        gain_out[:, here] = jnp.broadcast_to(grad, (step, 128)).T[:8] / gains[0:1, here]
        o = tn(a_low[:, here], mixed_rel[:half, :]) + tn(a_high[:, here], mixed_rel[half:, :])
        out[here, wide:] = o.astype(BF16)


def fetch(sources, targets, sems):
    copies = [pltpu.make_async_copy(one, two, sems.at[at]) for at, (one, two) in enumerate(zip(sources, targets))]
    for copy in copies:
        copy.start()
    return copies


def halves(own, source, targets, sems, base):
    block = targets[0].shape[0] // 2
    copies = []
    for kk, target in enumerate(targets):
        for yy in range(2):
            start = pl.multiple_of(((own ^ (2 * yy + kk)) & 3) * block, block)
            to = target.at[pl.ds(yy * block, block)]
            copies.append(pltpu.make_async_copy(source.at[0, pl.ds(start, block)], to, sems.at[base + len(copies)]))
    for copy in copies:
        copy.start()
    return copies


def prelude(
    index, query_from, key_from, value_from, output_from, one_from, two_from, hidden,
    out, hidden_near, hidden_far,
    query, key, value, output, one_gain, two_gain, sems,
):
    copies = fetch(
        (query_from, key_from, value_from, output_from, one_from, two_from),
        (query, key, value, output, one_gain, two_gain),
        sems,
    )
    late = halves(index[0], hidden, (hidden_near, hidden_far), sems, len(copies))
    for copy in copies:
        copy.wait()
    rows = query.shape[0]
    wide = query.shape[1] // 2
    for half in range(2):

        @pl.when(index[3] == half)
        def _():
            out[:rows, :wide] = query[:, half * wide : (half + 1) * wide]
            low = lanes((rows, 2 * HD)) < HD
            k, v = key[...].astype(F32), value[...].astype(F32)
            if half:
                kv = jnp.where(low, pltpu.roll(k, HD, 1), v)
            else:
                kv = jnp.where(low, k, pltpu.roll(v, HD, 1))
            out[:rows, wide : wide + 2 * HD] = kv.astype(BF16)
            out[:rows, wide + 2 * HD :] = output[half * wide : (half + 1) * wide, :].astype(F32).T.astype(BF16)

    one, two = one_gain[...].astype(F32)[None], two_gain[...].astype(F32)[None]
    first = lax.broadcasted_iota(jnp.int32, (16, rows), 0) == 0
    out[rows:, :rows] = jnp.where(first, one, two).astype(BF16)
    out[rows:, rows:] = jnp.zeros((16, out.shape[1] - rows), BF16)
    for copy in late:
        copy.wait()


def pack_feed_forward(index, *rest):
    cotangent, out, down_out, cotangent_near, cotangent_far, gate, upper, down, sems = rest[3:]
    copies = fetch(rest[:3], (gate, upper, down), sems)
    late = halves(index[0], cotangent, (cotangent_near, cotangent_far), sems, len(copies))
    for copy in copies:
        copy.wait()
    rows, hidden = gate.shape[0], gate.shape[1] // 2
    main = hidden // 128 * 128
    both, wide = 2 * main, 2 * hidden
    low = lanes((rows, 128)) < HD
    for half in range(2):

        @pl.when(index[3] == half)
        def _():
            tails = []
            for at, part in enumerate((gate, upper)):
                if half:
                    part = pltpu.roll(part[:, main:].astype(F32), main + HD, 1)
                else:
                    part = part[:, : main + 128].astype(F32)
                out[:, at * main : (at + 1) * main] = part[:, :main].astype(BF16)
                tails.append(part[:, main:])
            out[:, both:wide] = jnp.where(low, tails[0], pltpu.roll(tails[1], HD, 1)).astype(BF16)
            turned = down[half * hidden : (half + 1) * hidden, :].astype(F32)
            turned = jnp.concatenate([turned, jnp.zeros((HD, rows), F32)]).T
            down_out[...] = turned.astype(BF16)
    for copy in late:
        copy.wait()


def unpack_attention(index, mine, other, query, key, value, output):
    wide = query.shape[1] // 2
    low = lanes((mine.shape[0], 2 * HD)) < HD
    for half in range(2):

        @pl.when(index[3] == half)
        def _():
            first, second = (other, mine) if half else (mine, other)
            for at, part in enumerate((first, second)):
                query[:, at * wide : (at + 1) * wide] = part[:, :wide].astype(F32)
                output[at * wide : (at + 1) * wide, :] = part[:, wide + 2 * HD :].astype(F32).T
            one = first[:, wide : wide + 2 * HD].astype(F32)
            two = second[:, wide : wide + 2 * HD].astype(F32)
            key[...] = jnp.where(low, one, pltpu.roll(two, HD, 1))
            value[...] = jnp.where(low, pltpu.roll(one, HD, 1), two)


def unpack_feed_forward(index, mine, other, gate, upper, down):
    rows, hidden = mine.shape[0], gate.shape[1] // 2
    main = hidden // 128 * 128
    both, wide = 2 * main, 2 * hidden
    low = lanes((rows, 128)) < HD
    for half in range(2):

        @pl.when(index[3] == half)
        def _():
            first, second = (other, mine) if half else (mine, other)
            for at, to in enumerate((gate, upper)):
                to[:, :main] = first[:, at * main : (at + 1) * main].astype(F32)
                one = first[:, both : both + 128].astype(F32)
                two = second[:, both : both + 128].astype(F32)
                if at:
                    one = pltpu.roll(one, HD, 1)
                else:
                    two = pltpu.roll(two, HD, 1)
                end = second[:, at * main : (at + 1) * main].astype(F32)
                end = pltpu.roll(jnp.concatenate([end, jnp.zeros((rows, 128), F32)], 1), HD, 1)
                to[:, main : main + 128] = jnp.where(low, one, end[:, :128])
                to[:, main + 128 : 2 * main] = end[:, 128:main]
                to[:, 2 * main :] = jnp.where(low, end[:, main:], two)
            for at, part in enumerate((first, second)):
                turned = part[:, wide:].astype(F32).T
                down[at * hidden : (at + 1) * hidden, :] = turned[:hidden]


def unpack_rows(index, near, far, rows):
    block = near.shape[1]
    for kk, part in enumerate((near, far)):
        for yy in range(2):
            to = pl.multiple_of(((index[0] ^ (2 * yy + kk)) & 3) * block, block)
            rows[pl.ds(to, block), :] = part[yy].astype(rows.dtype)


def call(kernel, outs, args, scratch=(), limit=48, fetched=0, cost=0):
    vmem, hbm = pl.BlockSpec(memory_space=pltpu.VMEM), pl.BlockSpec(memory_space=pl.ANY)
    kinds = [
        pl.BlockSpec(memory_space=pltpu.SMEM)
        if arg.dtype == jnp.int32
        else hbm
        if fetched
        else vmem
        for arg in args
    ]
    scratch = [pltpu.VMEM(shape, kind) for shape, kind in scratch]
    if fetched:
        scratch += [pltpu.VMEM(arg.shape, arg.dtype) for arg in args[1 : 1 + fetched]]
        scratch += [pltpu.SemaphoreType.DMA((fetched + 4,))]
    return pl.pallas_call(
        kernel,
        out_shape=[jax.ShapeDtypeStruct(shape, kind) for shape, kind in outs],
        in_specs=kinds,
        out_specs=[vmem] * len(outs),
        scratch_shapes=scratch,
        compiler_params=pltpu.CompilerParams(vmem_limit_bytes=limit * 2**20),
        cost_estimate=pl.CostEstimate(flops=1000 + cost * 10**9, bytes_accessed=1000, transcendentals=0),
    )(*args)


def shards(
    hidden_in,
    lengths,
    positions,
    query_weight,
    key_weight,
    value_weight,
    output_weight,
    gate_weight,
    up_weight,
    down_weight,
    attention_gain,
    feedforward_gain,
    query_gain,
    key_gain,
    cotangent,
):
    ctx, why, core = lax.axis_index("ctx"), lax.axis_index("y"), lax.axis_index("core")
    local, width = hidden_in.shape[1:]
    block = local // 4
    every = 2 * local
    length = lengths[0]

    heads = query_weight.shape[1] // 2 // HD
    groups = key_weight.shape[1] // 2 // HD
    lane = 2 * HD
    wide = (heads + 2 * groups) * HD
    rows = query_weight.shape[0]
    hidden = gate_weight.shape[1] // 2
    main = hidden // 128 * 128
    assert hidden - main == HD and heads * HD == lane and groups == 1
    pack = 2 * hidden + main + lane
    own = ctx * 4 + why * 2 + core
    shard = lax.axis_index("fsdp")
    size = lax.axis_size("fsdp")
    index = jnp.stack([own, length, shard, ctx]).astype(jnp.int32)
    flag = length > 0

    attn_own, hidden_near, hidden_far = call(
        prelude,
        [((rows + 16, wide + lane), BF16)] + [((local // 2, width), BF16)] * 2,
        (
            index,
            query_weight,
            key_weight,
            value_weight,
            output_weight,
            attention_gain,
            feedforward_gain,
            hidden_in,
        ),
        limit=60,
        fetched=6,
    )
    hidden_other = swap(hidden_near, "ctx")
    if near_shards():
        attn_parts = direct([attn_own] * size)
    else:
        attn_parts = lax.all_gather(attn_own, "fsdp")
        gains = attn_parts[:, rows : rows + 8, :rows].astype(F32).transpose(1, 0, 2).reshape(8, -1)
        attn_parts = [attn_parts[:, :rows].reshape(-1, wide + lane), gains]

    def prepare(positions, gate_weight, up_weight, down_weight, cotangent):
        gu_own, down_own, *cotangent_rel = call(
            pack_feed_forward,
            [((rows, 2 * hidden), BF16), ((rows, main + lane), BF16)] + [((local // 2, width), BF16)] * 2,
            (index, gate_weight, up_weight, down_weight, cotangent),
            limit=60,
            fetched=3,
        )
        pieces = [
            lax.dynamic_slice_in_dim(positions[0], (2 * (why ^ yy) + (core ^ kk)) * block, block)
            for kk in range(2)
            for yy in range(2)
        ]
        places = jnp.concatenate(pieces).reshape(2, -1)
        places = jnp.stack([places, swap(places, "ctx")], 1).reshape(-1)
        freqs = rope_base ** (-2.0 * jnp.arange(HD // 2, dtype=F32) / HD)
        angles = places.astype(F32)[:, None] * jnp.tile(freqs, 4)[None, :]
        cosine = jnp.cos(angles)
        sine = jnp.sin(angles) * jnp.where(jnp.arange(lane) % HD < HD // 2, -1.0, 1.0)[None, :]
        return gu_own, down_own, cosine, sine, *cotangent_rel

    gu_own, down_own, cosine, sine, cotangent_near, cotangent_far = region(
        flag, prepare, positions, gate_weight, up_weight, down_weight, cotangent
    )
    attn_parts, gu_own, hidden_other, cotangent_near = together(attn_parts, gu_own, hidden_other, cotangent_near)
    gu_full = lax.all_gather(gu_own, "fsdp", axis=0, tiled=True)
    down_parts = [down_own]
    if near_shards():
        down_parts.append(onward(down_own))
    else:
        down_parts = [lax.all_gather(down_own, "fsdp", axis=0, tiled=True)]
    hidden_rel = (hidden_near, hidden_other, hidden_far, swap(hidden_other, "core"))
    cotangent_other = swap(cotangent_near, "ctx")
    inputs = hidden_near[:block].astype(F32)
    inverse = lax.rsqrt(jnp.mean(inputs * inputs, axis=-1, keepdims=True) + epsilon)
    valid = (own * block + jnp.arange(block, dtype=jnp.int32) < length).astype(F32)[:, None]
    query_row = jnp.tile(query_gain.astype(F32), 2)[None]
    key_row = jnp.concatenate([key_gain.astype(F32), jnp.ones((HD,), F32)])[None]

    def attend(hidden_rel, cosine, sine, query_row, key_row, attn_parts):
        attn_full, gains, near, far, unit, query, key, value, raw, mixed, mixed_rel, total = call(
            attention_forward,
            [((width, wide + lane), BF16), ((8, width), F32)]
            + [((every // 2, width), BF16)] * 2
            + [((every, width), BF16)]
            + [((every, lane), BF16)] * 3
            + [((every, 2 * lane), F32), ((every, lane), F32), ((every, lane), BF16), ((every, lane), F32)],
            (index, *hidden_rel, cosine, sine, query_row, key_row, *attn_parts),
            cost=8,
        )
        return near, far, gains, unit, mixed_rel, (attn_full, query, key, value, raw, mixed, total)

    near, far, gains, unit, mixed_rel, kept = region(
        flag, attend, hidden_rel, cosine, sine, query_row, key_row, attn_parts
    )
    kept = kept + (cosine, sine, query_row, key_row)
    near, down_parts = together(near, down_parts)
    if near_shards():
        down_parts.append(onward(down_parts[1]))
    middle = region(flag, lambda near, far, inputs: inputs + sum_scatter(near, far), near, far, inputs)
    attention_scale, feedforward_scale = gains[0:1], gains[1:2]
    middle, cotangent_other, down_parts = together(middle, cotangent_other, down_parts)
    if near_shards():
        down_parts.append(onward(down_parts[2]))

    def spread(middle, feedforward_scale, cotangent_other, cotangent_near):
        inverse_two = lax.rsqrt(jnp.mean(middle * middle, axis=-1, keepdims=True) + epsilon)
        *unit_two, cotangent_last = gather_plane(
            (middle * inverse_two * feedforward_scale).astype(BF16), cotangent_other
        )
        return inverse_two, unit_two, cotangent_last, cotangent_near[:block].astype(F32) * valid

    inverse_two, unit_two, cotangent_last, upstream = region(
        flag, spread, middle, feedforward_scale, cotangent_other, cotangent_near
    )
    if near_shards():
        unit_two, down_parts = together(unit_two, down_parts)
    unit_two_own = middle * inverse_two

    cotangent_rel = (cotangent_near, cotangent_other, cotangent_far, cotangent_last)
    down_full, back = call(
        activated_gradient,
        [((width, main + lane), BF16), ((every, main + lane), F32)],
        (index, *cotangent_rel, *down_parts),
    )
    gu_full, back = together(gu_full, back)
    near, far, ff_grad, activated = call(
        feed_forward,
        [((every // 2, width), BF16)] * 2 + [((width, pack), BF16), ((every, main + lane), BF16)],
        (index, *unit_two, *cotangent_rel, back, gu_full),
        [((every, 2 * hidden), BF16)],
    )
    ff_grad, near = together(ff_grad, near)
    ff_share = lax.psum_scatter(ff_grad, "fsdp", scatter_dimension=0, tiled=True)

    def turn(near, far, unit_two_own, inverse_two, upstream, feedforward_scale, activated, down_full, middle, rest):
        kept, unit, mixed_rel, gains, inputs = rest
        second = sum_scatter(near, far)
        c = second * feedforward_scale
        middle_grad = upstream + inverse_two * (
            c - unit_two_own * jnp.mean(c * unit_two_own, axis=-1, keepdims=True)
        )
        *attention_grad, _ = gather_plane(middle_grad.astype(BF16))
        branch_near, branch_far = call(
            down_product, [((every // 2, width), BF16)] * 2, (index, activated, down_full)
        )
        feedforward_branch = sum_scatter(branch_near, branch_far)
        output = ((middle + feedforward_branch) * valid).astype(BF16)
        near, far, back, head_sums = call(
            attention_backward,
            [((every // 2, width), BF16)] * 2 + [((every, 2 * lane), BF16), ((8, lane), F32)],
            (index, *attention_grad, *kept),
            [((every, lane), BF16)] + [((every, lane), F32)] * 3,
            cost=12,
        )
        output_y = swap(output, "y")
        attn_grad, attention_sums = call(
            attention_weights,
            [((width, wide + lane), BF16), ((8, width), F32)],
            (index, unit, back, *attention_grad, mixed_rel, kept[0], gains),
        )
        (small,) = call(
            small_sums,
            [((24, lane), F32)],
            (index, inputs, middle, feedforward_branch, second, inverse_two, gains, attention_sums, head_sums),
        )
        near, output_y = together(near, output_y)
        return near, far, attn_grad, small, jnp.stack([output, output_y]), middle_grad

    near, far, attn_grad, small, output, middle_grad = region(
        flag,
        turn,
        near,
        far,
        unit_two_own,
        inverse_two,
        upstream,
        feedforward_scale,
        activated,
        down_full,
        middle,
        (kept, unit, mixed_rel, gains, inputs),
    )
    attn_share = lax.psum_scatter(attn_grad, "fsdp", scatter_dimension=0, tiled=True)
    near, ff_share = together(near, ff_share)
    output_core = swap(output, "core")
    first, small = region(flag, last_sums, near, far, small)
    first, ff_share, output_core = together(first, ff_share, output_core)
    ff_other = swap(ff_share, "ctx")

    def finish(first, middle_grad, inputs, inverse, attention_scale, small):
        unit_own = inputs * inverse
        c = first * attention_scale
        input_grad = middle_grad + inverse * (c - unit_own * jnp.mean(c * unit_own, axis=-1, keepdims=True))
        input_grad = input_grad.astype(BF16)
        other, more = together(swap(input_grad, "y"), hop(small, "fsdp"))
        return jnp.stack([input_grad, other]), small + more

    pair, small = region(flag, finish, first, middle_grad, inputs, inverse, attention_scale, small)
    pair, attn_share = together(pair, attn_share)
    attn_other = swap(attn_share, "ctx")

    def unpack(index, pair, output, output_core, small, shard):
        step = 2
        while step < lax.axis_size("fsdp"):
            small = small + hop(small, "fsdp", step)
            step *= 2
        pair_core, small = together(swap(pair, "core"), small)
        (block_rows,) = call(unpack_rows, [((local, width), BF16)], (index, output, output_core))
        (input_rows,) = call(unpack_rows, [((local, width), F32)], (index, pair, pair_core))
        own_gain = attention_gain.shape[0]
        flat = small[:16].reshape(2, -1)
        shares = lax.dynamic_slice_in_dim(flat, shard * own_gain, own_gain, 1)
        stats = jnp.sqrt(small[17, :4] / (small[17, 4] * width))
        return input_rows, block_rows, shares, small[16, :HD], small[16, HD:], stats

    input_rows, block_rows, shares, query_share, key_share, stats = region(
        flag, unpack, index, pair, output, output_core, small, shard
    )
    ff_other, attn_other, input_rows = together(ff_other, attn_other, input_rows)
    ff_grads = call(
        unpack_feed_forward,
        [((rows, 2 * hidden), F32)] * 2 + [((2 * hidden, rows), F32)],
        (index, ff_share, ff_other),
    )
    attn_grads = call(
        unpack_attention,
        [((rows, 2 * lane), F32)] + [((rows, lane), F32)] * 2 + [((2 * lane, rows), F32)],
        (index, attn_share, attn_other),
    )
    return (
        block_rows[None],
        input_rows[None],
        *attn_grads,
        *ff_grads,
        shares[1],
        shares[0],
        query_share,
        key_share,
        stats,
    )


def solution(mesh):
    fsdp, ctx, tp = (mesh.shape[axis] for axis in ("fsdp", "ctx", "tp"))
    assert ctx == 2 and tp == 4
    plane = Mesh(mesh.devices.reshape(fsdp, 2, 2, 2), ("fsdp", "ctx", "y", "core"))
    tp = ("y", "core")
    in_specs = (
        P("fsdp", "ctx", None),
        P("fsdp"),
        P("fsdp", "ctx"),
        P("fsdp", tp),
        P("fsdp", tp),
        P("fsdp", tp),
        P(tp, "fsdp"),
        P("fsdp", tp),
        P("fsdp", tp),
        P(tp, "fsdp"),
        P("fsdp"),
        P("fsdp"),
        P(),
        P(),
        P("fsdp", "ctx", None),
    )
    out_specs = (
        P("fsdp", "ctx", None),
        P("fsdp", "ctx", None),
        P("fsdp", tp),
        P("fsdp", tp),
        P("fsdp", tp),
        P(tp, "fsdp"),
        P("fsdp", tp),
        P("fsdp", tp),
        P(tp, "fsdp"),
        P("fsdp"),
        P("fsdp"),
        P(),
        P(),
        P(),
    )
    return jax.shard_map(shards, mesh=plane, in_specs=in_specs, out_specs=out_specs, check_vma=False)
```

```python
import jax
import jax.numpy as jnp
from jax import lax
from jax.experimental import pallas as pl
from jax.experimental.pallas import tpu as pltpu
from jax.sharding import Mesh, PartitionSpec as P

HD = 64
epsilon = 1e-05
rope_base = 1000000.0
F32 = jnp.float32
BF16 = jnp.bfloat16
PLANE = ("ctx", "y", "core")


def swap(value, axis):
    return lax.ppermute(value, axis, [(0, 1), (1, 0)])


def hop(value, axis, step=1):
    size = lax.axis_size(axis)
    return lax.ppermute(value, axis, [(i, i ^ step) for i in range(size)])


def scatter_start(near, far):
    rows, width = near.shape[0] // 2, near.shape[1] // 2
    low, keep = ((rows, width), BF16), ((rows, width), F32)
    left_low, right_low, left, right = call(split_sum, [low, low, keep, keep], (near, far))
    return left, swap(left_low, "ctx"), right, swap(right_low, "y")


def scatter_next(left, from_x, right, from_y):
    rows, width = left.shape[0] // 2, left.shape[1]
    low, keep = ((rows, width), BF16), ((rows, width), F32)
    left, left_low, right, right_low = call(split_again, [keep, low, keep, low], (left, from_x, right, from_y))
    return left, swap(left_low, "y"), right, swap(right_low, "ctx")


def sum_scatter(near, far):
    return scatter_next(*scatter_start(near, swap(far, "core")))


def gather_end(left, left_x, right, right_y):
    width = left.shape[1]
    left = jnp.stack([left, left_x])
    right = jnp.stack([right, right_y])
    left = jnp.stack([left, swap(left, "y")], 1)
    right = jnp.stack([right, swap(right, "ctx")], 0)
    near = jnp.concatenate([left, right], -1).reshape(-1, 2 * width)
    return near, swap(near, "core")


def gather_plane(left, right, beside):
    beside, left_x, right_y = together(swap(beside, "core"), swap(left, "ctx"), swap(right, "y"))
    return *gather_end(left, left_x, right, right_y), beside


def near_shards():
    return lax.axis_size("fsdp") <= 4


def direct(pieces):
    size = lax.axis_size("fsdp")
    return [
        piece if step == 0 else lax.ppermute(piece, "fsdp", [(i, i ^ step) for i in range(size)])
        for step, piece in enumerate(pieces)
    ]


def onward(value):
    size = lax.axis_size("fsdp")
    return lax.ppermute(value, "fsdp", [(i, (i + 1) % size) for i in range(size)])


def together(*values):
    return lax.optimization_barrier(values)


def region(flag, work, *args):
    shapes = jax.eval_shape(work, *args)
    return lax.cond(flag, work, lambda *_: jax.tree.map(lambda x: jnp.zeros(x.shape, x.dtype), shapes), *args)


def lanes(shape):
    return lax.broadcasted_iota(jnp.int32, shape, len(shape) - 1)


def nt(left, right):
    return lax.dot_general(left, right, (((1,), (1,)), ((), ())), preferred_element_type=F32)


def tn(left, right):
    return lax.dot_general(left, right, (((0,), (0,)), ((), ())), preferred_element_type=F32)


def nn(left, right):
    return lax.dot_general(left, right, (((1,), (0,)), ((), ())), preferred_element_type=F32)


def half_sums(values, low):
    first = jnp.sum(jnp.where(low, values, 0.0), axis=-1, keepdims=True)
    second = jnp.sum(jnp.where(low, 0.0, values), axis=-1, keepdims=True)
    return first, second


def turned(values):
    return jnp.where(lanes(values.shape) % HD < HD // 2, pltpu.roll(values, 96, 1), pltpu.roll(values, 32, 1))


def rows_of(own, kk, xx, yy, block):
    return pl.multiple_of((own ^ (xx * 4 + yy * 2 + kk)) * block, block)


def attention_forward(
    index, h0, h1, h2, h3, cosine, sine, query_gain, key_gain, *rest
):
    *parts, w, gains, part_low, part_high, unit, query, key, value, raw, mixed, mixed_rel, inverse = rest
    own, length = index[0], index[1]
    if len(parts) > 2:
        rows = w.shape[0] // len(parts)
        for at, part in enumerate(parts):
            to = pl.multiple_of((index[2] ^ at) * rows, rows)
            w[pl.ds(to, rows), :] = part[:rows, :]
            gains[:, pl.ds(to, rows)] = part[rows : rows + 16, :rows].astype(F32)[:8]
    else:
        w[...] = parts[0][...]
        gains[...] = parts[1][...]
    gain = gains[0:1, :]
    pair = h0.shape[0]
    block = pair // 2
    low = lanes((pair, 2 * HD)) < HD
    for at, h in enumerate((h0, h1, h2, h3)):
        kk, xx = divmod(at, 2)
        here = slice(at * pair, (at + 1) * pair)
        x = h[...].astype(F32)
        r = lax.rsqrt(jnp.mean(x * x, axis=-1, keepdims=True) + epsilon)
        u = (x * r * gain).astype(BF16)
        unit[here, :] = u
        lin = nn(u, w[:, : 4 * HD])
        raw[here, :] = lin
        q, kv = lin[:, : 2 * HD], lin[:, 2 * HD :]
        one, two = half_sums(q * q, low)
        r = jnp.where(low, lax.rsqrt(one / HD + epsilon), lax.rsqrt(two / HD + epsilon))
        y = q * r * query_gain[...]
        c, s = cosine[here, :], sine[here, :]
        q = (y * c + turned(y) * s).astype(BF16).astype(F32) * HD**-0.5
        one, _ = half_sums(kv * kv, low)
        y = kv * lax.rsqrt(one / HD + epsilon) * key_gain[...]
        kv = jnp.where(low, y * c + turned(y) * s, kv)
        other = pltpu.roll(kv, HD, 1)
        k, v = jnp.where(low, kv, other), jnp.where(low, other, kv)
        for yy in range(2):
            to = rows_of(own, kk, xx, yy, block)
            some = slice(yy * block, (yy + 1) * block)
            query[pl.ds(to, block), :] = q[some].astype(BF16)
            key[pl.ds(to, block), :] = k[some].astype(BF16)
            value[pl.ds(to, block), :] = v[some].astype(BF16)
    for at in range(4):
        here = slice(at * pair, (at + 1) * pair)
        n = (at + 1) * pair
        q = query[here, :]
        q = jnp.concatenate([jnp.where(low, q, jnp.zeros_like(q)), jnp.where(low, jnp.zeros_like(q), q)])
        e = masked_exp(q, key, at, pair, length)
        total = 1.0 / jnp.sum(e, axis=-1, keepdims=True)
        o = nn((e * total).astype(BF16), value[:n, :])
        mixed[here, :] = jnp.where(low, o[:pair], o[pair:])
        inverse[here, :] = jnp.where(low, total[:pair], total[pair:])
    for at in range(4):
        kk, xx = divmod(at, 2)
        pieces = [mixed[pl.ds(rows_of(own, kk, xx, yy, block), block), :] for yy in range(2)]
        m = jnp.concatenate(pieces).astype(BF16)
        mixed_rel[at * pair : (at + 1) * pair, :] = m
        part = nt(m, w[:, 4 * HD :]).astype(BF16)
        to = part_high if kk else part_low
        to[xx * pair : (xx + 1) * pair, :] = part


def masked_exp(query, key, at, pair, length):
    parts = []
    for past in range(at + 1):
        scores = nt(query, key[past * pair : (past + 1) * pair, :])
        columns = lax.broadcasted_iota(jnp.int32, scores.shape, 1)
        here = columns < length - past * pair
        if past == at:
            here = here & (columns <= lax.broadcasted_iota(jnp.int32, scores.shape, 0) % pair)
        parts.append(jnp.where(here, jnp.exp(scores), 0.0))
    return jnp.concatenate(parts, 1)


def attention_backward(
    index, a_low, a_high, w, query, key, value, raw, mixed, inverse, cosine, sine, query_gain, key_gain,
    first_low, first_high, back, gains, down, dq, dk, dv,
):
    own, length = index[0], index[1]
    pair = a_low.shape[0] // 2
    block = pair // 2
    low = lanes((pair, 2 * HD)) < HD
    for at in range(4):
        kk, xx = divmod(at, 2)
        a = a_high if kk else a_low
        m = nn(a[xx * pair : (xx + 1) * pair, :], w[:, 4 * HD :]).astype(BF16)
        for yy in range(2):
            down[pl.ds(rows_of(own, kk, xx, yy, block), block), :] = m[yy * block : (yy + 1) * block]
    dk[...] = jnp.zeros_like(dk)
    dv[...] = jnp.zeros_like(dv)
    for at in range(4):
        here = slice(at * pair, (at + 1) * pair)
        n = (at + 1) * pair
        q, m = query[here, :], down[here, :]
        zero = jnp.zeros_like(q)
        q = jnp.concatenate([jnp.where(low, q, zero), jnp.where(low, zero, q)])
        one, two = half_sums(m.astype(F32) * mixed[here, :], low)
        drop = jnp.concatenate([one, two])
        m = jnp.concatenate([jnp.where(low, m, zero), jnp.where(low, zero, m)])
        total = jnp.concatenate([inverse[here, 0:1], inverse[here, HD : HD + 1]])
        p = masked_exp(q, key, at, pair, length) * total
        g = (p * (nt(m, value[:n, :]) - drop)).astype(BF16)
        dv[:n, :] += tn(p.astype(BF16), m)
        dk[:n, :] += tn(g, q)
        o = nn(g, key[:n, :])
        dq[here, :] = jnp.where(low, o[:pair], o[pair:]) * HD**-0.5
    query_sum = jnp.zeros((1, 2 * HD), F32)
    key_sum = jnp.zeros((1, 2 * HD), F32)
    for at in range(4):
        kk, xx = divmod(at, 2)
        here = slice(at * pair, (at + 1) * pair)
        spots = [pl.ds(rows_of(own, kk, xx, yy, block), block) for yy in range(2)]
        c, s = cosine[here, :], sine[here, :]
        x, kv = raw[here, : 2 * HD], raw[here, 2 * HD :]
        one, two = half_sums(x * x, low)
        r = jnp.where(low, lax.rsqrt(one / HD + epsilon), lax.rsqrt(two / HD + epsilon))
        z = x * r
        y = jnp.concatenate([dq[spot, :] for spot in spots])
        y = y * c - turned(y) * s
        query_sum += jnp.sum(y * z, axis=0, keepdims=True)
        y = y * query_gain[...]
        one, two = half_sums(y * z, low)
        x = r * (y - z * jnp.where(low, one / HD, two / HD))
        one, _ = half_sums(kv * kv, low)
        r = lax.rsqrt(one / HD + epsilon)
        z = kv * r
        y = jnp.concatenate([dk[spot, :] for spot in spots])
        y = y + pltpu.roll(y, HD, 1)
        y = y * c - turned(y) * s
        key_sum += jnp.sum(y * z, axis=0, keepdims=True)
        y = y * key_gain[...]
        one, _ = half_sums(y * z, low)
        v = jnp.concatenate([dv[spot, :] for spot in spots])
        kv = jnp.where(low, r * (y - z * (one / HD)), v + pltpu.roll(v, HD, 1))
        lin = jnp.concatenate([x, kv], axis=1).astype(BF16)
        back[here, :] = lin
        part = nt(lin, w[:, : 4 * HD]).astype(BF16)
        to = first_high if kk else first_low
        to[xx * pair : (xx + 1) * pair, :] = part
    gains[0:1, :] = query_sum
    gains[1:2, :] = key_sum


def activated_gradient(index, b0, b1, b2, b3, *rest):
    *parts, down_w, back = rest
    own, length = index[0], index[1]
    count, rows = len(parts), parts[0].shape[0]
    for at, part in enumerate(parts):
        to = pl.multiple_of((index[2] + count - at) % count * rows, rows)
        down_w[pl.ds(to, rows), :] = part[...]
    pair = b0.shape[0]
    block = pair // 2
    row = lax.broadcasted_iota(jnp.int32, (pair, 1), 0)
    for at, b in enumerate((b0, b1, b2, b3)):
        kk, xx = divmod(at, 2)
        ok = (own ^ (kk + 4 * xx + jnp.where(row >= block, 2, 0))) * block + row % block < length
        back[at * pair : (at + 1) * pair, :] = jnp.where(ok, nn(b[...], down_w[...]), 0.0)


def feed_forward(index, x_low, x_high, b0, b1, b2, b3, back_all, gu_w, second_low, second_high, grad, activated, gate_up):
    own, length = index[0], index[1]
    width = x_low.shape[1]
    pair = b0.shape[0]
    block, four = pair // 2, 2 * pair
    main = gate_up.shape[1] // 2 // 128 * 128
    both = 2 * main
    wide = both + 128
    low = lanes((four, 128)) < HD
    row = lax.broadcasted_iota(jnp.int32, (four, 1), 0)
    bs = (b0, b1, b2, b3)
    for kk, (x, to) in enumerate(((x_low, second_low), (x_high, second_high))):
        here = slice(kk * four, (kk + 1) * four)
        start = own ^ (kk + jnp.where(row >= pair, 4, 0) + jnp.where(row % pair >= block, 2, 0))
        ok = start * block + row % block < length
        gu = nn(x[...], gu_w[...])
        back = back_all[here, :]
        tail = gu[:, both:]
        gate = jnp.concatenate([gu[:, :main], tail], 1)
        upper = jnp.concatenate([gu[:, main:both], pltpu.roll(tail, HD, 1)], 1)
        sigmoid = 1.0 / (1.0 + jnp.exp(-gate))
        silu = gate * sigmoid
        act = jnp.where(ok, silu * upper, 0.0)
        gate_back = back * upper * (sigmoid + silu * (1.0 - sigmoid))
        upper_back = back * silu
        activated[here, :main] = act[:, :main].astype(BF16)
        activated[here, main:] = jnp.where(low, act[:, main:], 0.0).astype(BF16)
        mix = jnp.where(low, gate_back[:, main:], pltpu.roll(upper_back[:, main:], HD, 1))
        gate_up[here, :main] = gate_back[:, :main].astype(BF16)
        gate_up[here, main:both] = upper_back[:, :main].astype(BF16)
        gate_up[here, both:] = mix.astype(BF16)
        to[...] = nt(gate_up[here, :], gu_w[...]).astype(BF16)
    step = width // 2
    for row in range(0, width, step):
        here = slice(row, row + step)
        out = tn(x_low[:, here], gate_up[:four, :]) + tn(x_high[:, here], gate_up[four:, :])
        grad[here, :wide] = out.astype(BF16)
        out = tn(b0[:, here], activated[:pair, :])
        for piece in range(1, 4):
            out += tn(bs[piece][:, here], activated[piece * pair : (piece + 1) * pair, :])
        grad[here, wide:] = out.astype(BF16)


def down_product(index, activated, down_w, branch_low, branch_high):
    four = branch_low.shape[0]
    branch_low[...] = nt(activated[:four, :], down_w[...]).astype(BF16)
    branch_high[...] = nt(activated[four:, :], down_w[...]).astype(BF16)


def split_sum(near, far, left_low, right_low, left, right):
    rows, width = left.shape
    block = rows // 2
    for xx in range(2):
        for yy in range(2):
            here = slice((2 * xx + yy) * block, (2 * xx + yy + 1) * block)
            total = near[here, :].astype(F32) + far[here, :].astype(F32)
            for to, part, sent, at in (
                ((left_low if xx else left), total[:, :width], xx, yy),
                ((right_low if yy else right), total[:, width:], yy, xx),
            ):
                to[at * block : (at + 1) * block, :] = part.astype(BF16) if sent else part


def split_again(left, from_x, right, from_y, left_out, left_low, right_out, right_low):
    block = left_out.shape[0]
    for part, other, out, low in ((left, from_x, left_out, left_low), (right, from_y, right_out, right_low)):
        total = part[...] + other[...].astype(F32)
        out[...] = total[:block]
        low[...] = total[block:].astype(BF16)


def joined(left, from_y, right, from_x):
    left = left[...] + from_y[...].astype(F32)
    return jnp.concatenate([left, right[...] + from_x[...].astype(F32)], 1)


def inverse_of(values):
    return lax.rsqrt(jnp.mean(values * values, axis=-1, keepdims=True) + epsilon)


def validity(index, block):
    row = lax.broadcasted_iota(jnp.int32, (block, 1), 0)
    return (index[0] * block + row < index[1]).astype(F32)


def halves_of(values, left, right):
    width = left.shape[1]
    left[...] = values[:, :width].astype(BF16)
    right[...] = values[:, width:].astype(BF16)


def to_middle(left, from_y, right, from_x, hidden, gains, middle, inverse, out_left, out_right):
    block = middle.shape[0]
    m = hidden[:block, :].astype(F32) + joined(left, from_y, right, from_x)
    r = inverse_of(m)
    middle[...] = m
    inverse[...] = jnp.broadcast_to(r, inverse.shape)
    halves_of(m * r * gains[1:2, :], out_left, out_right)


def to_middle_grad(
    index, left, from_y, right, from_x, middle, inverse, cotangent, gains, second, middle_grad, out_left, out_right
):
    block = middle.shape[0]
    total = joined(left, from_y, right, from_x)
    second[...] = total
    r = inverse[:, 0:1]
    u, c = middle[...] * r, total * gains[1:2, :]
    upstream = cotangent[:block, :].astype(F32) * validity(index, block)
    grad = upstream + r * (c - u * jnp.mean(c * u, axis=-1, keepdims=True))
    middle_grad[...] = grad
    halves_of(grad, out_left, out_right)


def to_output(index, left, from_y, right, from_x, middle, branch, output):
    total = joined(left, from_y, right, from_x)
    branch[...] = total
    output[...] = ((middle[...] + total) * validity(index, middle.shape[0])).astype(BF16)


def to_input_grad(left, from_y, right, from_x, middle_grad, hidden, gains, out):
    block = out.shape[0]
    x = hidden[:block, :].astype(F32)
    r = inverse_of(x)
    u = x * r
    c = joined(left, from_y, right, from_x) * gains[0:1, :]
    out[...] = (middle_grad[...] + r * (c - u * jnp.mean(c * u, axis=-1, keepdims=True))).astype(BF16)


def small_sums(index, hidden, middle, branch, second, inverse, attention_sums, head_sums, out):
    block, width = middle.shape
    valid = validity(index, block)
    x, m = hidden[:block, :].astype(F32), middle[...]
    feedforward_sums = jnp.sum(second[...] * (m * inverse[:, 0:1]), axis=0, keepdims=True)
    for at in range(width // 128):
        here = slice(at * 128, (at + 1) * 128)
        out[at : at + 1, :] = feedforward_sums[:, here]
        out[width // 128 + at : width // 128 + at + 1, :] = attention_sums[0:1, here]
    lane = lanes((1, 128))
    q = head_sums[0:1, :] + pltpu.roll(head_sums[0:1, :], HD, 1)
    out[16:17, :] = jnp.where(lane < HD, q, pltpu.roll(head_sums[1:2, :], HD, 1))
    line = jnp.where(lane == 4, jnp.sum(valid), 0.0)
    for at, item in enumerate((x, m - x, m, branch[...])):
        line = jnp.where(lane == at, jnp.sum(item * item * valid), line)
    out[17:18, :] = line
    out[18:, :] = jnp.zeros((out.shape[0] - 18, 128), F32)


def attention_weights(index, unit, back, a_low, a_high, mixed_rel, w, gains, out, gain_out):
    wide = back.shape[1]
    half = a_low.shape[0]
    step = 256
    for row in range(0, out.shape[0], step):
        here = slice(row, row + step)
        grad = tn(unit[:, here], back[...])
        out[here, :wide] = grad.astype(BF16)
        grad = jnp.sum(grad * w[here, :wide].astype(F32), axis=1, keepdims=True)
        gain_out[:, here] = jnp.broadcast_to(grad, (step, 128)).T[:8] / gains[0:1, here]
        o = tn(a_low[:, here], mixed_rel[:half, :]) + tn(a_high[:, here], mixed_rel[half:, :])
        out[here, wide:] = o.astype(BF16)


def fetch(sources, targets, sems):
    copies = [pltpu.make_async_copy(one, two, sems.at[at]) for at, (one, two) in enumerate(zip(sources, targets))]
    for copy in copies:
        copy.start()
    return copies


def halves(own, source, targets, sems, base):
    block = targets[0].shape[0] // 2
    copies = []
    for kk, target in enumerate(targets):
        for yy in range(2):
            start = pl.multiple_of(((own ^ (2 * yy + kk)) & 3) * block, block)
            to = target.at[pl.ds(yy * block, block)]
            copies.append(pltpu.make_async_copy(source.at[0, pl.ds(start, block)], to, sems.at[base + len(copies)]))
    for copy in copies:
        copy.start()
    return copies


def prelude(
    index, query_from, key_from, value_from, output_from, one_from, two_from, hidden,
    out, hidden_near, hidden_far,
    query, key, value, output, one_gain, two_gain, sems,
):
    copies = fetch(
        (query_from, key_from, value_from, output_from, one_from, two_from),
        (query, key, value, output, one_gain, two_gain),
        sems,
    )
    late = halves(index[0], hidden, (hidden_near, hidden_far), sems, len(copies))
    for copy in copies:
        copy.wait()
    rows = query.shape[0]
    wide = query.shape[1] // 2
    for half in range(2):

        @pl.when(index[3] == half)
        def _():
            out[:rows, :wide] = query[:, half * wide : (half + 1) * wide]
            low = lanes((rows, 2 * HD)) < HD
            k, v = key[...].astype(F32), value[...].astype(F32)
            if half:
                kv = jnp.where(low, pltpu.roll(k, HD, 1), v)
            else:
                kv = jnp.where(low, k, pltpu.roll(v, HD, 1))
            out[:rows, wide : wide + 2 * HD] = kv.astype(BF16)
            out[:rows, wide + 2 * HD :] = output[half * wide : (half + 1) * wide, :].astype(F32).T.astype(BF16)

    one, two = one_gain[...].astype(F32)[None], two_gain[...].astype(F32)[None]
    first = lax.broadcasted_iota(jnp.int32, (16, rows), 0) == 0
    out[rows:, :rows] = jnp.where(first, one, two).astype(BF16)
    out[rows:, rows:] = jnp.zeros((16, out.shape[1] - rows), BF16)
    for copy in late:
        copy.wait()


def pack_feed_forward(index, *rest):
    cotangent, out, down_out, cotangent_near, cotangent_far, gate, upper, down, sems = rest[3:]
    copies = fetch(rest[:3], (gate, upper, down), sems)
    late = halves(index[0], cotangent, (cotangent_near, cotangent_far), sems, len(copies))
    for copy in copies:
        copy.wait()
    rows, hidden = gate.shape[0], gate.shape[1] // 2
    main = hidden // 128 * 128
    both, wide = 2 * main, 2 * hidden
    low = lanes((rows, 128)) < HD
    for half in range(2):

        @pl.when(index[3] == half)
        def _():
            tails = []
            for at, part in enumerate((gate, upper)):
                if half:
                    part = pltpu.roll(part[:, main:].astype(F32), main + HD, 1)
                else:
                    part = part[:, : main + 128].astype(F32)
                out[:, at * main : (at + 1) * main] = part[:, :main].astype(BF16)
                tails.append(part[:, main:])
            out[:, both:wide] = jnp.where(low, tails[0], pltpu.roll(tails[1], HD, 1)).astype(BF16)
            turned = down[half * hidden : (half + 1) * hidden, :].astype(F32)
            turned = jnp.concatenate([turned, jnp.zeros((HD, rows), F32)]).T
            down_out[...] = turned.astype(BF16)
    for copy in late:
        copy.wait()


def unpack_attention(index, mine, other, query, key, value, output):
    wide = query.shape[1] // 2
    low = lanes((mine.shape[0], 2 * HD)) < HD
    for half in range(2):

        @pl.when(index[3] == half)
        def _():
            first, second = (other, mine) if half else (mine, other)
            for at, part in enumerate((first, second)):
                query[:, at * wide : (at + 1) * wide] = part[:, :wide].astype(F32)
                output[at * wide : (at + 1) * wide, :] = part[:, wide + 2 * HD :].astype(F32).T
            one = first[:, wide : wide + 2 * HD].astype(F32)
            two = second[:, wide : wide + 2 * HD].astype(F32)
            key[...] = jnp.where(low, one, pltpu.roll(two, HD, 1))
            value[...] = jnp.where(low, pltpu.roll(one, HD, 1), two)


def unpack_feed_forward(index, mine, other, gate, upper, down):
    rows, hidden = mine.shape[0], gate.shape[1] // 2
    main = hidden // 128 * 128
    both, wide = 2 * main, 2 * hidden
    low = lanes((rows, 128)) < HD
    for half in range(2):

        @pl.when(index[3] == half)
        def _():
            first, second = (other, mine) if half else (mine, other)
            for at, to in enumerate((gate, upper)):
                to[:, :main] = first[:, at * main : (at + 1) * main].astype(F32)
                one = first[:, both : both + 128].astype(F32)
                two = second[:, both : both + 128].astype(F32)
                if at:
                    one = pltpu.roll(one, HD, 1)
                else:
                    two = pltpu.roll(two, HD, 1)
                end = second[:, at * main : (at + 1) * main].astype(F32)
                end = pltpu.roll(jnp.concatenate([end, jnp.zeros((rows, 128), F32)], 1), HD, 1)
                to[:, main : main + 128] = jnp.where(low, one, end[:, :128])
                to[:, main + 128 : 2 * main] = end[:, 128:main]
                to[:, 2 * main :] = jnp.where(low, end[:, main:], two)
            for at, part in enumerate((first, second)):
                turned = part[:, wide:].astype(F32).T
                down[at * hidden : (at + 1) * hidden, :] = turned[:hidden]


def unpack_rows(index, near, far, rows):
    block = near.shape[1]
    for kk, part in enumerate((near, far)):
        for yy in range(2):
            to = pl.multiple_of(((index[0] ^ (2 * yy + kk)) & 3) * block, block)
            rows[pl.ds(to, block), :] = part[yy].astype(rows.dtype)


def call(kernel, outs, args, scratch=(), limit=48, fetched=0, cost=0):
    vmem, hbm = pl.BlockSpec(memory_space=pltpu.VMEM), pl.BlockSpec(memory_space=pl.ANY)
    kinds = [
        pl.BlockSpec(memory_space=pltpu.SMEM)
        if arg.dtype == jnp.int32
        else hbm
        if fetched
        else vmem
        for arg in args
    ]
    scratch = [pltpu.VMEM(shape, kind) for shape, kind in scratch]
    if fetched:
        scratch += [pltpu.VMEM(arg.shape, arg.dtype) for arg in args[1 : 1 + fetched]]
        scratch += [pltpu.SemaphoreType.DMA((fetched + 4,))]
    return pl.pallas_call(
        kernel,
        out_shape=[jax.ShapeDtypeStruct(shape, kind) for shape, kind in outs],
        in_specs=kinds,
        out_specs=[vmem] * len(outs),
        scratch_shapes=scratch,
        compiler_params=pltpu.CompilerParams(vmem_limit_bytes=limit * 2**20),
        cost_estimate=pl.CostEstimate(flops=1000 + cost * 10**9, bytes_accessed=1000, transcendentals=0),
    )(*args)


def shards(
    hidden_in,
    lengths,
    positions,
    query_weight,
    key_weight,
    value_weight,
    output_weight,
    gate_weight,
    up_weight,
    down_weight,
    attention_gain,
    feedforward_gain,
    query_gain,
    key_gain,
    cotangent,
):
    ctx, why, core = lax.axis_index("ctx"), lax.axis_index("y"), lax.axis_index("core")
    local, width = hidden_in.shape[1:]
    block = local // 4
    every = 2 * local
    length = lengths[0]

    heads = query_weight.shape[1] // 2 // HD
    groups = key_weight.shape[1] // 2 // HD
    lane = 2 * HD
    wide = (heads + 2 * groups) * HD
    rows = query_weight.shape[0]
    hidden = gate_weight.shape[1] // 2
    main = hidden // 128 * 128
    assert hidden - main == HD and heads * HD == lane and groups == 1
    pack = 2 * hidden + main + lane
    own = ctx * 4 + why * 2 + core
    shard = lax.axis_index("fsdp")
    size = lax.axis_size("fsdp")
    index = jnp.stack([own, length, shard, ctx]).astype(jnp.int32)
    flag = length > 0

    attn_own, hidden_near, hidden_far = call(
        prelude,
        [((rows + 16, wide + lane), BF16)] + [((local // 2, width), BF16)] * 2,
        (
            index,
            query_weight,
            key_weight,
            value_weight,
            output_weight,
            attention_gain,
            feedforward_gain,
            hidden_in,
        ),
        limit=60,
        fetched=6,
    )
    hidden_other = swap(hidden_near, "ctx")
    if near_shards():
        attn_parts = direct([attn_own] * size)
    else:
        attn_parts = lax.all_gather(attn_own, "fsdp")
        gains = attn_parts[:, rows : rows + 8, :rows].astype(F32).transpose(1, 0, 2).reshape(8, -1)
        attn_parts = [attn_parts[:, :rows].reshape(-1, wide + lane), gains]

    def prepare(positions, gate_weight, up_weight, down_weight, cotangent):
        gu_own, down_own, *cotangent_rel = call(
            pack_feed_forward,
            [((rows, 2 * hidden), BF16), ((rows, main + lane), BF16)] + [((local // 2, width), BF16)] * 2,
            (index, gate_weight, up_weight, down_weight, cotangent),
            limit=60,
            fetched=3,
        )
        pieces = [
            lax.dynamic_slice_in_dim(positions[0], (2 * (why ^ yy) + (core ^ kk)) * block, block)
            for kk in range(2)
            for yy in range(2)
        ]
        places = jnp.concatenate(pieces).reshape(2, -1)
        places = jnp.stack([places, swap(places, "ctx")], 1).reshape(-1)
        freqs = rope_base ** (-2.0 * jnp.arange(HD // 2, dtype=F32) / HD)
        angles = places.astype(F32)[:, None] * jnp.tile(freqs, 4)[None, :]
        cosine = jnp.cos(angles)
        sine = jnp.sin(angles) * jnp.where(jnp.arange(lane) % HD < HD // 2, -1.0, 1.0)[None, :]
        return gu_own, down_own, cosine, sine, *cotangent_rel

    gu_own, down_own, cosine, sine, cotangent_near, cotangent_far = region(
        flag, prepare, positions, gate_weight, up_weight, down_weight, cotangent
    )
    attn_parts, gu_own, hidden_other, cotangent_near = together(attn_parts, gu_own, hidden_other, cotangent_near)
    gu_full = lax.all_gather(gu_own, "fsdp", axis=0, tiled=True)
    down_parts = [down_own]
    if near_shards():
        down_parts.append(onward(down_own))
    else:
        down_parts = [lax.all_gather(down_own, "fsdp", axis=0, tiled=True)]
    hidden_rel = (hidden_near, hidden_other, hidden_far, swap(hidden_other, "core"))
    cotangent_other = swap(cotangent_near, "ctx")
    query_row = jnp.tile(query_gain.astype(F32), 2)[None]
    key_row = jnp.concatenate([key_gain.astype(F32), jnp.ones((HD,), F32)])[None]

    def attend(hidden_rel, cosine, sine, query_row, key_row, attn_parts):
        attn_full, gains, near, far, unit, query, key, value, raw, mixed, mixed_rel, total = call(
            attention_forward,
            [((width, wide + lane), BF16), ((8, width), F32)]
            + [((every // 2, width), BF16)] * 2
            + [((every, width), BF16)]
            + [((every, lane), BF16)] * 3
            + [((every, 2 * lane), F32), ((every, lane), F32), ((every, lane), BF16), ((every, lane), F32)],
            (index, *hidden_rel, cosine, sine, query_row, key_row, *attn_parts),
            cost=8,
        )
        return near, far, gains, unit, mixed_rel, (attn_full, query, key, value, raw, mixed, total)

    near, far, gains, unit, mixed_rel, kept = region(
        flag, attend, hidden_rel, cosine, sine, query_row, key_row, attn_parts
    )
    kept = kept + (cosine, sine, query_row, key_row)
    near, down_parts = together(near, down_parts)
    if near_shards():
        down_parts.append(onward(down_parts[1]))
    quarter, whole = ((block, width // 2), BF16), ((block, width), F32)

    def add_attention(near, far, hidden_near, gains):
        return call(
            to_middle,
            [whole, ((block, lane), F32), quarter, quarter],
            (*sum_scatter(near, far), hidden_near, gains),
        )

    middle, inverse_two, *spread = region(flag, add_attention, near, far, hidden_near, gains)
    spread, cotangent_other, down_parts = together(spread, cotangent_other, down_parts)
    if near_shards():
        down_parts.append(onward(down_parts[2]))
    *unit_two, cotangent_last = region(flag, gather_plane, *spread, cotangent_other)
    if near_shards():
        unit_two, down_parts = together(unit_two, down_parts)

    cotangent_rel = (cotangent_near, cotangent_other, cotangent_far, cotangent_last)
    down_full, back = call(
        activated_gradient,
        [((width, main + lane), BF16), ((every, main + lane), F32)],
        (index, *cotangent_rel, *down_parts),
    )
    gu_full, back = together(gu_full, back)
    near, far, ff_grad, activated = call(
        feed_forward,
        [((every // 2, width), BF16)] * 2 + [((width, pack), BF16), ((every, main + lane), BF16)],
        (index, *unit_two, *cotangent_rel, back, gu_full),
        [((every, 2 * hidden), BF16)],
    )
    ff_grad, near = together(ff_grad, near)
    ff_share = lax.psum_scatter(ff_grad, "fsdp", scatter_dimension=0, tiled=True)

    def turn(near, far, middle, inverse_two, cotangent_near, gains, activated, down_full, kept):
        far, branch_parts = together(
            swap(far, "core"), call(down_product, [((every // 2, width), BF16)] * 2, (index, activated, down_full))
        )
        terms, branch_far = together(scatter_start(near, far), swap(branch_parts[1], "core"))
        terms, branch = together(scatter_next(*terms), scatter_start(branch_parts[0], branch_far))
        second, middle_grad, left, right = call(
            to_middle_grad,
            [whole, whole, quarter, quarter],
            (index, *terms, middle, inverse_two, cotangent_near, gains),
        )
        left_x, right_y, branch = together(swap(left, "ctx"), swap(right, "y"), scatter_next(*branch))
        branch, output = call(to_output, [whole, ((block, width), BF16)], (index, *branch, middle))
        attention_grad = gather_end(left, left_x, right, right_y)
        attention_grad, branch, output = together(attention_grad, branch, output)
        near, far, back, head_sums = call(
            attention_backward,
            [((every // 2, width), BF16)] * 2 + [((every, 2 * lane), BF16), ((8, lane), F32)],
            (index, *attention_grad, *kept),
            [((every, lane), BF16)] + [((every, lane), F32)] * 3,
        )
        output_y = swap(output, "y")
        near, output_y = together(near, output_y)
        output = jnp.stack([output, output_y])
        return near, far, back, head_sums, attention_grad, branch, second, middle_grad, output, swap(output, "core")

    near, far, back, head_sums, attention_grad, branch, second, middle_grad, output, output_core = region(
        flag,
        turn,
        near,
        far,
        middle,
        inverse_two,
        cotangent_near,
        gains,
        activated,
        down_full,
        kept,
    )

    def sum_first(near, far, back, head_sums, attention_grad, branch, second, middle, inverse, hidden_near, gains, rest):
        unit, mixed_rel, attn_full = rest
        terms = scatter_start(near, swap(far, "core"))
        attn_grad, attention_sums = call(
            attention_weights,
            [((width, wide + lane), BF16), ((8, width), F32)],
            (index, unit, back, *attention_grad, mixed_rel, attn_full, gains),
        )
        (small,) = call(
            small_sums,
            [((24, lane), F32)],
            (index, hidden_near, middle, branch, second, inverse, attention_sums, head_sums),
        )
        terms, attn_grad, small = together(terms, attn_grad, small)
        small = small + hop(small, "core")
        terms, more = together(scatter_next(*terms), hop(small, "ctx"))
        return terms, attn_grad, small + more

    pieces, attn_grad, small = region(
        flag,
        sum_first,
        near,
        far,
        back,
        head_sums,
        attention_grad,
        branch,
        second,
        middle,
        inverse_two,
        hidden_near,
        gains,
        (unit, mixed_rel, kept[0]),
    )
    attn_share = lax.psum_scatter(attn_grad, "fsdp", scatter_dimension=0, tiled=True)
    pieces, ff_share = together(pieces, ff_share)
    ff_other = swap(ff_share, "ctx")

    def finish(pieces, middle_grad, hidden_near, gains, small):
        (input_grad,) = call(
            to_input_grad, [((block, width), BF16)], (*pieces, middle_grad, hidden_near, gains)
        )
        other = swap(input_grad, "y")
        small = small + hop(small, "y")
        if near_shards():
            other, *more = together(other, *(hop(small, "fsdp", step) for step in range(1, size)))
            small = small + sum(more)
        else:
            step = 1
            while step < size:
                small = small + hop(small, "fsdp", step)
                step *= 2
        return jnp.stack([input_grad, other]), small

    pair, small = region(flag, finish, pieces, middle_grad, hidden_near, gains, small)

    def unpack_blocks(index, pair, output, output_core):
        (block_rows,) = call(unpack_rows, [((local, width), BF16)], (index, output, output_core))
        return swap(pair, "core"), block_rows

    pair_core, block_rows = region(flag, unpack_blocks, index, pair, output, output_core)
    (input_rows,) = call(unpack_rows, [((local, width), F32)], (index, pair, pair_core))
    own_gain = attention_gain.shape[0]
    shares = lax.dynamic_slice_in_dim(small[:16].reshape(2, -1), shard * own_gain, own_gain, 1)
    stats = jnp.sqrt(small[17, :4] / (small[17, 4] * width))
    ff_other, attn_share, input_rows, shares, stats = together(ff_other, attn_share, input_rows, shares, stats)

    def unpack_weights(index, ff_share, ff_other, attn_share):
        attn_other = swap(attn_share, "ctx")
        ff_grads = call(
            unpack_feed_forward,
            [((rows, 2 * hidden), F32)] * 2 + [((2 * hidden, rows), F32)],
            (index, ff_share, ff_other),
        )
        attn_other, ff_grads = together(attn_other, ff_grads)
        attn_grads = call(
            unpack_attention,
            [((rows, 2 * lane), F32)] + [((rows, lane), F32)] * 2 + [((2 * lane, rows), F32)],
            (index, attn_share, attn_other),
        )
        return ff_grads, attn_grads

    ff_grads, attn_grads = region(flag, unpack_weights, index, ff_share, ff_other, attn_share)
    return (
        block_rows[None],
        input_rows[None],
        *attn_grads,
        *ff_grads,
        shares[1],
        shares[0],
        small[16, :HD],
        small[16, HD:],
        stats,
    )


def solution(mesh):
    fsdp, ctx, tp = (mesh.shape[axis] for axis in ("fsdp", "ctx", "tp"))
    assert ctx == 2 and tp == 4
    plane = Mesh(mesh.devices.reshape(fsdp, 2, 2, 2), ("fsdp", "ctx", "y", "core"))
    tp = ("y", "core")
    in_specs = (
        P("fsdp", "ctx", None),
        P("fsdp"),
        P("fsdp", "ctx"),
        P("fsdp", tp),
        P("fsdp", tp),
        P("fsdp", tp),
        P(tp, "fsdp"),
        P("fsdp", tp),
        P("fsdp", tp),
        P(tp, "fsdp"),
        P("fsdp"),
        P("fsdp"),
        P(),
        P(),
        P("fsdp", "ctx", None),
    )
    out_specs = (
        P("fsdp", "ctx", None),
        P("fsdp", "ctx", None),
        P("fsdp", tp),
        P("fsdp", tp),
        P("fsdp", tp),
        P(tp, "fsdp"),
        P("fsdp", tp),
        P("fsdp", tp),
        P(tp, "fsdp"),
        P("fsdp"),
        P("fsdp"),
        P(),
        P(),
        P(),
    )
    return jax.shard_map(shards, mesh=plane, in_specs=in_specs, out_specs=out_specs, check_vma=False)
```

```python
import jax
import jax.numpy as jnp
from jax import lax
from jax.experimental import pallas as pl
from jax.experimental.pallas import tpu as pltpu
from jax.sharding import Mesh, PartitionSpec as P

HD = 64
epsilon = 1e-05
rope_base = 1000000.0
F32 = jnp.float32
BF16 = jnp.bfloat16
PLANE = ("ctx", "y", "core")


def swap(value, axis):
    return lax.ppermute(value, axis, [(0, 1), (1, 0)])


def hop(value, axis, step=1):
    size = lax.axis_size(axis)
    return lax.ppermute(value, axis, [(i, i ^ step) for i in range(size)])


def scatter_start(near, far):
    rows, width = near.shape[0] // 2, near.shape[1] // 2
    low, keep = ((rows, width), BF16), ((rows, width), F32)
    left_low, right_low, left, right = call(split_sum, [low, low, keep, keep], (near, far))
    return left, swap(left_low, "ctx"), right, swap(right_low, "y")


def scatter_halves(left, from_x, right, from_y):
    rows, width = left.shape[0] // 2, left.shape[1]
    low, keep = ((rows, width), BF16), ((rows, width), F32)
    return call(split_again, [keep, low, keep, low], (left, from_x, right, from_y))


def scatter_swap(left, left_low, right, right_low):
    return left, swap(left_low, "y"), right, swap(right_low, "ctx")


def scatter_next(left, from_x, right, from_y):
    return scatter_swap(*scatter_halves(left, from_x, right, from_y))


def sum_scatter(near, far):
    return scatter_next(*scatter_start(near, swap(far, "core")))


def gather_end(left, left_x, right, right_y):
    width = left.shape[1]
    left = jnp.stack([left, left_x])
    right = jnp.stack([right, right_y])
    left = jnp.stack([left, swap(left, "y")], 1)
    right = jnp.stack([right, swap(right, "ctx")], 0)
    near = jnp.concatenate([left, right], -1).reshape(-1, 2 * width)
    return near, swap(near, "core")


def gather_plane(left, right, beside):
    beside, left_x, right_y = together(swap(beside, "core"), swap(left, "ctx"), swap(right, "y"))
    return *gather_end(left, left_x, right, right_y), beside


def near_shards():
    return lax.axis_size("fsdp") <= 4


def direct(pieces):
    size = lax.axis_size("fsdp")
    return [
        piece if step == 0 else lax.ppermute(piece, "fsdp", [(i, i ^ step) for i in range(size)])
        for step, piece in enumerate(pieces)
    ]


def onward(value):
    size = lax.axis_size("fsdp")
    return lax.ppermute(value, "fsdp", [(i, (i + 1) % size) for i in range(size)])


def together(*values):
    return lax.optimization_barrier(values)


def region(flag, work, *args):
    shapes = jax.eval_shape(work, *args)
    return lax.cond(flag, work, lambda *_: jax.tree.map(lambda x: jnp.zeros(x.shape, x.dtype), shapes), *args)


def lanes(shape):
    return lax.broadcasted_iota(jnp.int32, shape, len(shape) - 1)


def nt(left, right):
    return lax.dot_general(left, right, (((1,), (1,)), ((), ())), preferred_element_type=F32)


def tn(left, right):
    return lax.dot_general(left, right, (((0,), (0,)), ((), ())), preferred_element_type=F32)


def nn(left, right):
    return lax.dot_general(left, right, (((1,), (0,)), ((), ())), preferred_element_type=F32)


def half_sums(values, low):
    first = jnp.sum(jnp.where(low, values, 0.0), axis=-1, keepdims=True)
    second = jnp.sum(jnp.where(low, 0.0, values), axis=-1, keepdims=True)
    return first, second


def turned(values):
    return jnp.where(lanes(values.shape) % HD < HD // 2, pltpu.roll(values, 96, 1), pltpu.roll(values, 32, 1))


def rows_of(own, kk, xx, yy, block):
    return pl.multiple_of((own ^ (xx * 4 + yy * 2 + kk)) * block, block)


def attention_forward(
    index, h0, h1, h2, h3, cosine, sine, query_gain, key_gain, *rest
):
    *parts, w, gains, part_low, part_high, unit, query, key, value, raw, mixed, mixed_rel, inverse = rest
    own, length = index[0], index[1]
    if len(parts) > 2:
        rows = w.shape[0] // len(parts)
        for at, part in enumerate(parts):
            to = pl.multiple_of((index[2] ^ at) * rows, rows)
            w[pl.ds(to, rows), :] = part[:rows, :]
            gains[:, pl.ds(to, rows)] = part[rows : rows + 16, :rows].astype(F32)[:8]
    else:
        w[...] = parts[0][...]
        gains[...] = parts[1][...]
    gain = gains[0:1, :]
    pair = h0.shape[0]
    block = pair // 2
    low = lanes((pair, 2 * HD)) < HD
    for at, h in enumerate((h0, h1, h2, h3)):
        kk, xx = divmod(at, 2)
        here = slice(at * pair, (at + 1) * pair)
        x = h[...].astype(F32)
        r = lax.rsqrt(jnp.mean(x * x, axis=-1, keepdims=True) + epsilon)
        u = (x * r * gain).astype(BF16)
        unit[here, :] = u
        lin = nn(u, w[:, : 4 * HD])
        raw[here, :] = lin
        q, kv = lin[:, : 2 * HD], lin[:, 2 * HD :]
        one, two = half_sums(q * q, low)
        r = jnp.where(low, lax.rsqrt(one / HD + epsilon), lax.rsqrt(two / HD + epsilon))
        y = q * r * query_gain[...]
        c, s = cosine[here, :], sine[here, :]
        q = (y * c + turned(y) * s).astype(BF16).astype(F32) * HD**-0.5
        one, _ = half_sums(kv * kv, low)
        y = kv * lax.rsqrt(one / HD + epsilon) * key_gain[...]
        kv = jnp.where(low, y * c + turned(y) * s, kv)
        other = pltpu.roll(kv, HD, 1)
        k, v = jnp.where(low, kv, other), jnp.where(low, other, kv)
        for yy in range(2):
            to = rows_of(own, kk, xx, yy, block)
            some = slice(yy * block, (yy + 1) * block)
            query[pl.ds(to, block), :] = q[some].astype(BF16)
            key[pl.ds(to, block), :] = k[some].astype(BF16)
            value[pl.ds(to, block), :] = v[some].astype(BF16)
    for at in range(4):
        here = slice(at * pair, (at + 1) * pair)
        n = (at + 1) * pair
        q = query[here, :]
        q = jnp.concatenate([jnp.where(low, q, jnp.zeros_like(q)), jnp.where(low, jnp.zeros_like(q), q)])
        e = masked_exp(q, key, at, pair, length)
        total = 1.0 / jnp.sum(e, axis=-1, keepdims=True)
        o = nn((e * total).astype(BF16), value[:n, :])
        mixed[here, :] = jnp.where(low, o[:pair], o[pair:])
        inverse[here, :] = jnp.where(low, total[:pair], total[pair:])
    for at in range(4):
        kk, xx = divmod(at, 2)
        pieces = [mixed[pl.ds(rows_of(own, kk, xx, yy, block), block), :] for yy in range(2)]
        m = jnp.concatenate(pieces).astype(BF16)
        mixed_rel[at * pair : (at + 1) * pair, :] = m
        part = nt(m, w[:, 4 * HD :]).astype(BF16)
        to = part_high if kk else part_low
        to[xx * pair : (xx + 1) * pair, :] = part


def masked_exp(query, key, at, pair, length):
    parts = []
    for past in range(at + 1):
        scores = nt(query, key[past * pair : (past + 1) * pair, :])
        columns = lax.broadcasted_iota(jnp.int32, scores.shape, 1)
        here = columns < length - past * pair
        if past == at:
            here = here & (columns <= lax.broadcasted_iota(jnp.int32, scores.shape, 0) % pair)
        parts.append(jnp.where(here, jnp.exp(scores), 0.0))
    return jnp.concatenate(parts, 1)


def attention_backward(
    index, a_low, a_high, w, query, key, value, raw, mixed, inverse, cosine, sine, query_gain, key_gain,
    first_low, first_high, back, gains, down, dq, dk, dv,
):
    own, length = index[0], index[1]
    pair = a_low.shape[0] // 2
    block = pair // 2
    low = lanes((pair, 2 * HD)) < HD
    for at in range(4):
        kk, xx = divmod(at, 2)
        a = a_high if kk else a_low
        m = nn(a[xx * pair : (xx + 1) * pair, :], w[:, 4 * HD :]).astype(BF16)
        for yy in range(2):
            down[pl.ds(rows_of(own, kk, xx, yy, block), block), :] = m[yy * block : (yy + 1) * block]
    dk[...] = jnp.zeros_like(dk)
    dv[...] = jnp.zeros_like(dv)
    for at in range(4):
        here = slice(at * pair, (at + 1) * pair)
        n = (at + 1) * pair
        q, m = query[here, :], down[here, :]
        zero = jnp.zeros_like(q)
        q = jnp.concatenate([jnp.where(low, q, zero), jnp.where(low, zero, q)])
        one, two = half_sums(m.astype(F32) * mixed[here, :], low)
        drop = jnp.concatenate([one, two])
        m = jnp.concatenate([jnp.where(low, m, zero), jnp.where(low, zero, m)])
        total = jnp.concatenate([inverse[here, 0:1], inverse[here, HD : HD + 1]])
        p = masked_exp(q, key, at, pair, length) * total
        g = (p * (nt(m, value[:n, :]) - drop)).astype(BF16)
        dv[:n, :] += tn(p.astype(BF16), m)
        dk[:n, :] += tn(g, q)
        o = nn(g, key[:n, :])
        dq[here, :] = jnp.where(low, o[:pair], o[pair:]) * HD**-0.5
    query_sum = jnp.zeros((1, 2 * HD), F32)
    key_sum = jnp.zeros((1, 2 * HD), F32)
    for at in range(4):
        kk, xx = divmod(at, 2)
        here = slice(at * pair, (at + 1) * pair)
        spots = [pl.ds(rows_of(own, kk, xx, yy, block), block) for yy in range(2)]
        c, s = cosine[here, :], sine[here, :]
        x, kv = raw[here, : 2 * HD], raw[here, 2 * HD :]
        one, two = half_sums(x * x, low)
        r = jnp.where(low, lax.rsqrt(one / HD + epsilon), lax.rsqrt(two / HD + epsilon))
        z = x * r
        y = jnp.concatenate([dq[spot, :] for spot in spots])
        y = y * c - turned(y) * s
        query_sum += jnp.sum(y * z, axis=0, keepdims=True)
        y = y * query_gain[...]
        one, two = half_sums(y * z, low)
        x = r * (y - z * jnp.where(low, one / HD, two / HD))
        one, _ = half_sums(kv * kv, low)
        r = lax.rsqrt(one / HD + epsilon)
        z = kv * r
        y = jnp.concatenate([dk[spot, :] for spot in spots])
        y = y + pltpu.roll(y, HD, 1)
        y = y * c - turned(y) * s
        key_sum += jnp.sum(y * z, axis=0, keepdims=True)
        y = y * key_gain[...]
        one, _ = half_sums(y * z, low)
        v = jnp.concatenate([dv[spot, :] for spot in spots])
        kv = jnp.where(low, r * (y - z * (one / HD)), v + pltpu.roll(v, HD, 1))
        lin = jnp.concatenate([x, kv], axis=1).astype(BF16)
        back[here, :] = lin
        part = nt(lin, w[:, : 4 * HD]).astype(BF16)
        to = first_high if kk else first_low
        to[xx * pair : (xx + 1) * pair, :] = part
    gains[0:1, :] = query_sum
    gains[1:2, :] = key_sum


def activated_gradient(index, b0, b1, b2, b3, *rest):
    *parts, down_w, back = rest
    own, length = index[0], index[1]
    count, rows = len(parts), parts[0].shape[0]
    for at, part in enumerate(parts):
        to = pl.multiple_of((index[2] + count - at) % count * rows, rows)
        down_w[pl.ds(to, rows), :] = part[...]
    pair = b0.shape[0]
    block = pair // 2
    row = lax.broadcasted_iota(jnp.int32, (pair, 1), 0)
    for at, b in enumerate((b0, b1, b2, b3)):
        kk, xx = divmod(at, 2)
        ok = (own ^ (kk + 4 * xx + jnp.where(row >= block, 2, 0))) * block + row % block < length
        back[at * pair : (at + 1) * pair, :] = jnp.where(ok, nn(b[...], down_w[...]), 0.0)


def feed_forward(index, x_low, x_high, b0, b1, b2, b3, back_all, gu_w, second_low, second_high, grad, activated, gate_up):
    own, length = index[0], index[1]
    width = x_low.shape[1]
    pair = b0.shape[0]
    block, four = pair // 2, 2 * pair
    main = gate_up.shape[1] // 2 // 128 * 128
    both = 2 * main
    wide = both + 128
    low = lanes((four, 128)) < HD
    row = lax.broadcasted_iota(jnp.int32, (four, 1), 0)
    bs = (b0, b1, b2, b3)
    for kk, (x, to) in enumerate(((x_low, second_low), (x_high, second_high))):
        here = slice(kk * four, (kk + 1) * four)
        start = own ^ (kk + jnp.where(row >= pair, 4, 0) + jnp.where(row % pair >= block, 2, 0))
        ok = start * block + row % block < length
        gu = nn(x[...], gu_w[...])
        back = back_all[here, :]
        tail = gu[:, both:]
        gate = jnp.concatenate([gu[:, :main], tail], 1)
        upper = jnp.concatenate([gu[:, main:both], pltpu.roll(tail, HD, 1)], 1)
        sigmoid = 1.0 / (1.0 + jnp.exp(-gate))
        silu = gate * sigmoid
        act = jnp.where(ok, silu * upper, 0.0)
        gate_back = back * upper * (sigmoid + silu * (1.0 - sigmoid))
        upper_back = back * silu
        activated[here, :main] = act[:, :main].astype(BF16)
        activated[here, main:] = jnp.where(low, act[:, main:], 0.0).astype(BF16)
        mix = jnp.where(low, gate_back[:, main:], pltpu.roll(upper_back[:, main:], HD, 1))
        gate_up[here, :main] = gate_back[:, :main].astype(BF16)
        gate_up[here, main:both] = upper_back[:, :main].astype(BF16)
        gate_up[here, both:] = mix.astype(BF16)
        to[...] = nt(gate_up[here, :], gu_w[...]).astype(BF16)
    step = width // 2
    for row in range(0, width, step):
        here = slice(row, row + step)
        out = tn(x_low[:, here], gate_up[:four, :]) + tn(x_high[:, here], gate_up[four:, :])
        grad[here, :wide] = out.astype(BF16)
        out = tn(b0[:, here], activated[:pair, :])
        for piece in range(1, 4):
            out += tn(bs[piece][:, here], activated[piece * pair : (piece + 1) * pair, :])
        grad[here, wide:] = out.astype(BF16)


def down_product(index, activated, down_w, branch_low, branch_high):
    four = branch_low.shape[0]
    branch_low[...] = nt(activated[:four, :], down_w[...]).astype(BF16)
    branch_high[...] = nt(activated[four:, :], down_w[...]).astype(BF16)


def split_sum(near, far, left_low, right_low, left, right):
    rows, width = left.shape
    block = rows // 2
    for xx in range(2):
        for yy in range(2):
            here = slice((2 * xx + yy) * block, (2 * xx + yy + 1) * block)
            total = near[here, :].astype(F32) + far[here, :].astype(F32)
            for to, part, sent, at in (
                ((left_low if xx else left), total[:, :width], xx, yy),
                ((right_low if yy else right), total[:, width:], yy, xx),
            ):
                to[at * block : (at + 1) * block, :] = part.astype(BF16) if sent else part


def split_again(left, from_x, right, from_y, left_out, left_low, right_out, right_low):
    block = left_out.shape[0]
    for part, other, out, low in ((left, from_x, left_out, left_low), (right, from_y, right_out, right_low)):
        total = part[...] + other[...].astype(F32)
        out[...] = total[:block]
        low[...] = total[block:].astype(BF16)


def joined(left, from_y, right, from_x):
    left = left[...] + from_y[...].astype(F32)
    return jnp.concatenate([left, right[...] + from_x[...].astype(F32)], 1)


def inverse_of(values):
    return lax.rsqrt(jnp.mean(values * values, axis=-1, keepdims=True) + epsilon)


def validity(index, block):
    row = lax.broadcasted_iota(jnp.int32, (block, 1), 0)
    return (index[0] * block + row < index[1]).astype(F32)


def halves_of(values, left, right):
    width = left.shape[1]
    left[...] = values[:, :width].astype(BF16)
    right[...] = values[:, width:].astype(BF16)


def to_middle(left, from_y, right, from_x, hidden, gains, middle, inverse, out_left, out_right):
    block = middle.shape[0]
    m = hidden[:block, :].astype(F32) + joined(left, from_y, right, from_x)
    r = inverse_of(m)
    middle[...] = m
    inverse[...] = jnp.broadcast_to(r, inverse.shape)
    halves_of(m * r * gains[1:2, :], out_left, out_right)


def to_middle_grad(
    index, left, from_y, right, from_x, middle, inverse, cotangent, gains, second, middle_grad, out_left, out_right
):
    block = middle.shape[0]
    total = joined(left, from_y, right, from_x)
    second[...] = total
    r = inverse[:, 0:1]
    u, c = middle[...] * r, total * gains[1:2, :]
    upstream = cotangent[:block, :].astype(F32) * validity(index, block)
    grad = upstream + r * (c - u * jnp.mean(c * u, axis=-1, keepdims=True))
    middle_grad[...] = grad
    halves_of(grad, out_left, out_right)


def to_output(index, left, from_y, right, from_x, middle, branch, output):
    total = joined(left, from_y, right, from_x)
    branch[...] = total
    output[...] = ((middle[...] + total) * validity(index, middle.shape[0])).astype(BF16)


def to_input_grad(left, from_y, right, from_x, middle_grad, hidden, gains, output, out):
    block = middle_grad.shape[0]
    x = hidden[:block, :].astype(F32)
    r = inverse_of(x)
    u = x * r
    c = joined(left, from_y, right, from_x) * gains[0:1, :]
    out[:block, :] = (middle_grad[...] + r * (c - u * jnp.mean(c * u, axis=-1, keepdims=True))).astype(BF16)
    out[block:, :] = output[...]


def small_sums(index, hidden, middle, branch, second, inverse, attention_sums, head_sums, out):
    block, width = middle.shape
    valid = validity(index, block)
    x, m = hidden[:block, :].astype(F32), middle[...]
    feedforward_sums = jnp.sum(second[...] * (m * inverse[:, 0:1]), axis=0, keepdims=True)
    for at in range(width // 128):
        here = slice(at * 128, (at + 1) * 128)
        out[at : at + 1, :] = feedforward_sums[:, here]
        out[width // 128 + at : width // 128 + at + 1, :] = attention_sums[0:1, here]
    lane = lanes((1, 128))
    q = head_sums[0:1, :] + pltpu.roll(head_sums[0:1, :], HD, 1)
    out[16:17, :] = jnp.where(lane < HD, q, pltpu.roll(head_sums[1:2, :], HD, 1))
    line = jnp.where(lane == 4, jnp.sum(valid), 0.0)
    for at, item in enumerate((x, m - x, m, branch[...])):
        line = jnp.where(lane == at, jnp.sum(item * item * valid), line)
    out[17:18, :] = line
    out[18:, :] = jnp.zeros((out.shape[0] - 18, 128), F32)


def attention_weights(index, unit, back, a_low, a_high, mixed_rel, w, gains, out, gain_out):
    wide = back.shape[1]
    half = a_low.shape[0]
    step = 256
    for row in range(0, out.shape[0], step):
        here = slice(row, row + step)
        grad = tn(unit[:, here], back[...])
        out[here, :wide] = grad.astype(BF16)
        grad = jnp.sum(grad * w[here, :wide].astype(F32), axis=1, keepdims=True)
        gain_out[:, here] = jnp.broadcast_to(grad, (step, 128)).T[:8] / gains[0:1, here]
        o = tn(a_low[:, here], mixed_rel[:half, :]) + tn(a_high[:, here], mixed_rel[half:, :])
        out[here, wide:] = o.astype(BF16)


def fetch(sources, targets, sems):
    copies = [pltpu.make_async_copy(one, two, sems.at[at]) for at, (one, two) in enumerate(zip(sources, targets))]
    for copy in copies:
        copy.start()
    return copies


def halves(own, source, targets, sems, base):
    block = targets[0].shape[0] // 2
    copies = []
    for kk, target in enumerate(targets):
        for yy in range(2):
            start = pl.multiple_of(((own ^ (2 * yy + kk)) & 3) * block, block)
            to = target.at[pl.ds(yy * block, block)]
            copies.append(pltpu.make_async_copy(source.at[0, pl.ds(start, block)], to, sems.at[base + len(copies)]))
    for copy in copies:
        copy.start()
    return copies


def prelude(
    index, query_from, key_from, value_from, output_from, one_from, two_from, hidden,
    out, hidden_near, hidden_far,
    query, key, value, output, one_gain, two_gain, sems,
):
    copies = fetch(
        (query_from, key_from, value_from, output_from, one_from, two_from),
        (query, key, value, output, one_gain, two_gain),
        sems,
    )
    late = halves(index[0], hidden, (hidden_near, hidden_far), sems, len(copies))
    for copy in copies:
        copy.wait()
    rows = query.shape[0]
    wide = query.shape[1] // 2
    for half in range(2):

        @pl.when(index[3] == half)
        def _():
            out[:rows, :wide] = query[:, half * wide : (half + 1) * wide]
            low = lanes((rows, 2 * HD)) < HD
            k, v = key[...].astype(F32), value[...].astype(F32)
            if half:
                kv = jnp.where(low, pltpu.roll(k, HD, 1), v)
            else:
                kv = jnp.where(low, k, pltpu.roll(v, HD, 1))
            out[:rows, wide : wide + 2 * HD] = kv.astype(BF16)
            out[:rows, wide + 2 * HD :] = output[half * wide : (half + 1) * wide, :].astype(F32).T.astype(BF16)

    one, two = one_gain[...].astype(F32)[None], two_gain[...].astype(F32)[None]
    first = lax.broadcasted_iota(jnp.int32, (16, rows), 0) == 0
    out[rows:, :rows] = jnp.where(first, one, two).astype(BF16)
    out[rows:, rows:] = jnp.zeros((16, out.shape[1] - rows), BF16)
    for copy in late:
        copy.wait()


def pack_feed_forward(index, *rest):
    cotangent, out, down_out, cotangent_near, cotangent_far, gate, upper, down, sems = rest[3:]
    copies = fetch(rest[:3], (gate, upper, down), sems)
    late = halves(index[0], cotangent, (cotangent_near, cotangent_far), sems, len(copies))
    for copy in copies:
        copy.wait()
    rows, hidden = gate.shape[0], gate.shape[1] // 2
    main = hidden // 128 * 128
    both, wide = 2 * main, 2 * hidden
    low = lanes((rows, 128)) < HD
    for half in range(2):

        @pl.when(index[3] == half)
        def _():
            tails = []
            for at, part in enumerate((gate, upper)):
                if half:
                    part = pltpu.roll(part[:, main:].astype(F32), main + HD, 1)
                else:
                    part = part[:, : main + 128].astype(F32)
                out[:, at * main : (at + 1) * main] = part[:, :main].astype(BF16)
                tails.append(part[:, main:])
            out[:, both:wide] = jnp.where(low, tails[0], pltpu.roll(tails[1], HD, 1)).astype(BF16)
            turned = down[half * hidden : (half + 1) * hidden, :].astype(F32)
            turned = jnp.concatenate([turned, jnp.zeros((HD, rows), F32)]).T
            down_out[...] = turned.astype(BF16)
    for copy in late:
        copy.wait()


def unpack_attention(index, mine, other, query, key, value, output):
    wide = query.shape[1] // 2
    low = lanes((mine.shape[0], 2 * HD)) < HD
    for half in range(2):

        @pl.when(index[3] == half)
        def _():
            first, second = (other, mine) if half else (mine, other)
            for at, part in enumerate((first, second)):
                query[:, at * wide : (at + 1) * wide] = part[:, :wide].astype(F32)
                output[at * wide : (at + 1) * wide, :] = part[:, wide + 2 * HD :].astype(F32).T
            one = first[:, wide : wide + 2 * HD].astype(F32)
            two = second[:, wide : wide + 2 * HD].astype(F32)
            key[...] = jnp.where(low, one, pltpu.roll(two, HD, 1))
            value[...] = jnp.where(low, pltpu.roll(one, HD, 1), two)


def unpack_feed_forward(index, mine, other, gate, upper, down):
    rows, hidden = mine.shape[0], gate.shape[1] // 2
    main = hidden // 128 * 128
    both, wide = 2 * main, 2 * hidden
    low = lanes((rows, 128)) < HD
    for half in range(2):

        @pl.when(index[3] == half)
        def _():
            first, second = (other, mine) if half else (mine, other)
            for at, to in enumerate((gate, upper)):
                to[:, :main] = first[:, at * main : (at + 1) * main].astype(F32)
                one = first[:, both : both + 128].astype(F32)
                two = second[:, both : both + 128].astype(F32)
                if at:
                    one = pltpu.roll(one, HD, 1)
                else:
                    two = pltpu.roll(two, HD, 1)
                end = second[:, at * main : (at + 1) * main].astype(F32)
                end = pltpu.roll(jnp.concatenate([end, jnp.zeros((rows, 128), F32)], 1), HD, 1)
                to[:, main : main + 128] = jnp.where(low, one, end[:, :128])
                to[:, main + 128 : 2 * main] = end[:, 128:main]
                to[:, 2 * main :] = jnp.where(low, end[:, main:], two)
            for at, part in enumerate((first, second)):
                turned = part[:, wide:].astype(F32).T
                down[at * hidden : (at + 1) * hidden, :] = turned[:hidden]


def small_results(index, small, feedforward_gain, attention_gain, query_gain, key_gain, stats):
    for at, to in enumerate((feedforward_gain, attention_gain)):
        line = jnp.concatenate([small[8 * at + row : 8 * at + row + 1, :] for row in range(8)], 1)
        shift = (line.shape[1] - index[2] * to.shape[0]) % line.shape[1]
        to[...] = pltpu.roll(line, shift, 1)[0, : to.shape[0]]
    query_gain[...] = small[16:17, :][0, :HD]
    key_gain[...] = pltpu.roll(small[16:17, :], HD, 1)[0, :HD]
    line = small[17:18, :]
    count = jnp.sum(jnp.where(lanes((1, 128)) == 4, line, 0.0))
    stats[...] = jnp.sqrt(line / (count * index[4].astype(F32)))[0, :4]


def unpack_rows(index, own, from_y, from_core, from_both, rows, block_rows):
    block = own.shape[0] // 2
    for at, part in enumerate((own, from_y, from_core, from_both)):
        to = pl.multiple_of(((index[0] ^ (2 * (at % 2) + at // 2)) & 3) * block, block)
        rows[pl.ds(to, block), :] = part[:block, :].astype(F32)
        block_rows[pl.ds(to, block), :] = part[block:, :]


def call(kernel, outs, args, scratch=(), limit=48, fetched=0, cost=0):
    vmem, hbm = pl.BlockSpec(memory_space=pltpu.VMEM), pl.BlockSpec(memory_space=pl.ANY)
    kinds = [
        pl.BlockSpec(memory_space=pltpu.SMEM)
        if arg.dtype == jnp.int32
        else hbm
        if fetched
        else vmem
        for arg in args
    ]
    scratch = [pltpu.VMEM(shape, kind) for shape, kind in scratch]
    if fetched:
        scratch += [pltpu.VMEM(arg.shape, arg.dtype) for arg in args[1 : 1 + fetched]]
        scratch += [pltpu.SemaphoreType.DMA((fetched + 4,))]
    return pl.pallas_call(
        kernel,
        out_shape=[jax.ShapeDtypeStruct(shape, kind) for shape, kind in outs],
        in_specs=kinds,
        out_specs=[vmem] * len(outs),
        scratch_shapes=scratch,
        compiler_params=pltpu.CompilerParams(vmem_limit_bytes=limit * 2**20),
        cost_estimate=pl.CostEstimate(flops=1000 + cost * 10**9, bytes_accessed=1000, transcendentals=0),
    )(*args)


def shards(
    hidden_in,
    lengths,
    positions,
    query_weight,
    key_weight,
    value_weight,
    output_weight,
    gate_weight,
    up_weight,
    down_weight,
    attention_gain,
    feedforward_gain,
    query_gain,
    key_gain,
    cotangent,
):
    ctx, why, core = lax.axis_index("ctx"), lax.axis_index("y"), lax.axis_index("core")
    local, width = hidden_in.shape[1:]
    block = local // 4
    every = 2 * local
    length = lengths[0]

    heads = query_weight.shape[1] // 2 // HD
    groups = key_weight.shape[1] // 2 // HD
    lane = 2 * HD
    wide = (heads + 2 * groups) * HD
    rows = query_weight.shape[0]
    hidden = gate_weight.shape[1] // 2
    main = hidden // 128 * 128
    assert hidden - main == HD and heads * HD == lane and groups == 1
    pack = 2 * hidden + main + lane
    own = ctx * 4 + why * 2 + core
    shard = lax.axis_index("fsdp")
    size = lax.axis_size("fsdp")
    index = jnp.stack([own, length, shard, ctx, jnp.int32(width)]).astype(jnp.int32)
    flag = length > 0

    attn_own, hidden_near, hidden_far = call(
        prelude,
        [((rows + 16, wide + lane), BF16)] + [((local // 2, width), BF16)] * 2,
        (
            index,
            query_weight,
            key_weight,
            value_weight,
            output_weight,
            attention_gain,
            feedforward_gain,
            hidden_in,
        ),
        limit=60,
        fetched=6,
    )
    hidden_other = swap(hidden_near, "ctx")
    if near_shards():
        attn_parts = direct([attn_own] * size)
    else:
        attn_parts = lax.all_gather(attn_own, "fsdp")
        gains = attn_parts[:, rows : rows + 8, :rows].astype(F32).transpose(1, 0, 2).reshape(8, -1)
        attn_parts = [attn_parts[:, :rows].reshape(-1, wide + lane), gains]

    def prepare(positions, gate_weight, up_weight, down_weight, cotangent):
        gu_own, down_own, *cotangent_rel = call(
            pack_feed_forward,
            [((rows, 2 * hidden), BF16), ((rows, main + lane), BF16)] + [((local // 2, width), BF16)] * 2,
            (index, gate_weight, up_weight, down_weight, cotangent),
            limit=60,
            fetched=3,
        )
        pieces = [
            lax.dynamic_slice_in_dim(positions[0], (2 * (why ^ yy) + (core ^ kk)) * block, block)
            for kk in range(2)
            for yy in range(2)
        ]
        places = jnp.concatenate(pieces).reshape(2, -1)
        places = jnp.stack([places, swap(places, "ctx")], 1).reshape(-1)
        freqs = rope_base ** (-2.0 * jnp.arange(HD // 2, dtype=F32) / HD)
        angles = places.astype(F32)[:, None] * jnp.tile(freqs, 4)[None, :]
        cosine = jnp.cos(angles)
        sine = jnp.sin(angles) * jnp.where(jnp.arange(lane) % HD < HD // 2, -1.0, 1.0)[None, :]
        return gu_own, down_own, cosine, sine, *cotangent_rel

    gu_own, down_own, cosine, sine, cotangent_near, cotangent_far = region(
        flag, prepare, positions, gate_weight, up_weight, down_weight, cotangent
    )
    attn_parts, gu_own, hidden_other, cotangent_near = together(attn_parts, gu_own, hidden_other, cotangent_near)
    gu_full = lax.all_gather(gu_own, "fsdp", axis=0, tiled=True)
    down_parts = [down_own]
    if near_shards():
        down_parts.append(onward(down_own))
    else:
        down_parts = [lax.all_gather(down_own, "fsdp", axis=0, tiled=True)]
    hidden_rel = (hidden_near, hidden_other, hidden_far, swap(hidden_other, "core"))
    cotangent_other = swap(cotangent_near, "ctx")
    query_row = jnp.tile(query_gain.astype(F32), 2)[None]
    key_row = jnp.concatenate([key_gain.astype(F32), jnp.ones((HD,), F32)])[None]

    def attend(hidden_rel, cosine, sine, query_row, key_row, attn_parts):
        attn_full, gains, near, far, unit, query, key, value, raw, mixed, mixed_rel, total = call(
            attention_forward,
            [((width, wide + lane), BF16), ((8, width), F32)]
            + [((every // 2, width), BF16)] * 2
            + [((every, width), BF16)]
            + [((every, lane), BF16)] * 3
            + [((every, 2 * lane), F32), ((every, lane), F32), ((every, lane), BF16), ((every, lane), F32)],
            (index, *hidden_rel, cosine, sine, query_row, key_row, *attn_parts),
            cost=8,
        )
        return near, far, gains, unit, mixed_rel, (attn_full, query, key, value, raw, mixed, total)

    near, far, gains, unit, mixed_rel, kept = region(
        flag, attend, hidden_rel, cosine, sine, query_row, key_row, attn_parts
    )
    kept = kept + (cosine, sine, query_row, key_row)
    near, down_parts = together(near, down_parts)
    if near_shards():
        down_parts.append(onward(down_parts[1]))
    quarter, whole = ((block, width // 2), BF16), ((block, width), F32)

    def add_attention(near, far, hidden_near, gains):
        return call(
            to_middle,
            [whole, ((block, lane), F32), quarter, quarter],
            (*sum_scatter(near, far), hidden_near, gains),
        )

    middle, inverse_two, *spread = region(flag, add_attention, near, far, hidden_near, gains)
    spread, cotangent_other, down_parts = together(spread, cotangent_other, down_parts)
    if near_shards():
        down_parts.append(onward(down_parts[2]))
    *unit_two, cotangent_last = region(flag, gather_plane, *spread, cotangent_other)
    if near_shards():
        unit_two, down_parts = together(unit_two, down_parts)

    cotangent_rel = (cotangent_near, cotangent_other, cotangent_far, cotangent_last)
    down_full, back = call(
        activated_gradient,
        [((width, main + lane), BF16), ((every, main + lane), F32)],
        (index, *cotangent_rel, *down_parts),
    )
    gu_full, back = together(gu_full, back)
    near, far, ff_grad, activated = call(
        feed_forward,
        [((every // 2, width), BF16)] * 2 + [((width, pack), BF16), ((every, main + lane), BF16)],
        (index, *unit_two, *cotangent_rel, back, gu_full),
        [((every, 2 * hidden), BF16)],
    )
    ff_grad, near = together(ff_grad, near)
    ff_share = lax.psum_scatter(ff_grad, "fsdp", scatter_dimension=0, tiled=True)

    def turn(near, far, middle, inverse_two, cotangent_near, gains, activated, down_full, unit, mixed_rel, kept):
        far, branch_parts = together(
            swap(far, "core"), call(down_product, [((every // 2, width), BF16)] * 2, (index, activated, down_full))
        )
        terms, branch_far = together(scatter_start(near, far), swap(branch_parts[1], "core"))
        second, middle_grad, left, right = call(
            to_middle_grad,
            [whole, whole, quarter, quarter],
            (index, *scatter_next(*terms), middle, inverse_two, cotangent_near, gains),
        )
        attention_grad = gather_end(left, swap(left, "ctx"), right, swap(right, "y"))
        attention_grad, branch_far = together(attention_grad, branch_far)
        branch = scatter_start(branch_parts[0], branch_far)
        near, far, back, head_sums = call(
            attention_backward,
            [((every // 2, width), BF16)] * 2 + [((every, 2 * lane), BF16), ((8, lane), F32)],
            (index, *attention_grad, *kept),
            [((every, lane), BF16)] + [((every, lane), F32)] * 3,
        )
        back, branch = together(back, branch)
        rows_of_branch = scatter_halves(*branch)
        back, rows_of_branch = together(back, rows_of_branch)
        branch = scatter_swap(*rows_of_branch)
        attn_grad, attention_sums = call(
            attention_weights,
            [((width, wide + lane), BF16), ((8, width), F32)],
            (index, unit, back, *attention_grad, mixed_rel, kept[0], gains),
        )
        attn_grad, branch = together(attn_grad, branch)
        return near, far, attn_grad, attention_sums, head_sums, branch, second, middle_grad

    near, far, attn_grad, attention_sums, head_sums, branch, second, middle_grad = region(
        flag,
        turn,
        near,
        far,
        middle,
        inverse_two,
        cotangent_near,
        gains,
        activated,
        down_full,
        unit,
        mixed_rel,
        kept,
    )
    attn_share = lax.psum_scatter(attn_grad, "fsdp", scatter_dimension=0, tiled=True)

    def sum_first(near, far, branch, middle, hidden_near, second, inverse, attention_sums, head_sums):
        far = swap(far, "core")
        branch, output = call(to_output, [whole, ((block, width), BF16)], (index, *branch, middle))
        (small,) = call(
            small_sums,
            [((24, lane), F32)],
            (index, hidden_near, middle, branch, second, inverse, attention_sums, head_sums),
        )
        far, small = together(far, small)
        terms = scatter_start(near, far)
        small = small + hop(small, "core")
        terms, more = together(terms, hop(small, "ctx"))
        small = small + more
        terms, more = together(scatter_next(*terms), hop(small, "y"))
        return terms, small + more, output

    pieces, small, output = region(
        flag,
        sum_first,
        near,
        far,
        branch,
        middle,
        hidden_near,
        second,
        inverse_two,
        attention_sums,
        head_sums,
    )
    pieces, ff_share = together(pieces, ff_share)
    ff_other = swap(ff_share, "ctx")

    def finish(pieces, middle_grad, hidden_near, gains, output, small):
        (own_rows,) = call(
            to_input_grad, [((2 * block, width), BF16)], (*pieces, middle_grad, hidden_near, gains, output)
        )
        rows_y, rows_core = swap(own_rows, "y"), swap(own_rows, "core")
        step = 1
        while step < size:
            small = small + hop(small, "fsdp", step)
            step *= 2
        rows_y, rows_core, small = together(rows_y, rows_core, small)
        return own_rows, rows_y, rows_core, small

    *three, small = region(flag, finish, pieces, middle_grad, hidden_near, gains, output, small)
    three, attn_share, ff_other = together(three, attn_share, ff_other)
    attn_other = swap(attn_share, "ctx")

    def unpack(index, three, ff_share, ff_other, small):
        last = swap(three[1], "core")
        ff_grads = call(
            unpack_feed_forward,
            [((rows, 2 * hidden), F32)] * 2 + [((2 * hidden, rows), F32)],
            (index, ff_share, ff_other),
        )
        results = call(
            small_results, [((rows,), F32)] * 2 + [((HD,), F32)] * 2 + [((4,), F32)], (index, small)
        )
        return together(last, ff_grads, results)

    last, ff_grads, results = region(flag, unpack, index, three, ff_share, ff_other, small)
    input_rows, block_rows = call(
        unpack_rows, [((local, width), F32), ((local, width), BF16)], (index, *three, last)
    )
    attn_other, input_rows = together(attn_other, input_rows)
    attn_grads = call(
        unpack_attention,
        [((rows, 2 * lane), F32)] + [((rows, lane), F32)] * 2 + [((2 * lane, rows), F32)],
        (index, attn_share, attn_other),
    )
    grads = (*attn_grads, *ff_grads)
    feedforward_share, attention_share, query_share, key_share, stats = results
    return (
        block_rows[None],
        input_rows[None],
        *grads,
        attention_share,
        feedforward_share,
        query_share,
        key_share,
        stats,
    )


def solution(mesh):
    fsdp, ctx, tp = (mesh.shape[axis] for axis in ("fsdp", "ctx", "tp"))
    assert ctx == 2 and tp == 4
    plane = Mesh(mesh.devices.reshape(fsdp, 2, 2, 2), ("fsdp", "ctx", "y", "core"))
    tp = ("y", "core")
    in_specs = (
        P("fsdp", "ctx", None),
        P("fsdp"),
        P("fsdp", "ctx"),
        P("fsdp", tp),
        P("fsdp", tp),
        P("fsdp", tp),
        P(tp, "fsdp"),
        P("fsdp", tp),
        P("fsdp", tp),
        P(tp, "fsdp"),
        P("fsdp"),
        P("fsdp"),
        P(),
        P(),
        P("fsdp", "ctx", None),
    )
    out_specs = (
        P("fsdp", "ctx", None),
        P("fsdp", "ctx", None),
        P("fsdp", tp),
        P("fsdp", tp),
        P("fsdp", tp),
        P(tp, "fsdp"),
        P("fsdp", tp),
        P("fsdp", tp),
        P(tp, "fsdp"),
        P("fsdp"),
        P("fsdp"),
        P(),
        P(),
        P(),
    )
    return jax.shard_map(shards, mesh=plane, in_specs=in_specs, out_specs=out_specs, check_vma=False)
```

```python
import jax
import jax.numpy as jnp
from jax import lax
from jax.experimental import pallas as pl
from jax.experimental.pallas import tpu as pltpu
from jax.sharding import Mesh, PartitionSpec as P

HD = 64
epsilon = 1e-05
rope_base = 1000000.0
F32 = jnp.float32
BF16 = jnp.bfloat16
PLANE = ("ctx", "y", "core")


def swap(value, axis):
    return lax.ppermute(value, axis, [(0, 1), (1, 0)])


def hop(value, axis, step=1):
    size = lax.axis_size(axis)
    return lax.ppermute(value, axis, [(i, i ^ step) for i in range(size)])


def scatter_start(near, far):
    rows, width = near.shape[0] // 2, near.shape[1] // 2
    low, keep = ((rows, width), BF16), ((rows, width), F32)
    left_low, right_low, left, right = call(split_sum, [low, low, keep, keep], (near, far))
    return left, swap(left_low, "ctx"), right, swap(right_low, "y")


def scatter_halves(left, from_x, right, from_y):
    rows, width = left.shape[0] // 2, left.shape[1]
    low, keep = ((rows, width), BF16), ((rows, width), F32)
    return call(split_again, [keep, low, keep, low], (left, from_x, right, from_y))


def scatter_swap(left, left_low, right, right_low):
    return left, swap(left_low, "y"), right, swap(right_low, "ctx")


def scatter_next(left, from_x, right, from_y):
    return scatter_swap(*scatter_halves(left, from_x, right, from_y))


def sum_scatter(near, far):
    return scatter_next(*scatter_start(near, swap(far, "core")))


def gather_end(left, left_x, right, right_y):
    width = left.shape[1]
    left = jnp.stack([left, left_x])
    right = jnp.stack([right, right_y])
    left = jnp.stack([left, swap(left, "y")], 1)
    right = jnp.stack([right, swap(right, "ctx")], 0)
    near = jnp.concatenate([left, right], -1).reshape(-1, 2 * width)
    return near, swap(near, "core")


def gather_plane(left, right, beside):
    beside, left_x, right_y = together(swap(beside, "core"), swap(left, "ctx"), swap(right, "y"))
    return *gather_end(left, left_x, right, right_y), beside


def near_shards():
    return lax.axis_size("fsdp") <= 4


def direct(pieces):
    size = lax.axis_size("fsdp")
    return [
        piece if step == 0 else lax.ppermute(piece, "fsdp", [(i, i ^ step) for i in range(size)])
        for step, piece in enumerate(pieces)
    ]


def onward(value):
    size = lax.axis_size("fsdp")
    return lax.ppermute(value, "fsdp", [(i, (i + 1) % size) for i in range(size)])


def together(*values):
    return lax.optimization_barrier(values)


def region(flag, work, *args):
    shapes = jax.eval_shape(work, *args)
    return lax.cond(flag, work, lambda *_: jax.tree.map(lambda x: jnp.zeros(x.shape, x.dtype), shapes), *args)


def lanes(shape):
    return lax.broadcasted_iota(jnp.int32, shape, len(shape) - 1)


def nt(left, right):
    return lax.dot_general(left, right, (((1,), (1,)), ((), ())), preferred_element_type=F32)


def tn(left, right):
    return lax.dot_general(left, right, (((0,), (0,)), ((), ())), preferred_element_type=F32)


def nn(left, right):
    return lax.dot_general(left, right, (((1,), (0,)), ((), ())), preferred_element_type=F32)


def half_sums(values, low):
    first = jnp.sum(jnp.where(low, values, 0.0), axis=-1, keepdims=True)
    second = jnp.sum(jnp.where(low, 0.0, values), axis=-1, keepdims=True)
    return first, second


def turned(values):
    return jnp.where(lanes(values.shape) % HD < HD // 2, pltpu.roll(values, 96, 1), pltpu.roll(values, 32, 1))


def rows_of(own, kk, xx, yy, block):
    return pl.multiple_of((own ^ (xx * 4 + yy * 2 + kk)) * block, block)


def attention_forward(
    index, h0, h1, h2, h3, cosine, sine, query_gain, key_gain, *rest
):
    *parts, w, gains, part_low, part_high, unit, query, key, value, raw, mixed, mixed_rel, inverse = rest
    own, length = index[0], index[1]
    if len(parts) > 2:
        rows = w.shape[0] // len(parts)
        for at, part in enumerate(parts):
            to = pl.multiple_of((index[2] ^ at) * rows, rows)
            w[pl.ds(to, rows), :] = part[:rows, :]
            gains[:, pl.ds(to, rows)] = part[rows : rows + 16, :rows].astype(F32)[:8]
    else:
        w[...] = parts[0][...]
        gains[...] = parts[1][...]
    gain = gains[0:1, :]
    pair = h0.shape[0]
    block = pair // 2
    low = lanes((pair, 2 * HD)) < HD
    for at, h in enumerate((h0, h1, h2, h3)):
        kk, xx = divmod(at, 2)
        here = slice(at * pair, (at + 1) * pair)
        x = h[...].astype(F32)
        r = lax.rsqrt(jnp.mean(x * x, axis=-1, keepdims=True) + epsilon)
        u = (x * r * gain).astype(BF16)
        unit[here, :] = u
        lin = nn(u, w[:, : 4 * HD])
        raw[here, :] = lin
        q, kv = lin[:, : 2 * HD], lin[:, 2 * HD :]
        one, two = half_sums(q * q, low)
        r = jnp.where(low, lax.rsqrt(one / HD + epsilon), lax.rsqrt(two / HD + epsilon))
        y = q * r * query_gain[...]
        c, s = cosine[here, :], sine[here, :]
        q = (y * c + turned(y) * s).astype(BF16).astype(F32) * HD**-0.5
        one, _ = half_sums(kv * kv, low)
        y = kv * lax.rsqrt(one / HD + epsilon) * key_gain[...]
        kv = jnp.where(low, y * c + turned(y) * s, kv)
        other = pltpu.roll(kv, HD, 1)
        k, v = jnp.where(low, kv, other), jnp.where(low, other, kv)
        for yy in range(2):
            to = rows_of(own, kk, xx, yy, block)
            some = slice(yy * block, (yy + 1) * block)
            query[pl.ds(to, block), :] = q[some].astype(BF16)
            key[pl.ds(to, block), :] = k[some].astype(BF16)
            value[pl.ds(to, block), :] = v[some].astype(BF16)
    for at in range(4):
        here = slice(at * pair, (at + 1) * pair)
        n = (at + 1) * pair
        q = query[here, :]
        q = jnp.concatenate([jnp.where(low, q, jnp.zeros_like(q)), jnp.where(low, jnp.zeros_like(q), q)])
        e = masked_exp(q, key, at, pair, length)
        total = 1.0 / jnp.sum(e, axis=-1, keepdims=True)
        o = nn((e * total).astype(BF16), value[:n, :])
        mixed[here, :] = jnp.where(low, o[:pair], o[pair:])
        inverse[here, :] = jnp.where(low, total[:pair], total[pair:])
    for at in range(4):
        kk, xx = divmod(at, 2)
        pieces = [mixed[pl.ds(rows_of(own, kk, xx, yy, block), block), :] for yy in range(2)]
        m = jnp.concatenate(pieces).astype(BF16)
        mixed_rel[at * pair : (at + 1) * pair, :] = m
        part = nt(m, w[:, 4 * HD :]).astype(BF16)
        to = part_high if kk else part_low
        to[xx * pair : (xx + 1) * pair, :] = part


def masked_exp(query, key, at, pair, length):
    parts = []
    for past in range(at + 1):
        scores = nt(query, key[past * pair : (past + 1) * pair, :])
        columns = lax.broadcasted_iota(jnp.int32, scores.shape, 1)
        here = columns < length - past * pair
        if past == at:
            here = here & (columns <= lax.broadcasted_iota(jnp.int32, scores.shape, 0) % pair)
        parts.append(jnp.where(here, jnp.exp(scores), 0.0))
    return jnp.concatenate(parts, 1)


def attention_backward(
    index, a_low, a_high, w, query, key, value, raw, mixed, inverse, cosine, sine, query_gain, key_gain,
    first_low, first_high, back, gains, down, dq, dk, dv,
):
    own, length = index[0], index[1]
    pair = a_low.shape[0] // 2
    block = pair // 2
    low = lanes((pair, 2 * HD)) < HD
    for at in range(4):
        kk, xx = divmod(at, 2)
        a = a_high if kk else a_low
        m = nn(a[xx * pair : (xx + 1) * pair, :], w[:, 4 * HD :]).astype(BF16)
        for yy in range(2):
            down[pl.ds(rows_of(own, kk, xx, yy, block), block), :] = m[yy * block : (yy + 1) * block]
    dk[...] = jnp.zeros_like(dk)
    dv[...] = jnp.zeros_like(dv)
    for at in range(4):
        here = slice(at * pair, (at + 1) * pair)
        n = (at + 1) * pair
        q, m = query[here, :], down[here, :]
        zero = jnp.zeros_like(q)
        q = jnp.concatenate([jnp.where(low, q, zero), jnp.where(low, zero, q)])
        one, two = half_sums(m.astype(F32) * mixed[here, :], low)
        drop = jnp.concatenate([one, two])
        m = jnp.concatenate([jnp.where(low, m, zero), jnp.where(low, zero, m)])
        total = jnp.concatenate([inverse[here, 0:1], inverse[here, HD : HD + 1]])
        p = masked_exp(q, key, at, pair, length) * total
        g = (p * (nt(m, value[:n, :]) - drop)).astype(BF16)
        dv[:n, :] += tn(p.astype(BF16), m)
        dk[:n, :] += tn(g, q)
        o = nn(g, key[:n, :])
        dq[here, :] = jnp.where(low, o[:pair], o[pair:]) * HD**-0.5
    query_sum = jnp.zeros((1, 2 * HD), F32)
    key_sum = jnp.zeros((1, 2 * HD), F32)
    for at in range(4):
        kk, xx = divmod(at, 2)
        here = slice(at * pair, (at + 1) * pair)
        spots = [pl.ds(rows_of(own, kk, xx, yy, block), block) for yy in range(2)]
        c, s = cosine[here, :], sine[here, :]
        x, kv = raw[here, : 2 * HD], raw[here, 2 * HD :]
        one, two = half_sums(x * x, low)
        r = jnp.where(low, lax.rsqrt(one / HD + epsilon), lax.rsqrt(two / HD + epsilon))
        z = x * r
        y = jnp.concatenate([dq[spot, :] for spot in spots])
        y = y * c - turned(y) * s
        query_sum += jnp.sum(y * z, axis=0, keepdims=True)
        y = y * query_gain[...]
        one, two = half_sums(y * z, low)
        x = r * (y - z * jnp.where(low, one / HD, two / HD))
        one, _ = half_sums(kv * kv, low)
        r = lax.rsqrt(one / HD + epsilon)
        z = kv * r
        y = jnp.concatenate([dk[spot, :] for spot in spots])
        y = y + pltpu.roll(y, HD, 1)
        y = y * c - turned(y) * s
        key_sum += jnp.sum(y * z, axis=0, keepdims=True)
        y = y * key_gain[...]
        one, _ = half_sums(y * z, low)
        v = jnp.concatenate([dv[spot, :] for spot in spots])
        kv = jnp.where(low, r * (y - z * (one / HD)), v + pltpu.roll(v, HD, 1))
        lin = jnp.concatenate([x, kv], axis=1).astype(BF16)
        back[here, :] = lin
        part = nt(lin, w[:, : 4 * HD]).astype(BF16)
        to = first_high if kk else first_low
        to[xx * pair : (xx + 1) * pair, :] = part
    gains[0:1, :] = query_sum
    gains[1:2, :] = key_sum


def activated_gradient(index, b0, b1, b2, b3, *rest):
    *parts, down_w, back = rest
    own, length = index[0], index[1]
    count, rows = len(parts), parts[0].shape[0]
    for at, part in enumerate(parts):
        to = pl.multiple_of((index[2] + count - at) % count * rows, rows)
        down_w[pl.ds(to, rows), :] = part[...]
    pair = b0.shape[0]
    block = pair // 2
    row = lax.broadcasted_iota(jnp.int32, (pair, 1), 0)
    for at, b in enumerate((b0, b1, b2, b3)):
        kk, xx = divmod(at, 2)
        ok = (own ^ (kk + 4 * xx + jnp.where(row >= block, 2, 0))) * block + row % block < length
        back[at * pair : (at + 1) * pair, :] = jnp.where(ok, nn(b[...], down_w[...]), 0.0)


def feed_forward(index, x_low, x_high, b0, b1, b2, b3, back_all, gu_w, second_low, second_high, grad, activated, gate_up):
    own, length = index[0], index[1]
    width = x_low.shape[1]
    pair = b0.shape[0]
    block, four = pair // 2, 2 * pair
    main = gate_up.shape[1] // 2 // 128 * 128
    both = 2 * main
    wide = both + 128
    low = lanes((pair, 128)) < HD
    row = lax.broadcasted_iota(jnp.int32, (pair, 1), 0)
    bs = (b0, b1, b2, b3)
    for kk, (x, to) in enumerate(((x_low, second_low), (x_high, second_high))):

        @pl.loop(0, 2)
        def _(xx, kk=kk, x=x, to=to):
            some = pl.ds(pl.multiple_of(xx * pair, pair), pair)
            here = pl.ds(pl.multiple_of(kk * four + xx * pair, pair), pair)
            start = own ^ (kk + 4 * xx + jnp.where(row >= block, 2, 0))
            ok = start * block + row % block < length
            gu = nn(x[some, :], gu_w[...])
            back = back_all[here, :]
            tail = gu[:, both:]
            gate = jnp.concatenate([gu[:, :main], tail], 1)
            upper = jnp.concatenate([gu[:, main:both], pltpu.roll(tail, HD, 1)], 1)
            sigmoid = 1.0 / (1.0 + jnp.exp(-gate))
            silu = gate * sigmoid
            act = jnp.where(ok, silu * upper, 0.0)
            gate_back = back * upper * (sigmoid + silu * (1.0 - sigmoid))
            upper_back = back * silu
            activated[here, :main] = act[:, :main].astype(BF16)
            activated[here, main:] = jnp.where(low, act[:, main:], 0.0).astype(BF16)
            mix = jnp.where(low, gate_back[:, main:], pltpu.roll(upper_back[:, main:], HD, 1))
            gate_up[here, :main] = gate_back[:, :main].astype(BF16)
            gate_up[here, main:both] = upper_back[:, :main].astype(BF16)
            gate_up[here, both:] = mix.astype(BF16)
            to[some, :] = nt(gate_up[here, :], gu_w[...]).astype(BF16)

    step = 256

    @pl.loop(0, width // step)
    def _(at):
        here = pl.ds(pl.multiple_of(at * step, step), step)
        out = tn(x_low[:, here], gate_up[:four, :]) + tn(x_high[:, here], gate_up[four:, :])
        grad[here, :wide] = out.astype(BF16)
        out = tn(b0[:, here], activated[:pair, :])
        for piece in range(1, 4):
            out += tn(bs[piece][:, here], activated[piece * pair : (piece + 1) * pair, :])
        grad[here, wide:] = out.astype(BF16)


def down_product(index, activated, down_w, branch_low, branch_high):
    four = branch_low.shape[0]
    for at, branch in ((0, branch_low), (four, branch_high)):

        @pl.loop(0, 2)
        def _(xx, at=at, branch=branch):
            here = pl.ds(pl.multiple_of(at + xx * (four // 2), four // 2), four // 2)
            some = pl.ds(pl.multiple_of(xx * (four // 2), four // 2), four // 2)
            branch[some, :] = nt(activated[here, :], down_w[...]).astype(BF16)


def split_sum(near, far, left_low, right_low, left, right):
    rows, width = left.shape
    block = rows // 2
    for xx in range(2):
        for yy in range(2):
            here = slice((2 * xx + yy) * block, (2 * xx + yy + 1) * block)
            total = near[here, :].astype(F32) + far[here, :].astype(F32)
            for to, part, sent, at in (
                ((left_low if xx else left), total[:, :width], xx, yy),
                ((right_low if yy else right), total[:, width:], yy, xx),
            ):
                to[at * block : (at + 1) * block, :] = part.astype(BF16) if sent else part


def split_again(left, from_x, right, from_y, left_out, left_low, right_out, right_low):
    block = left_out.shape[0]
    for part, other, out, low in ((left, from_x, left_out, left_low), (right, from_y, right_out, right_low)):
        total = part[...] + other[...].astype(F32)
        out[...] = total[:block]
        low[...] = total[block:].astype(BF16)


def joined(left, from_y, right, from_x):
    left = left[...] + from_y[...].astype(F32)
    return jnp.concatenate([left, right[...] + from_x[...].astype(F32)], 1)


def inverse_of(values):
    return lax.rsqrt(jnp.mean(values * values, axis=-1, keepdims=True) + epsilon)


def validity(index, block):
    row = lax.broadcasted_iota(jnp.int32, (block, 1), 0)
    return (index[0] * block + row < index[1]).astype(F32)


def halves_of(values, left, right):
    width = left.shape[1]
    left[...] = values[:, :width].astype(BF16)
    right[...] = values[:, width:].astype(BF16)


def to_middle(left, from_y, right, from_x, hidden, gains, middle, inverse, out_left, out_right):
    block = middle.shape[0]
    m = hidden[:block, :].astype(F32) + joined(left, from_y, right, from_x)
    r = inverse_of(m)
    middle[...] = m
    inverse[...] = jnp.broadcast_to(r, inverse.shape)
    halves_of(m * r * gains[1:2, :], out_left, out_right)


def to_middle_grad(
    index, left, from_y, right, from_x, middle, inverse, cotangent, gains, second, middle_grad, out_left, out_right
):
    block = middle.shape[0]
    total = joined(left, from_y, right, from_x)
    second[...] = total
    r = inverse[:, 0:1]
    u, c = middle[...] * r, total * gains[1:2, :]
    upstream = cotangent[:block, :].astype(F32) * validity(index, block)
    grad = upstream + r * (c - u * jnp.mean(c * u, axis=-1, keepdims=True))
    middle_grad[...] = grad
    halves_of(grad, out_left, out_right)


def to_output(index, left, from_y, right, from_x, middle, branch, output):
    total = joined(left, from_y, right, from_x)
    branch[...] = total
    output[...] = ((middle[...] + total) * validity(index, middle.shape[0])).astype(BF16)


def to_input_grad(left, from_y, right, from_x, middle_grad, hidden, gains, output, out):
    block = middle_grad.shape[0]
    x = hidden[:block, :].astype(F32)
    r = inverse_of(x)
    u = x * r
    c = joined(left, from_y, right, from_x) * gains[0:1, :]
    out[:block, :] = (middle_grad[...] + r * (c - u * jnp.mean(c * u, axis=-1, keepdims=True))).astype(BF16)
    out[block:, :] = output[...]


def small_sums(index, hidden, middle, branch, second, inverse, attention_sums, head_sums, out):
    block, width = middle.shape
    valid = validity(index, block)
    x, m = hidden[:block, :].astype(F32), middle[...]
    feedforward_sums = jnp.sum(second[...] * (m * inverse[:, 0:1]), axis=0, keepdims=True)
    for at in range(width // 128):
        here = slice(at * 128, (at + 1) * 128)
        out[at : at + 1, :] = feedforward_sums[:, here]
        out[width // 128 + at : width // 128 + at + 1, :] = attention_sums[0:1, here]
    lane = lanes((1, 128))
    q = head_sums[0:1, :] + pltpu.roll(head_sums[0:1, :], HD, 1)
    out[16:17, :] = jnp.where(lane < HD, q, pltpu.roll(head_sums[1:2, :], HD, 1))
    line = jnp.where(lane == 4, jnp.sum(valid), 0.0)
    for at, item in enumerate((x, m - x, m, branch[...])):
        line = jnp.where(lane == at, jnp.sum(item * item * valid), line)
    out[17:18, :] = line
    out[18:, :] = jnp.zeros((out.shape[0] - 18, 128), F32)


def attention_weights(index, unit, back, a_low, a_high, mixed_rel, w, gains, out, gain_out):
    wide = back.shape[1]
    half = a_low.shape[0]
    step = 256
    for row in range(0, out.shape[0], step):
        here = slice(row, row + step)
        grad = tn(unit[:, here], back[...])
        out[here, :wide] = grad.astype(BF16)
        grad = jnp.sum(grad * w[here, :wide].astype(F32), axis=1, keepdims=True)
        gain_out[:, here] = jnp.broadcast_to(grad, (step, 128)).T[:8] / gains[0:1, here]
        o = tn(a_low[:, here], mixed_rel[:half, :]) + tn(a_high[:, here], mixed_rel[half:, :])
        out[here, wide:] = o.astype(BF16)


def fetch(sources, targets, sems):
    copies = [pltpu.make_async_copy(one, two, sems.at[at]) for at, (one, two) in enumerate(zip(sources, targets))]
    for copy in copies:
        copy.start()
    return copies


def halves(own, source, targets, sems, base):
    block = targets[0].shape[0] // 2
    copies = []
    for kk, target in enumerate(targets):
        for yy in range(2):
            start = pl.multiple_of(((own ^ (2 * yy + kk)) & 3) * block, block)
            to = target.at[pl.ds(yy * block, block)]
            copies.append(pltpu.make_async_copy(source.at[0, pl.ds(start, block)], to, sems.at[base + len(copies)]))
    for copy in copies:
        copy.start()
    return copies


def prelude(
    index, query_from, key_from, value_from, output_from, one_from, two_from, hidden,
    out, hidden_near, hidden_far,
    query, key, value, output, one_gain, two_gain, sems,
):
    copies = fetch(
        (query_from, key_from, value_from, output_from, one_from, two_from),
        (query, key, value, output, one_gain, two_gain),
        sems,
    )
    late = halves(index[0], hidden, (hidden_near, hidden_far), sems, len(copies))
    for copy in copies:
        copy.wait()
    rows = query.shape[0]
    wide = query.shape[1] // 2
    for half in range(2):

        @pl.when(index[3] == half)
        def _():
            out[:rows, :wide] = query[:, half * wide : (half + 1) * wide]
            low = lanes((rows, 2 * HD)) < HD
            k, v = key[...].astype(F32), value[...].astype(F32)
            if half:
                kv = jnp.where(low, pltpu.roll(k, HD, 1), v)
            else:
                kv = jnp.where(low, k, pltpu.roll(v, HD, 1))
            out[:rows, wide : wide + 2 * HD] = kv.astype(BF16)
            out[:rows, wide + 2 * HD :] = output[half * wide : (half + 1) * wide, :].astype(F32).T.astype(BF16)

    one, two = one_gain[...].astype(F32)[None], two_gain[...].astype(F32)[None]
    first = lax.broadcasted_iota(jnp.int32, (16, rows), 0) == 0
    out[rows:, :rows] = jnp.where(first, one, two).astype(BF16)
    out[rows:, rows:] = jnp.zeros((16, out.shape[1] - rows), BF16)
    for copy in late:
        copy.wait()


def pack_feed_forward(index, *rest):
    cotangent, out, down_out, cotangent_near, cotangent_far, gate, upper, down, sems = rest[3:]
    copies = fetch(rest[:3], (gate, upper, down), sems)
    late = halves(index[0], cotangent, (cotangent_near, cotangent_far), sems, len(copies))
    for copy in copies:
        copy.wait()
    rows, hidden = gate.shape[0], gate.shape[1] // 2
    main = hidden // 128 * 128
    both, wide = 2 * main, 2 * hidden
    low = lanes((rows, 128)) < HD
    for half in range(2):

        @pl.when(index[3] == half)
        def _():
            tails = []
            for at, part in enumerate((gate, upper)):
                if half:
                    part = pltpu.roll(part[:, main:].astype(F32), main + HD, 1)
                else:
                    part = part[:, : main + 128].astype(F32)
                out[:, at * main : (at + 1) * main] = part[:, :main].astype(BF16)
                tails.append(part[:, main:])
            out[:, both:wide] = jnp.where(low, tails[0], pltpu.roll(tails[1], HD, 1)).astype(BF16)
            turned = down[half * hidden : (half + 1) * hidden, :].astype(F32)
            turned = jnp.concatenate([turned, jnp.zeros((HD, rows), F32)]).T
            down_out[...] = turned.astype(BF16)
    for copy in late:
        copy.wait()


def unpack_attention(index, mine, other, query, key, value, output):
    wide = query.shape[1] // 2
    low = lanes((mine.shape[0], 2 * HD)) < HD
    for half in range(2):

        @pl.when(index[3] == half)
        def _():
            first, second = (other, mine) if half else (mine, other)
            for at, part in enumerate((first, second)):
                query[:, at * wide : (at + 1) * wide] = part[:, :wide].astype(F32)
                output[at * wide : (at + 1) * wide, :] = part[:, wide + 2 * HD :].astype(F32).T
            one = first[:, wide : wide + 2 * HD].astype(F32)
            two = second[:, wide : wide + 2 * HD].astype(F32)
            key[...] = jnp.where(low, one, pltpu.roll(two, HD, 1))
            value[...] = jnp.where(low, pltpu.roll(one, HD, 1), two)


def unpack_feed_forward(index, mine, other, gate, upper, down):
    rows, hidden = mine.shape[0], gate.shape[1] // 2
    main = hidden // 128 * 128
    both, wide = 2 * main, 2 * hidden
    low = lanes((rows, 128)) < HD
    for half in range(2):

        @pl.when(index[3] == half)
        def _():
            first, second = (other, mine) if half else (mine, other)
            for at, to in enumerate((gate, upper)):
                to[:, :main] = first[:, at * main : (at + 1) * main].astype(F32)
                one = first[:, both : both + 128].astype(F32)
                two = second[:, both : both + 128].astype(F32)
                if at:
                    one = pltpu.roll(one, HD, 1)
                else:
                    two = pltpu.roll(two, HD, 1)
                end = second[:, at * main : (at + 1) * main].astype(F32)
                end = pltpu.roll(jnp.concatenate([end, jnp.zeros((rows, 128), F32)], 1), HD, 1)
                to[:, main : main + 128] = jnp.where(low, one, end[:, :128])
                to[:, main + 128 : 2 * main] = end[:, 128:main]
                to[:, 2 * main :] = jnp.where(low, end[:, main:], two)
            for at, part in enumerate((first, second)):
                turned = part[:, wide:].astype(F32).T
                down[at * hidden : (at + 1) * hidden, :] = turned[:hidden]


def small_results(index, small, feedforward_gain, attention_gain, query_gain, key_gain, stats):
    for at, to in enumerate((feedforward_gain, attention_gain)):
        line = jnp.concatenate([small[8 * at + row : 8 * at + row + 1, :] for row in range(8)], 1)
        shift = (line.shape[1] - index[2] * to.shape[0]) % line.shape[1]
        to[...] = pltpu.roll(line, shift, 1)[0, : to.shape[0]]
    query_gain[...] = small[16:17, :][0, :HD]
    key_gain[...] = pltpu.roll(small[16:17, :], HD, 1)[0, :HD]
    line = small[17:18, :]
    count = jnp.sum(jnp.where(lanes((1, 128)) == 4, line, 0.0))
    stats[...] = jnp.sqrt(line / (count * index[4].astype(F32)))[0, :4]


def unpack_rows(index, own, from_y, from_core, from_both, rows, block_rows):
    block = own.shape[0] // 2
    for at, part in enumerate((own, from_y, from_core, from_both)):
        to = pl.multiple_of(((index[0] ^ (2 * (at % 2) + at // 2)) & 3) * block, block)
        rows[pl.ds(to, block), :] = part[:block, :].astype(F32)
        block_rows[pl.ds(to, block), :] = part[block:, :]


def call(kernel, outs, args, scratch=(), limit=48, fetched=0, cost=0):
    vmem, hbm = pl.BlockSpec(memory_space=pltpu.VMEM), pl.BlockSpec(memory_space=pl.ANY)
    kinds = [
        pl.BlockSpec(memory_space=pltpu.SMEM)
        if arg.dtype == jnp.int32
        else hbm
        if fetched
        else vmem
        for arg in args
    ]
    scratch = [pltpu.VMEM(shape, kind) for shape, kind in scratch]
    if fetched:
        scratch += [pltpu.VMEM(arg.shape, arg.dtype) for arg in args[1 : 1 + fetched]]
        scratch += [pltpu.SemaphoreType.DMA((fetched + 4,))]
    return pl.pallas_call(
        kernel,
        out_shape=[jax.ShapeDtypeStruct(shape, kind) for shape, kind in outs],
        in_specs=kinds,
        out_specs=[vmem] * len(outs),
        scratch_shapes=scratch,
        compiler_params=pltpu.CompilerParams(vmem_limit_bytes=limit * 2**20),
        cost_estimate=pl.CostEstimate(flops=1000 + cost * 10**9, bytes_accessed=1000, transcendentals=0),
    )(*args)


def shards(
    hidden_in,
    lengths,
    positions,
    query_weight,
    key_weight,
    value_weight,
    output_weight,
    gate_weight,
    up_weight,
    down_weight,
    attention_gain,
    feedforward_gain,
    query_gain,
    key_gain,
    cotangent,
):
    ctx, why, core = lax.axis_index("ctx"), lax.axis_index("y"), lax.axis_index("core")
    local, width = hidden_in.shape[1:]
    block = local // 4
    every = 2 * local
    length = lengths[0]

    heads = query_weight.shape[1] // 2 // HD
    groups = key_weight.shape[1] // 2 // HD
    lane = 2 * HD
    wide = (heads + 2 * groups) * HD
    rows = query_weight.shape[0]
    hidden = gate_weight.shape[1] // 2
    main = hidden // 128 * 128
    assert hidden - main == HD and heads * HD == lane and groups == 1
    pack = 2 * hidden + main + lane
    own = ctx * 4 + why * 2 + core
    shard = lax.axis_index("fsdp")
    size = lax.axis_size("fsdp")
    index = jnp.stack([own, length, shard, ctx, jnp.int32(width)]).astype(jnp.int32)
    flag = length > 0

    attn_own, hidden_near, hidden_far = call(
        prelude,
        [((rows + 16, wide + lane), BF16)] + [((local // 2, width), BF16)] * 2,
        (
            index,
            query_weight,
            key_weight,
            value_weight,
            output_weight,
            attention_gain,
            feedforward_gain,
            hidden_in,
        ),
        limit=60,
        fetched=6,
    )
    hidden_other = swap(hidden_near, "ctx")
    if near_shards():
        attn_parts = direct([attn_own] * size)
    else:
        attn_parts = lax.all_gather(attn_own, "fsdp")
        gains = attn_parts[:, rows : rows + 8, :rows].astype(F32).transpose(1, 0, 2).reshape(8, -1)
        attn_parts = [attn_parts[:, :rows].reshape(-1, wide + lane), gains]

    def prepare(positions, gate_weight, up_weight, down_weight, cotangent):
        gu_own, down_own, *cotangent_rel = call(
            pack_feed_forward,
            [((rows, 2 * hidden), BF16), ((rows, main + lane), BF16)] + [((local // 2, width), BF16)] * 2,
            (index, gate_weight, up_weight, down_weight, cotangent),
            limit=60,
            fetched=3,
        )
        pieces = [
            lax.dynamic_slice_in_dim(positions[0], (2 * (why ^ yy) + (core ^ kk)) * block, block)
            for kk in range(2)
            for yy in range(2)
        ]
        places = jnp.concatenate(pieces).reshape(2, -1)
        places = jnp.stack([places, swap(places, "ctx")], 1).reshape(-1)
        freqs = rope_base ** (-2.0 * jnp.arange(HD // 2, dtype=F32) / HD)
        angles = places.astype(F32)[:, None] * jnp.tile(freqs, 4)[None, :]
        cosine = jnp.cos(angles)
        sine = jnp.sin(angles) * jnp.where(jnp.arange(lane) % HD < HD // 2, -1.0, 1.0)[None, :]
        return gu_own, down_own, cosine, sine, *cotangent_rel

    gu_own, down_own, cosine, sine, cotangent_near, cotangent_far = region(
        flag, prepare, positions, gate_weight, up_weight, down_weight, cotangent
    )
    attn_parts, gu_own, hidden_other, cotangent_near = together(attn_parts, gu_own, hidden_other, cotangent_near)
    gu_full = lax.all_gather(gu_own, "fsdp", axis=0, tiled=True)
    down_parts = [down_own]
    if near_shards():
        down_parts.append(onward(down_own))
    else:
        down_parts = [lax.all_gather(down_own, "fsdp", axis=0, tiled=True)]
    hidden_rel = (hidden_near, hidden_other, hidden_far, swap(hidden_other, "core"))
    cotangent_other = swap(cotangent_near, "ctx")
    query_row = jnp.tile(query_gain.astype(F32), 2)[None]
    key_row = jnp.concatenate([key_gain.astype(F32), jnp.ones((HD,), F32)])[None]

    def attend(hidden_rel, cosine, sine, query_row, key_row, attn_parts):
        attn_full, gains, near, far, unit, query, key, value, raw, mixed, mixed_rel, total = call(
            attention_forward,
            [((width, wide + lane), BF16), ((8, width), F32)]
            + [((every // 2, width), BF16)] * 2
            + [((every, width), BF16)]
            + [((every, lane), BF16)] * 3
            + [((every, 2 * lane), F32), ((every, lane), F32), ((every, lane), BF16), ((every, lane), F32)],
            (index, *hidden_rel, cosine, sine, query_row, key_row, *attn_parts),
            cost=8,
        )
        return near, far, gains, unit, mixed_rel, (attn_full, query, key, value, raw, mixed, total)

    near, far, gains, unit, mixed_rel, kept = region(
        flag, attend, hidden_rel, cosine, sine, query_row, key_row, attn_parts
    )
    kept = kept + (cosine, sine, query_row, key_row)
    near, down_parts = together(near, down_parts)
    if near_shards():
        down_parts.append(onward(down_parts[1]))
    quarter, whole = ((block, width // 2), BF16), ((block, width), F32)

    def add_attention(near, far, hidden_near, gains):
        return call(
            to_middle,
            [whole, ((block, lane), F32), quarter, quarter],
            (*sum_scatter(near, far), hidden_near, gains),
        )

    middle, inverse_two, *spread = region(flag, add_attention, near, far, hidden_near, gains)
    spread, cotangent_other, down_parts = together(spread, cotangent_other, down_parts)
    if near_shards():
        down_parts.append(onward(down_parts[2]))
    *unit_two, cotangent_last = region(flag, gather_plane, *spread, cotangent_other)
    if near_shards():
        unit_two, down_parts = together(unit_two, down_parts)

    cotangent_rel = (cotangent_near, cotangent_other, cotangent_far, cotangent_last)
    down_full, back = call(
        activated_gradient,
        [((width, main + lane), BF16), ((every, main + lane), F32)],
        (index, *cotangent_rel, *down_parts),
    )
    gu_full, back = together(gu_full, back)
    near, far, ff_grad, activated = call(
        feed_forward,
        [((every // 2, width), BF16)] * 2 + [((width, pack), BF16), ((every, main + lane), BF16)],
        (index, *unit_two, *cotangent_rel, back, gu_full),
        [((every, 2 * hidden), BF16)],
    )
    ff_grad, near = together(ff_grad, near)
    ff_share = lax.psum_scatter(ff_grad, "fsdp", scatter_dimension=0, tiled=True)

    def turn(near, far, middle, inverse_two, cotangent_near, gains, activated, down_full, unit, mixed_rel, kept):
        far, branch_parts = together(
            swap(far, "core"), call(down_product, [((every // 2, width), BF16)] * 2, (index, activated, down_full))
        )
        terms, branch_far = together(scatter_start(near, far), swap(branch_parts[1], "core"))
        second, middle_grad, left, right = call(
            to_middle_grad,
            [whole, whole, quarter, quarter],
            (index, *scatter_next(*terms), middle, inverse_two, cotangent_near, gains),
        )
        attention_grad = gather_end(left, swap(left, "ctx"), right, swap(right, "y"))
        attention_grad, branch_far = together(attention_grad, branch_far)
        branch = scatter_start(branch_parts[0], branch_far)
        near, far, back, head_sums = call(
            attention_backward,
            [((every // 2, width), BF16)] * 2 + [((every, 2 * lane), BF16), ((8, lane), F32)],
            (index, *attention_grad, *kept),
            [((every, lane), BF16)] + [((every, lane), F32)] * 3,
        )
        back, branch = together(back, branch)
        rows_of_branch = scatter_halves(*branch)
        back, rows_of_branch = together(back, rows_of_branch)
        branch = scatter_swap(*rows_of_branch)
        attn_grad, attention_sums = call(
            attention_weights,
            [((width, wide + lane), BF16), ((8, width), F32)],
            (index, unit, back, *attention_grad, mixed_rel, kept[0], gains),
        )
        attn_grad, branch = together(attn_grad, branch)
        return near, far, attn_grad, attention_sums, head_sums, branch, second, middle_grad

    near, far, attn_grad, attention_sums, head_sums, branch, second, middle_grad = region(
        flag,
        turn,
        near,
        far,
        middle,
        inverse_two,
        cotangent_near,
        gains,
        activated,
        down_full,
        unit,
        mixed_rel,
        kept,
    )
    attn_share = lax.psum_scatter(attn_grad, "fsdp", scatter_dimension=0, tiled=True)

    def sum_first(near, far, branch, middle, hidden_near, second, inverse, attention_sums, head_sums):
        far = swap(far, "core")
        branch, output = call(to_output, [whole, ((block, width), BF16)], (index, *branch, middle))
        (small,) = call(
            small_sums,
            [((24, lane), F32)],
            (index, hidden_near, middle, branch, second, inverse, attention_sums, head_sums),
        )
        far, small = together(far, small)
        terms = scatter_start(near, far)
        small = small + hop(small, "core")
        terms, more = together(terms, hop(small, "ctx"))
        small = small + more
        terms, more = together(scatter_next(*terms), hop(small, "y"))
        return terms, small + more, output

    pieces, small, output = region(
        flag,
        sum_first,
        near,
        far,
        branch,
        middle,
        hidden_near,
        second,
        inverse_two,
        attention_sums,
        head_sums,
    )
    pieces, ff_share = together(pieces, ff_share)
    ff_other = swap(ff_share, "ctx")

    def finish(pieces, middle_grad, hidden_near, gains, output, small):
        (own_rows,) = call(
            to_input_grad, [((2 * block, width), BF16)], (*pieces, middle_grad, hidden_near, gains, output)
        )
        rows_y, rows_core = swap(own_rows, "y"), swap(own_rows, "core")
        step = 1
        while step < size:
            small = small + hop(small, "fsdp", step)
            step *= 2
        rows_y, rows_core, small = together(rows_y, rows_core, small)
        return own_rows, rows_y, rows_core, small

    *three, small = region(flag, finish, pieces, middle_grad, hidden_near, gains, output, small)
    three, attn_share, ff_other = together(three, attn_share, ff_other)
    attn_other = swap(attn_share, "ctx")

    def unpack(index, three, ff_share, ff_other, small):
        last = swap(three[1], "core")
        ff_grads = call(
            unpack_feed_forward,
            [((rows, 2 * hidden), F32)] * 2 + [((2 * hidden, rows), F32)],
            (index, ff_share, ff_other),
        )
        results = call(
            small_results, [((rows,), F32)] * 2 + [((HD,), F32)] * 2 + [((4,), F32)], (index, small)
        )
        return together(last, ff_grads, results)

    last, ff_grads, results = region(flag, unpack, index, three, ff_share, ff_other, small)
    input_rows, block_rows = call(
        unpack_rows, [((local, width), F32), ((local, width), BF16)], (index, *three, last)
    )
    attn_other, input_rows = together(attn_other, input_rows)
    attn_grads = call(
        unpack_attention,
        [((rows, 2 * lane), F32)] + [((rows, lane), F32)] * 2 + [((2 * lane, rows), F32)],
        (index, attn_share, attn_other),
    )
    grads = (*attn_grads, *ff_grads)
    feedforward_share, attention_share, query_share, key_share, stats = results
    return (
        block_rows[None],
        input_rows[None],
        *grads,
        attention_share,
        feedforward_share,
        query_share,
        key_share,
        stats,
    )


def solution(mesh):
    fsdp, ctx, tp = (mesh.shape[axis] for axis in ("fsdp", "ctx", "tp"))
    assert ctx == 2 and tp == 4
    plane = Mesh(mesh.devices.reshape(fsdp, 2, 2, 2), ("fsdp", "ctx", "y", "core"))
    tp = ("y", "core")
    in_specs = (
        P("fsdp", "ctx", None),
        P("fsdp"),
        P("fsdp", "ctx"),
        P("fsdp", tp),
        P("fsdp", tp),
        P("fsdp", tp),
        P(tp, "fsdp"),
        P("fsdp", tp),
        P("fsdp", tp),
        P(tp, "fsdp"),
        P("fsdp"),
        P("fsdp"),
        P(),
        P(),
        P("fsdp", "ctx", None),
    )
    out_specs = (
        P("fsdp", "ctx", None),
        P("fsdp", "ctx", None),
        P("fsdp", tp),
        P("fsdp", tp),
        P("fsdp", tp),
        P(tp, "fsdp"),
        P("fsdp", tp),
        P("fsdp", tp),
        P(tp, "fsdp"),
        P("fsdp"),
        P("fsdp"),
        P(),
        P(),
        P(),
    )
    return jax.shard_map(shards, mesh=plane, in_specs=in_specs, out_specs=out_specs, check_vma=False)
```

```python
import jax
import jax.numpy as jnp
from jax import lax
from jax.experimental import pallas as pl
from jax.experimental.pallas import tpu as pltpu
from jax.sharding import Mesh, PartitionSpec as P

HD = 64
epsilon = 1e-05
rope_base = 1000000.0
F32 = jnp.float32
BF16 = jnp.bfloat16
PLANE = ("ctx", "y", "core")


def swap(value, axis):
    return lax.ppermute(value, axis, [(0, 1), (1, 0)])


def hop(value, axis, step=1):
    size = lax.axis_size(axis)
    return lax.ppermute(value, axis, [(i, i ^ step) for i in range(size)])


def scatter_start(near, far):
    rows, width = near.shape[0] // 2, near.shape[1] // 2
    low, keep = ((rows, width), BF16), ((rows, width), F32)
    left_low, right_low, left, right = call(split_sum, [low, low, keep, keep], (near, far))
    return left, swap(left_low, "ctx"), right, swap(right_low, "y")


def scatter_halves(left, from_x, right, from_y):
    rows, width = left.shape[0] // 2, left.shape[1]
    low, keep = ((rows, width), BF16), ((rows, width), F32)
    return call(split_again, [keep, low, keep, low], (left, from_x, right, from_y))


def scatter_swap(left, left_low, right, right_low):
    return left, swap(left_low, "y"), right, swap(right_low, "ctx")


def scatter_next(left, from_x, right, from_y):
    return scatter_swap(*scatter_halves(left, from_x, right, from_y))


def sum_scatter(near, far):
    return scatter_next(*scatter_start(near, swap(far, "core")))


def gather_end(left, left_x, right, right_y):
    width = left.shape[1]
    left = jnp.stack([left, left_x])
    right = jnp.stack([right, right_y])
    left = jnp.stack([left, swap(left, "y")], 1)
    right = jnp.stack([right, swap(right, "ctx")], 0)
    near = jnp.concatenate([left, right], -1).reshape(-1, 2 * width)
    return near, swap(near, "core")


def gather_plane(left, right, beside):
    beside, left_x, right_y = together(swap(beside, "core"), swap(left, "ctx"), swap(right, "y"))
    return *gather_end(left, left_x, right, right_y), beside


def near_shards():
    return lax.axis_size("fsdp") <= 4


def direct(pieces):
    size = lax.axis_size("fsdp")
    return [
        piece if step == 0 else lax.ppermute(piece, "fsdp", [(i, i ^ step) for i in range(size)])
        for step, piece in enumerate(pieces)
    ]


def onward(value):
    size = lax.axis_size("fsdp")
    return lax.ppermute(value, "fsdp", [(i, (i + 1) % size) for i in range(size)])


def together(*values):
    return lax.optimization_barrier(values)


def region(flag, work, *args):
    shapes = jax.eval_shape(work, *args)
    return lax.cond(flag, work, lambda *_: jax.tree.map(lambda x: jnp.zeros(x.shape, x.dtype), shapes), *args)


def lanes(shape):
    return lax.broadcasted_iota(jnp.int32, shape, len(shape) - 1)


def nt(left, right):
    return lax.dot_general(left, right, (((1,), (1,)), ((), ())), preferred_element_type=F32)


def tn(left, right):
    return lax.dot_general(left, right, (((0,), (0,)), ((), ())), preferred_element_type=F32)


def nn(left, right):
    return lax.dot_general(left, right, (((1,), (0,)), ((), ())), preferred_element_type=F32)


def half_sums(values, low):
    first = jnp.sum(jnp.where(low, values, 0.0), axis=-1, keepdims=True)
    second = jnp.sum(jnp.where(low, 0.0, values), axis=-1, keepdims=True)
    return first, second


def turned(values):
    return jnp.where(lanes(values.shape) % HD < HD // 2, pltpu.roll(values, 96, 1), pltpu.roll(values, 32, 1))


def rows_of(own, kk, xx, yy, block):
    return pl.multiple_of((own ^ (xx * 4 + yy * 2 + kk)) * block, block)


def attention_forward(
    index, h0, h1, h2, h3, cosine, sine, query_gain, key_gain, *rest
):
    *parts, w, gains, part_low, part_high, unit, query, key, value, raw, mixed, mixed_rel, inverse = rest
    own, length = index[0], index[1]
    if len(parts) > 2:
        rows = w.shape[0] // len(parts)
        for at, part in enumerate(parts):
            to = pl.multiple_of((index[2] ^ at) * rows, rows)
            w[pl.ds(to, rows), :] = part[:rows, :]
            gains[:, pl.ds(to, rows)] = part[rows : rows + 16, :rows].astype(F32)[:8]
    else:
        w[...] = parts[0][...]
        gains[...] = parts[1][...]
    gain = gains[0:1, :]
    pair = h0.shape[0]
    block = pair // 2
    low = lanes((pair, 2 * HD)) < HD
    for at, h in enumerate((h0, h1, h2, h3)):
        kk, xx = divmod(at, 2)
        here = slice(at * pair, (at + 1) * pair)
        x = h[...].astype(F32)
        r = lax.rsqrt(jnp.mean(x * x, axis=-1, keepdims=True) + epsilon)
        u = (x * r * gain).astype(BF16)
        unit[here, :] = u
        lin = nn(u, w[:, : 4 * HD])
        raw[here, :] = lin
        q, kv = lin[:, : 2 * HD], lin[:, 2 * HD :]
        one, two = half_sums(q * q, low)
        r = jnp.where(low, lax.rsqrt(one / HD + epsilon), lax.rsqrt(two / HD + epsilon))
        y = q * r * query_gain[...]
        c, s = cosine[here, :], sine[here, :]
        q = (y * c + turned(y) * s).astype(BF16).astype(F32) * HD**-0.5
        one, _ = half_sums(kv * kv, low)
        y = kv * lax.rsqrt(one / HD + epsilon) * key_gain[...]
        kv = jnp.where(low, y * c + turned(y) * s, kv)
        other = pltpu.roll(kv, HD, 1)
        k, v = jnp.where(low, kv, other), jnp.where(low, other, kv)
        for yy in range(2):
            to = rows_of(own, kk, xx, yy, block)
            some = slice(yy * block, (yy + 1) * block)
            query[pl.ds(to, block), :] = q[some].astype(BF16)
            key[pl.ds(to, block), :] = k[some].astype(BF16)
            value[pl.ds(to, block), :] = v[some].astype(BF16)
    for at in range(4):
        here = slice(at * pair, (at + 1) * pair)
        n = (at + 1) * pair
        q = query[here, :]
        q = jnp.concatenate([jnp.where(low, q, jnp.zeros_like(q)), jnp.where(low, jnp.zeros_like(q), q)])
        e = masked_exp(q, key, at, pair, length)
        total = 1.0 / jnp.sum(e, axis=-1, keepdims=True)
        o = nn((e * total).astype(BF16), value[:n, :])
        mixed[here, :] = jnp.where(low, o[:pair], o[pair:])
        inverse[here, :] = jnp.where(low, total[:pair], total[pair:])
    for at in range(4):
        kk, xx = divmod(at, 2)
        pieces = [mixed[pl.ds(rows_of(own, kk, xx, yy, block), block), :] for yy in range(2)]
        m = jnp.concatenate(pieces).astype(BF16)
        mixed_rel[at * pair : (at + 1) * pair, :] = m
        part = nt(m, w[:, 4 * HD :]).astype(BF16)
        to = part_high if kk else part_low
        to[xx * pair : (xx + 1) * pair, :] = part


def masked_exp(query, key, at, pair, length):
    parts = []
    for past in range(at + 1):
        scores = nt(query, key[past * pair : (past + 1) * pair, :])
        columns = lax.broadcasted_iota(jnp.int32, scores.shape, 1)
        here = columns < length - past * pair
        if past == at:
            here = here & (columns <= lax.broadcasted_iota(jnp.int32, scores.shape, 0) % pair)
        parts.append(jnp.where(here, jnp.exp(scores), 0.0))
    return jnp.concatenate(parts, 1)


def attention_backward(
    index, a_low, a_high, w, query, key, value, raw, mixed, inverse, cosine, sine, query_gain, key_gain,
    first_low, first_high, back, gains, down, dq, dk, dv,
):
    own, length = index[0], index[1]
    pair = a_low.shape[0] // 2
    block = pair // 2
    low = lanes((pair, 2 * HD)) < HD
    for at in range(4):
        kk, xx = divmod(at, 2)
        a = a_high if kk else a_low
        m = nn(a[xx * pair : (xx + 1) * pair, :], w[:, 4 * HD :]).astype(BF16)
        for yy in range(2):
            down[pl.ds(rows_of(own, kk, xx, yy, block), block), :] = m[yy * block : (yy + 1) * block]
    dk[...] = jnp.zeros_like(dk)
    dv[...] = jnp.zeros_like(dv)
    for at in range(4):
        here = slice(at * pair, (at + 1) * pair)
        n = (at + 1) * pair
        q, m = query[here, :], down[here, :]
        zero = jnp.zeros_like(q)
        q = jnp.concatenate([jnp.where(low, q, zero), jnp.where(low, zero, q)])
        one, two = half_sums(m.astype(F32) * mixed[here, :], low)
        drop = jnp.concatenate([one, two])
        m = jnp.concatenate([jnp.where(low, m, zero), jnp.where(low, zero, m)])
        total = jnp.concatenate([inverse[here, 0:1], inverse[here, HD : HD + 1]])
        p = masked_exp(q, key, at, pair, length) * total
        g = (p * (nt(m, value[:n, :]) - drop)).astype(BF16)
        dv[:n, :] += tn(p.astype(BF16), m)
        dk[:n, :] += tn(g, q)
        o = nn(g, key[:n, :])
        dq[here, :] = jnp.where(low, o[:pair], o[pair:]) * HD**-0.5
    query_sum = jnp.zeros((1, 2 * HD), F32)
    key_sum = jnp.zeros((1, 2 * HD), F32)
    for at in range(4):
        kk, xx = divmod(at, 2)
        here = slice(at * pair, (at + 1) * pair)
        spots = [pl.ds(rows_of(own, kk, xx, yy, block), block) for yy in range(2)]
        c, s = cosine[here, :], sine[here, :]
        x, kv = raw[here, : 2 * HD], raw[here, 2 * HD :]
        one, two = half_sums(x * x, low)
        r = jnp.where(low, lax.rsqrt(one / HD + epsilon), lax.rsqrt(two / HD + epsilon))
        z = x * r
        y = jnp.concatenate([dq[spot, :] for spot in spots])
        y = y * c - turned(y) * s
        query_sum += jnp.sum(y * z, axis=0, keepdims=True)
        y = y * query_gain[...]
        one, two = half_sums(y * z, low)
        x = r * (y - z * jnp.where(low, one / HD, two / HD))
        one, _ = half_sums(kv * kv, low)
        r = lax.rsqrt(one / HD + epsilon)
        z = kv * r
        y = jnp.concatenate([dk[spot, :] for spot in spots])
        y = y + pltpu.roll(y, HD, 1)
        y = y * c - turned(y) * s
        key_sum += jnp.sum(y * z, axis=0, keepdims=True)
        y = y * key_gain[...]
        one, _ = half_sums(y * z, low)
        v = jnp.concatenate([dv[spot, :] for spot in spots])
        kv = jnp.where(low, r * (y - z * (one / HD)), v + pltpu.roll(v, HD, 1))
        lin = jnp.concatenate([x, kv], axis=1).astype(BF16)
        back[here, :] = lin
        part = nt(lin, w[:, : 4 * HD]).astype(BF16)
        to = first_high if kk else first_low
        to[xx * pair : (xx + 1) * pair, :] = part
    gains[0:1, :] = query_sum
    gains[1:2, :] = key_sum


def activated_gradient(index, b0, b1, b2, b3, *rest):
    *parts, down_w, back = rest
    own, length = index[0], index[1]
    count, rows = len(parts), parts[0].shape[0]
    for at, part in enumerate(parts):
        to = pl.multiple_of((index[2] + count - at) % count * rows, rows)
        down_w[pl.ds(to, rows), :] = part[...]
    pair = b0.shape[0]
    block = pair // 2
    row = lax.broadcasted_iota(jnp.int32, (pair, 1), 0)
    for at, b in enumerate((b0, b1, b2, b3)):
        kk, xx = divmod(at, 2)
        ok = (own ^ (kk + 4 * xx + jnp.where(row >= block, 2, 0))) * block + row % block < length
        back[at * pair : (at + 1) * pair, :] = jnp.where(ok, nn(b[...], down_w[...]), 0.0)


def feed_forward(index, x_low, x_high, b0, b1, b2, b3, back_all, gu_w, second_low, second_high, grad, activated, gate_up):
    own, length = index[0], index[1]
    width = x_low.shape[1]
    pair = b0.shape[0]
    block, four = pair // 2, 2 * pair
    main = gate_up.shape[1] // 2 // 128 * 128
    both = 2 * main
    wide = both + 128
    low = lanes((pair, 128)) < HD
    row = lax.broadcasted_iota(jnp.int32, (pair, 1), 0)
    bs = (b0, b1, b2, b3)
    for kk, (x, to) in enumerate(((x_low, second_low), (x_high, second_high))):

        @pl.loop(0, 2)
        def _(xx, kk=kk, x=x, to=to):
            some = pl.ds(pl.multiple_of(xx * pair, pair), pair)
            here = pl.ds(pl.multiple_of(kk * four + xx * pair, pair), pair)
            start = own ^ (kk + 4 * xx + jnp.where(row >= block, 2, 0))
            ok = start * block + row % block < length
            gu = nn(x[some, :], gu_w[...])
            back = back_all[here, :]
            tail = gu[:, both:]
            gate = jnp.concatenate([gu[:, :main], tail], 1)
            upper = jnp.concatenate([gu[:, main:both], pltpu.roll(tail, HD, 1)], 1)
            sigmoid = 1.0 / (1.0 + jnp.exp(-gate))
            silu = gate * sigmoid
            act = jnp.where(ok, silu * upper, 0.0)
            gate_back = back * upper * (sigmoid + silu * (1.0 - sigmoid))
            upper_back = back * silu
            activated[here, :main] = act[:, :main].astype(BF16)
            activated[here, main:] = jnp.where(low, act[:, main:], 0.0).astype(BF16)
            mix = jnp.where(low, gate_back[:, main:], pltpu.roll(upper_back[:, main:], HD, 1))
            gate_up[here, :main] = gate_back[:, :main].astype(BF16)
            gate_up[here, main:both] = upper_back[:, :main].astype(BF16)
            gate_up[here, both:] = mix.astype(BF16)
            to[some, :] = nt(gate_up[here, :], gu_w[...]).astype(BF16)

    step = 256

    @pl.loop(0, width // step)
    def _(at):
        here = pl.ds(pl.multiple_of(at * step, step), step)
        out = tn(x_low[:, here], gate_up[:four, :]) + tn(x_high[:, here], gate_up[four:, :])
        grad[here, :wide] = out.astype(BF16)
        out = tn(b0[:, here], activated[:pair, :])
        for piece in range(1, 4):
            out += tn(bs[piece][:, here], activated[piece * pair : (piece + 1) * pair, :])
        grad[here, wide:] = out.astype(BF16)


def down_product(index, activated, down_w, branch_low, branch_high):
    four = branch_low.shape[0]
    for at, branch in ((0, branch_low), (four, branch_high)):

        @pl.loop(0, 2)
        def _(xx, at=at, branch=branch):
            here = pl.ds(pl.multiple_of(at + xx * (four // 2), four // 2), four // 2)
            some = pl.ds(pl.multiple_of(xx * (four // 2), four // 2), four // 2)
            branch[some, :] = nt(activated[here, :], down_w[...]).astype(BF16)


def split_sum(near, far, left_low, right_low, left, right):
    rows, width = left.shape
    block = rows // 2
    for xx in range(2):
        for yy in range(2):
            here = slice((2 * xx + yy) * block, (2 * xx + yy + 1) * block)
            total = near[here, :].astype(F32) + far[here, :].astype(F32)
            for to, part, sent, at in (
                ((left_low if xx else left), total[:, :width], xx, yy),
                ((right_low if yy else right), total[:, width:], yy, xx),
            ):
                to[at * block : (at + 1) * block, :] = part.astype(BF16) if sent else part


def split_again(left, from_x, right, from_y, left_out, left_low, right_out, right_low):
    block = left_out.shape[0]
    for part, other, out, low in ((left, from_x, left_out, left_low), (right, from_y, right_out, right_low)):
        total = part[...] + other[...].astype(F32)
        out[...] = total[:block]
        low[...] = total[block:].astype(BF16)


def joined(left, from_y, right, from_x):
    left = left[...] + from_y[...].astype(F32)
    return jnp.concatenate([left, right[...] + from_x[...].astype(F32)], 1)


def inverse_of(values):
    return lax.rsqrt(jnp.mean(values * values, axis=-1, keepdims=True) + epsilon)


def validity(index, block):
    row = lax.broadcasted_iota(jnp.int32, (block, 1), 0)
    return (index[0] * block + row < index[1]).astype(F32)


def halves_of(values, left, right):
    width = left.shape[1]
    left[...] = values[:, :width].astype(BF16)
    right[...] = values[:, width:].astype(BF16)


def to_middle(left, from_y, right, from_x, hidden, gains, middle, inverse, out_left, out_right):
    block = middle.shape[0]
    m = hidden[:block, :].astype(F32) + joined(left, from_y, right, from_x)
    r = inverse_of(m)
    middle[...] = m
    inverse[...] = jnp.broadcast_to(r, inverse.shape)
    halves_of(m * r * gains[1:2, :], out_left, out_right)


def to_middle_grad(
    index, left, from_y, right, from_x, middle, inverse, cotangent, gains, second, middle_grad, out_left, out_right
):
    block = middle.shape[0]
    total = joined(left, from_y, right, from_x)
    second[...] = total
    r = inverse[:, 0:1]
    u, c = middle[...] * r, total * gains[1:2, :]
    upstream = cotangent[:block, :].astype(F32) * validity(index, block)
    grad = upstream + r * (c - u * jnp.mean(c * u, axis=-1, keepdims=True))
    middle_grad[...] = grad
    halves_of(grad, out_left, out_right)


def to_output(index, left, from_y, right, from_x, middle, branch, output):
    total = joined(left, from_y, right, from_x)
    branch[...] = total
    output[...] = ((middle[...] + total) * validity(index, middle.shape[0])).astype(BF16)


def to_input_grad(left, from_y, right, from_x, middle_grad, hidden, gains, out):
    block = out.shape[0]
    x = hidden[:block, :].astype(F32)
    r = inverse_of(x)
    u = x * r
    c = joined(left, from_y, right, from_x) * gains[0:1, :]
    out[...] = (middle_grad[...] + r * (c - u * jnp.mean(c * u, axis=-1, keepdims=True))).astype(BF16)


def small_sums(index, hidden, middle, branch, second, inverse, attention_sums, head_sums, out):
    block, width = middle.shape
    valid = validity(index, block)
    x, m = hidden[:block, :].astype(F32), middle[...]
    feedforward_sums = jnp.sum(second[...] * (m * inverse[:, 0:1]), axis=0, keepdims=True)
    for at in range(width // 128):
        here = slice(at * 128, (at + 1) * 128)
        out[at : at + 1, :] = feedforward_sums[:, here]
        out[width // 128 + at : width // 128 + at + 1, :] = attention_sums[0:1, here]
    lane = lanes((1, 128))
    q = head_sums[0:1, :] + pltpu.roll(head_sums[0:1, :], HD, 1)
    out[16:17, :] = jnp.where(lane < HD, q, pltpu.roll(head_sums[1:2, :], HD, 1))
    line = jnp.where(lane == 4, jnp.sum(valid), 0.0)
    for at, item in enumerate((x, m - x, m, branch[...])):
        line = jnp.where(lane == at, jnp.sum(item * item * valid), line)
    out[17:18, :] = line
    out[18:, :] = jnp.zeros((out.shape[0] - 18, 128), F32)


def attention_weights(index, unit, back, a_low, a_high, mixed_rel, w, gains, out, gain_out):
    wide = back.shape[1]
    half = a_low.shape[0]
    step = 256
    for row in range(0, out.shape[0], step):
        here = slice(row, row + step)
        grad = tn(unit[:, here], back[...])
        out[here, :wide] = grad.astype(BF16)
        grad = jnp.sum(grad * w[here, :wide].astype(F32), axis=1, keepdims=True)
        gain_out[:, here] = jnp.broadcast_to(grad, (step, 128)).T[:8] / gains[0:1, here]
        o = tn(a_low[:, here], mixed_rel[:half, :]) + tn(a_high[:, here], mixed_rel[half:, :])
        out[here, wide:] = o.astype(BF16)


def fetch(sources, targets, sems):
    copies = [pltpu.make_async_copy(one, two, sems.at[at]) for at, (one, two) in enumerate(zip(sources, targets))]
    for copy in copies:
        copy.start()
    return copies


def halves(own, source, targets, sems, base):
    block = targets[0].shape[0] // 2
    copies = []
    for kk, target in enumerate(targets):
        for yy in range(2):
            start = pl.multiple_of(((own ^ (2 * yy + kk)) & 3) * block, block)
            to = target.at[pl.ds(yy * block, block)]
            copies.append(pltpu.make_async_copy(source.at[0, pl.ds(start, block)], to, sems.at[base + len(copies)]))
    for copy in copies:
        copy.start()
    return copies


def prelude(
    index, query_from, key_from, value_from, output_from, one_from, two_from, hidden,
    out, hidden_near, hidden_far,
    query, key, value, output, one_gain, two_gain, sems,
):
    copies = fetch(
        (query_from, key_from, value_from, output_from, one_from, two_from),
        (query, key, value, output, one_gain, two_gain),
        sems,
    )
    late = halves(index[0], hidden, (hidden_near, hidden_far), sems, len(copies))
    for copy in copies:
        copy.wait()
    rows = query.shape[0]
    wide = query.shape[1] // 2
    for half in range(2):

        @pl.when(index[3] == half)
        def _():
            out[:rows, :wide] = query[:, half * wide : (half + 1) * wide]
            low = lanes((rows, 2 * HD)) < HD
            k, v = key[...].astype(F32), value[...].astype(F32)
            if half:
                kv = jnp.where(low, pltpu.roll(k, HD, 1), v)
            else:
                kv = jnp.where(low, k, pltpu.roll(v, HD, 1))
            out[:rows, wide : wide + 2 * HD] = kv.astype(BF16)
            out[:rows, wide + 2 * HD :] = output[half * wide : (half + 1) * wide, :].astype(F32).T.astype(BF16)

    one, two = one_gain[...].astype(F32)[None], two_gain[...].astype(F32)[None]
    first = lax.broadcasted_iota(jnp.int32, (16, rows), 0) == 0
    out[rows:, :rows] = jnp.where(first, one, two).astype(BF16)
    out[rows:, rows:] = jnp.zeros((16, out.shape[1] - rows), BF16)
    for copy in late:
        copy.wait()


def pack_feed_forward(index, *rest):
    cotangent, out, down_out, cotangent_near, cotangent_far, gate, upper, down, sems = rest[3:]
    copies = fetch(rest[:3], (gate, upper, down), sems)
    late = halves(index[0], cotangent, (cotangent_near, cotangent_far), sems, len(copies))
    for copy in copies:
        copy.wait()
    rows, hidden = gate.shape[0], gate.shape[1] // 2
    main = hidden // 128 * 128
    both, wide = 2 * main, 2 * hidden
    low = lanes((rows, 128)) < HD
    for half in range(2):

        @pl.when(index[3] == half)
        def _():
            tails = []
            for at, part in enumerate((gate, upper)):
                if half:
                    part = pltpu.roll(part[:, main:].astype(F32), main + HD, 1)
                else:
                    part = part[:, : main + 128].astype(F32)
                out[:, at * main : (at + 1) * main] = part[:, :main].astype(BF16)
                tails.append(part[:, main:])
            out[:, both:wide] = jnp.where(low, tails[0], pltpu.roll(tails[1], HD, 1)).astype(BF16)
            turned = down[half * hidden : (half + 1) * hidden, :].astype(F32)
            turned = jnp.concatenate([turned, jnp.zeros((HD, rows), F32)]).T
            down_out[...] = turned.astype(BF16)
    for copy in late:
        copy.wait()


def unpack_attention(index, mine, other, query, key, value, output):
    wide = query.shape[1] // 2
    low = lanes((mine.shape[0], 2 * HD)) < HD
    for half in range(2):

        @pl.when(index[3] == half)
        def _():
            first, second = (other, mine) if half else (mine, other)
            for at, part in enumerate((first, second)):
                query[:, at * wide : (at + 1) * wide] = part[:, :wide].astype(F32)
                output[at * wide : (at + 1) * wide, :] = part[:, wide + 2 * HD :].astype(F32).T
            one = first[:, wide : wide + 2 * HD].astype(F32)
            two = second[:, wide : wide + 2 * HD].astype(F32)
            key[...] = jnp.where(low, one, pltpu.roll(two, HD, 1))
            value[...] = jnp.where(low, pltpu.roll(one, HD, 1), two)


def unpack_feed_forward(index, mine, other, gate, upper, down):
    rows, hidden = mine.shape[0], gate.shape[1] // 2
    main = hidden // 128 * 128
    both, wide = 2 * main, 2 * hidden
    low = lanes((rows, 128)) < HD
    for half in range(2):

        @pl.when(index[3] == half)
        def _():
            first, second = (other, mine) if half else (mine, other)
            for at, to in enumerate((gate, upper)):
                to[:, :main] = first[:, at * main : (at + 1) * main].astype(F32)
                one = first[:, both : both + 128].astype(F32)
                two = second[:, both : both + 128].astype(F32)
                if at:
                    one = pltpu.roll(one, HD, 1)
                else:
                    two = pltpu.roll(two, HD, 1)
                end = second[:, at * main : (at + 1) * main].astype(F32)
                end = pltpu.roll(jnp.concatenate([end, jnp.zeros((rows, 128), F32)], 1), HD, 1)
                to[:, main : main + 128] = jnp.where(low, one, end[:, :128])
                to[:, main + 128 : 2 * main] = end[:, 128:main]
                to[:, 2 * main :] = jnp.where(low, end[:, main:], two)
            for at, part in enumerate((first, second)):
                turned = part[:, wide:].astype(F32).T
                down[at * hidden : (at + 1) * hidden, :] = turned[:hidden]


def small_results(index, small, feedforward_gain, attention_gain, query_gain, key_gain, stats):
    for at, to in enumerate((feedforward_gain, attention_gain)):
        line = jnp.concatenate([small[8 * at + row : 8 * at + row + 1, :] for row in range(8)], 1)
        shift = (line.shape[1] - index[2] * to.shape[0]) % line.shape[1]
        to[...] = pltpu.roll(line, shift, 1)[0, : to.shape[0]]
    query_gain[...] = small[16:17, :][0, :HD]
    key_gain[...] = pltpu.roll(small[16:17, :], HD, 1)[0, :HD]
    line = small[17:18, :]
    count = jnp.sum(jnp.where(lanes((1, 128)) == 4, line, 0.0))
    stats[...] = jnp.sqrt(line / (count * index[4].astype(F32)))[0, :4]


def unpack_rows(index, own, from_y, from_core, from_both, rows):
    block = own.shape[0]
    for at, part in enumerate((own, from_y, from_core, from_both)):
        to = pl.multiple_of(((index[0] ^ (2 * (at % 2) + at // 2)) & 3) * block, block)
        rows[pl.ds(to, block), :] = part[...].astype(rows.dtype)


def call(kernel, outs, args, scratch=(), limit=48, fetched=0, cost=0):
    vmem, hbm = pl.BlockSpec(memory_space=pltpu.VMEM), pl.BlockSpec(memory_space=pl.ANY)
    kinds = [
        pl.BlockSpec(memory_space=pltpu.SMEM)
        if arg.dtype == jnp.int32
        else hbm
        if fetched
        else vmem
        for arg in args
    ]
    scratch = [pltpu.VMEM(shape, kind) for shape, kind in scratch]
    if fetched:
        scratch += [pltpu.VMEM(arg.shape, arg.dtype) for arg in args[1 : 1 + fetched]]
        scratch += [pltpu.SemaphoreType.DMA((fetched + 4,))]
    return pl.pallas_call(
        kernel,
        out_shape=[jax.ShapeDtypeStruct(shape, kind) for shape, kind in outs],
        in_specs=kinds,
        out_specs=[vmem] * len(outs),
        scratch_shapes=scratch,
        compiler_params=pltpu.CompilerParams(vmem_limit_bytes=limit * 2**20),
        cost_estimate=pl.CostEstimate(flops=1000 + cost * 10**9, bytes_accessed=1000, transcendentals=0),
    )(*args)


def shards(
    hidden_in,
    lengths,
    positions,
    query_weight,
    key_weight,
    value_weight,
    output_weight,
    gate_weight,
    up_weight,
    down_weight,
    attention_gain,
    feedforward_gain,
    query_gain,
    key_gain,
    cotangent,
):
    ctx, why, core = lax.axis_index("ctx"), lax.axis_index("y"), lax.axis_index("core")
    local, width = hidden_in.shape[1:]
    block = local // 4
    every = 2 * local
    length = lengths[0]

    heads = query_weight.shape[1] // 2 // HD
    groups = key_weight.shape[1] // 2 // HD
    lane = 2 * HD
    wide = (heads + 2 * groups) * HD
    rows = query_weight.shape[0]
    hidden = gate_weight.shape[1] // 2
    main = hidden // 128 * 128
    assert hidden - main == HD and heads * HD == lane and groups == 1
    pack = 2 * hidden + main + lane
    own = ctx * 4 + why * 2 + core
    shard = lax.axis_index("fsdp")
    size = lax.axis_size("fsdp")
    index = jnp.stack([own, length, shard, ctx, jnp.int32(width)]).astype(jnp.int32)
    flag = length > 0

    attn_own, hidden_near, hidden_far = call(
        prelude,
        [((rows + 16, wide + lane), BF16)] + [((local // 2, width), BF16)] * 2,
        (
            index,
            query_weight,
            key_weight,
            value_weight,
            output_weight,
            attention_gain,
            feedforward_gain,
            hidden_in,
        ),
        limit=60,
        fetched=6,
    )
    if near_shards():
        attn_parts = direct([attn_own] * size)
    else:
        attn_parts = lax.all_gather(attn_own, "fsdp")
        gains = attn_parts[:, rows : rows + 8, :rows].astype(F32).transpose(1, 0, 2).reshape(8, -1)
        attn_parts = [attn_parts[:, :rows].reshape(-1, wide + lane), gains]

    def prepare(hidden_near, positions, gate_weight, up_weight, down_weight, cotangent):
        hidden_other = swap(hidden_near, "ctx")
        gu_own, down_own, *cotangent_rel = call(
            pack_feed_forward,
            [((rows, 2 * hidden), BF16), ((rows, main + lane), BF16)] + [((local // 2, width), BF16)] * 2,
            (index, gate_weight, up_weight, down_weight, cotangent),
            limit=60,
            fetched=3,
        )
        pieces = [
            lax.dynamic_slice_in_dim(positions[0], (2 * (why ^ yy) + (core ^ kk)) * block, block)
            for kk in range(2)
            for yy in range(2)
        ]
        places = jnp.concatenate(pieces).reshape(2, -1)
        places = jnp.stack([places, swap(places, "ctx")], 1).reshape(-1)
        freqs = rope_base ** (-2.0 * jnp.arange(HD // 2, dtype=F32) / HD)
        angles = places.astype(F32)[:, None] * jnp.tile(freqs, 4)[None, :]
        cosine = jnp.cos(angles)
        sine = jnp.sin(angles) * jnp.where(jnp.arange(lane) % HD < HD // 2, -1.0, 1.0)[None, :]
        hidden_other, gu_own, cosine, sine = together(hidden_other, gu_own, cosine, sine)
        return hidden_other, gu_own, down_own, cosine, sine, *cotangent_rel

    hidden_other, gu_own, down_own, cosine, sine, cotangent_near, cotangent_far = region(
        flag, prepare, hidden_near, positions, gate_weight, up_weight, down_weight, cotangent
    )
    attn_parts, gu_own, cotangent_near = together(attn_parts, gu_own, cotangent_near)
    gu_full = lax.all_gather(gu_own, "fsdp", axis=0, tiled=True)
    down_parts = [down_own]
    if near_shards():
        down_parts.append(onward(down_own))
    else:
        down_parts = [lax.all_gather(down_own, "fsdp", axis=0, tiled=True)]
    hidden_rel = (hidden_near, hidden_other, hidden_far, swap(hidden_other, "core"))
    cotangent_other = swap(cotangent_near, "ctx")
    query_row = jnp.tile(query_gain.astype(F32), 2)[None]
    key_row = jnp.concatenate([key_gain.astype(F32), jnp.ones((HD,), F32)])[None]

    def attend(hidden_rel, cosine, sine, query_row, key_row, attn_parts):
        attn_full, gains, near, far, unit, query, key, value, raw, mixed, mixed_rel, total = call(
            attention_forward,
            [((width, wide + lane), BF16), ((8, width), F32)]
            + [((every // 2, width), BF16)] * 2
            + [((every, width), BF16)]
            + [((every, lane), BF16)] * 3
            + [((every, 2 * lane), F32), ((every, lane), F32), ((every, lane), BF16), ((every, lane), F32)],
            (index, *hidden_rel, cosine, sine, query_row, key_row, *attn_parts),
            cost=8,
        )
        return near, far, gains, unit, mixed_rel, (attn_full, query, key, value, raw, mixed, total)

    near, far, gains, unit, mixed_rel, kept = region(
        flag, attend, hidden_rel, cosine, sine, query_row, key_row, attn_parts
    )
    kept = kept + (cosine, sine, query_row, key_row)
    near, down_parts = together(near, down_parts)
    if near_shards():
        down_parts.append(onward(down_parts[1]))
    quarter, whole = ((block, width // 2), BF16), ((block, width), F32)

    def add_attention(near, far, hidden_near, gains):
        return call(
            to_middle,
            [whole, ((block, lane), F32), quarter, quarter],
            (*sum_scatter(near, far), hidden_near, gains),
        )

    middle, inverse_two, *spread = region(flag, add_attention, near, far, hidden_near, gains)
    spread, cotangent_other, down_parts = together(spread, cotangent_other, down_parts)
    if near_shards():
        down_parts.append(onward(down_parts[2]))
    *unit_two, cotangent_last = region(flag, gather_plane, *spread, cotangent_other)
    if near_shards():
        unit_two, down_parts = together(unit_two, down_parts)

    cotangent_rel = (cotangent_near, cotangent_other, cotangent_far, cotangent_last)
    down_full, back = call(
        activated_gradient,
        [((width, main + lane), BF16), ((every, main + lane), F32)],
        (index, *cotangent_rel, *down_parts),
    )
    gu_full, back = together(gu_full, back)
    near, far, ff_grad, activated = call(
        feed_forward,
        [((every // 2, width), BF16)] * 2 + [((width, pack), BF16), ((every, main + lane), BF16)],
        (index, *unit_two, *cotangent_rel, back, gu_full),
        [((every, 2 * hidden), BF16)],
    )
    ff_grad, near = together(ff_grad, near)
    ff_share = lax.psum_scatter(ff_grad, "fsdp", scatter_dimension=0, tiled=True)

    def turn(near, far, middle, inverse_two, cotangent_near, gains, activated, down_full, unit, mixed_rel, kept):
        terms, branch_parts = together(
            scatter_start(near, swap(far, "core")),
            call(down_product, [((every // 2, width), BF16)] * 2, (index, activated, down_full)),
        )
        branch_far = swap(branch_parts[1], "core")
        second, middle_grad, left, right = call(
            to_middle_grad,
            [whole, whole, quarter, quarter],
            (index, *scatter_next(*terms), middle, inverse_two, cotangent_near, gains),
        )
        attention_grad = gather_end(left, swap(left, "ctx"), right, swap(right, "y"))
        attention_grad, branch_far = together(attention_grad, branch_far)
        branch = scatter_start(branch_parts[0], branch_far)
        near, far, back, head_sums = call(
            attention_backward,
            [((every // 2, width), BF16)] * 2 + [((every, 2 * lane), BF16), ((8, lane), F32)],
            (index, *attention_grad, *kept),
            [((every, lane), BF16)] + [((every, lane), F32)] * 3,
        )
        back, branch = together(back, branch)
        rows_of_branch = scatter_halves(*branch)
        back, rows_of_branch = together(back, rows_of_branch)
        branch = scatter_swap(*rows_of_branch)
        attn_grad, attention_sums = call(
            attention_weights,
            [((width, wide + lane), BF16), ((8, width), F32)],
            (index, unit, back, *attention_grad, mixed_rel, kept[0], gains),
        )
        attn_grad, branch = together(attn_grad, branch)
        return near, far, attn_grad, attention_sums, head_sums, branch, second, middle_grad

    near, far, attn_grad, attention_sums, head_sums, branch, second, middle_grad = region(
        flag,
        turn,
        near,
        far,
        middle,
        inverse_two,
        cotangent_near,
        gains,
        activated,
        down_full,
        unit,
        mixed_rel,
        kept,
    )
    attn_share = lax.psum_scatter(attn_grad, "fsdp", scatter_dimension=0, tiled=True)

    def sum_first(near, far, branch, middle, hidden_near, second, inverse, attention_sums, head_sums):
        terms = scatter_start(near, swap(far, "core"))
        branch, output = call(to_output, [whole, ((block, width), BF16)], (index, *branch, middle))
        (small,) = call(
            small_sums,
            [((24, lane), F32)],
            (index, hidden_near, middle, branch, second, inverse, attention_sums, head_sums),
        )
        small = small + hop(small, "core")
        terms, small = together(terms, small)
        terms, more = together(scatter_next(*terms), hop(small, "ctx"))
        return terms, small + more, output

    pieces, small, output = region(
        flag,
        sum_first,
        near,
        far,
        branch,
        middle,
        hidden_near,
        second,
        inverse_two,
        attention_sums,
        head_sums,
    )
    pieces, ff_share = together(pieces, ff_share)
    ff_other = swap(ff_share, "ctx")

    def finish(pieces, middle_grad, hidden_near, gains, output, small):
        (own_rows,) = call(
            to_input_grad, [((block, width), BF16)], (*pieces, middle_grad, hidden_near, gains)
        )
        own_rows, small = together(own_rows, small + hop(small, "y"))
        rows_y, rows_core = swap(own_rows, "y"), swap(own_rows, "core")
        output_y = swap(output, "y")
        rows_y, rows_core, output_y, small = together(rows_y, rows_core, output_y, small + hop(small, "fsdp"))
        (input_rows,) = call(
            unpack_rows, [((local, width), F32)], (index, own_rows, rows_y, rows_core, swap(rows_y, "core"))
        )
        step = 2
        while step < size:
            small = small + hop(small, "fsdp", step)
            step *= 2
        return together(input_rows, output_y, small)

    input_rows, output_y, small = region(flag, finish, pieces, middle_grad, hidden_near, gains, output, small)
    output_y, attn_share, ff_other = together(output_y, attn_share, ff_other)
    attn_other = swap(attn_share, "ctx")

    def unpack(index, output, output_y, ff_share, ff_other, small):
        output_core, last = swap(output, "core"), swap(output_y, "core")
        ff_grads = call(
            unpack_feed_forward,
            [((rows, 2 * hidden), F32)] * 2 + [((2 * hidden, rows), F32)],
            (index, ff_share, ff_other),
        )
        results = call(
            small_results, [((rows,), F32)] * 2 + [((HD,), F32)] * 2 + [((4,), F32)], (index, small)
        )
        output_core, last, ff_grads, results = together(output_core, last, ff_grads, results)
        (block_rows,) = call(
            unpack_rows, [((local, width), BF16)], (index, output, output_y, output_core, last)
        )
        return block_rows, ff_grads, results

    block_rows, ff_grads, results = region(flag, unpack, index, output, output_y, ff_share, ff_other, small)
    attn_other, block_rows = together(attn_other, block_rows)
    attn_grads = call(
        unpack_attention,
        [((rows, 2 * lane), F32)] + [((rows, lane), F32)] * 2 + [((2 * lane, rows), F32)],
        (index, attn_share, attn_other),
    )
    grads = (*attn_grads, *ff_grads)
    feedforward_share, attention_share, query_share, key_share, stats = results
    return (
        block_rows[None],
        input_rows[None],
        *grads,
        attention_share,
        feedforward_share,
        query_share,
        key_share,
        stats,
    )


def solution(mesh):
    fsdp, ctx, tp = (mesh.shape[axis] for axis in ("fsdp", "ctx", "tp"))
    assert ctx == 2 and tp == 4
    plane = Mesh(mesh.devices.reshape(fsdp, 2, 2, 2), ("fsdp", "ctx", "y", "core"))
    tp = ("y", "core")
    in_specs = (
        P("fsdp", "ctx", None),
        P("fsdp"),
        P("fsdp", "ctx"),
        P("fsdp", tp),
        P("fsdp", tp),
        P("fsdp", tp),
        P(tp, "fsdp"),
        P("fsdp", tp),
        P("fsdp", tp),
        P(tp, "fsdp"),
        P("fsdp"),
        P("fsdp"),
        P(),
        P(),
        P("fsdp", "ctx", None),
    )
    out_specs = (
        P("fsdp", "ctx", None),
        P("fsdp", "ctx", None),
        P("fsdp", tp),
        P("fsdp", tp),
        P("fsdp", tp),
        P(tp, "fsdp"),
        P("fsdp", tp),
        P("fsdp", tp),
        P(tp, "fsdp"),
        P("fsdp"),
        P("fsdp"),
        P(),
        P(),
        P(),
    )
    return jax.shard_map(shards, mesh=plane, in_specs=in_specs, out_specs=out_specs, check_vma=False)
```

```python
import jax
import jax.numpy as jnp
from jax import lax
from jax.experimental import pallas as pl
from jax.experimental.pallas import tpu as pltpu
from jax.sharding import Mesh, PartitionSpec as P

HD = 64
epsilon = 1e-05
rope_base = 1000000.0
F32 = jnp.float32
BF16 = jnp.bfloat16
PLANE = ("ctx", "y", "core")


def swap(value, axis):
    return lax.ppermute(value, axis, [(0, 1), (1, 0)])


def hop(value, axis, step=1):
    size = lax.axis_size(axis)
    return lax.ppermute(value, axis, [(i, i ^ step) for i in range(size)])


def scatter_start(near, far):
    rows, width = near.shape[0] // 2, near.shape[1] // 2
    low, keep = ((rows, width), BF16), ((rows, width), F32)
    left_low, right_low, left, right = call(split_sum, [low, low, keep, keep], (near, far))
    return left, swap(left_low, "ctx"), right, swap(right_low, "y")


def scatter_halves(left, from_x, right, from_y):
    rows, width = left.shape[0] // 2, left.shape[1]
    low, keep = ((rows, width), BF16), ((rows, width), F32)
    return call(split_again, [keep, low, keep, low], (left, from_x, right, from_y))


def scatter_swap(left, left_low, right, right_low):
    return left, swap(left_low, "y"), right, swap(right_low, "ctx")


def scatter_next(left, from_x, right, from_y):
    return scatter_swap(*scatter_halves(left, from_x, right, from_y))


def sum_scatter(near, far):
    return scatter_next(*scatter_start(near, swap(far, "core")))


def gather_end(left, left_x, right, right_y):
    width = left.shape[1]
    left = jnp.stack([left, left_x])
    right = jnp.stack([right, right_y])
    left = jnp.stack([left, swap(left, "y")], 1)
    right = jnp.stack([right, swap(right, "ctx")], 0)
    near = jnp.concatenate([left, right], -1).reshape(-1, 2 * width)
    return near, swap(near, "core")


def gather_plane(left, right, beside):
    beside, left_x, right_y = together(swap(beside, "core"), swap(left, "ctx"), swap(right, "y"))
    return *gather_end(left, left_x, right, right_y), beside


def near_shards():
    return lax.axis_size("fsdp") <= 4


def direct(pieces):
    size = lax.axis_size("fsdp")
    return [
        piece if step == 0 else lax.ppermute(piece, "fsdp", [(i, i ^ step) for i in range(size)])
        for step, piece in enumerate(pieces)
    ]


def onward(value):
    size = lax.axis_size("fsdp")
    return lax.ppermute(value, "fsdp", [(i, (i + 1) % size) for i in range(size)])


def together(*values):
    return lax.optimization_barrier(values)


def region(flag, work, *args):
    leaves, tree = jax.tree.flatten(jax.eval_shape(work, *args))

    def otherwise(*_):
        hbm = pl.BlockSpec(memory_space=pl.ANY)
        outs = pl.pallas_call(
            lambda *refs: None,
            out_shape=[jax.ShapeDtypeStruct(leaf.shape, leaf.dtype) for leaf in leaves],
            out_specs=[hbm] * len(leaves),
        )()
        return jax.tree.unflatten(tree, outs)

    return lax.cond(flag, work, otherwise, *args)


def lanes(shape):
    return lax.broadcasted_iota(jnp.int32, shape, len(shape) - 1)


def nt(left, right):
    return lax.dot_general(left, right, (((1,), (1,)), ((), ())), preferred_element_type=F32)


def tn(left, right):
    return lax.dot_general(left, right, (((0,), (0,)), ((), ())), preferred_element_type=F32)


def nn(left, right):
    return lax.dot_general(left, right, (((1,), (0,)), ((), ())), preferred_element_type=F32)


def half_sums(values, low):
    first = jnp.sum(jnp.where(low, values, 0.0), axis=-1, keepdims=True)
    second = jnp.sum(jnp.where(low, 0.0, values), axis=-1, keepdims=True)
    return first, second


def turned(values):
    return jnp.where(lanes(values.shape) % HD < HD // 2, pltpu.roll(values, 96, 1), pltpu.roll(values, 32, 1))


def rows_of(own, kk, xx, yy, block):
    return pl.multiple_of((own ^ (xx * 4 + yy * 2 + kk)) * block, block)


def attention_forward(
    index, h0, h1, h2, h3, cosine, sine, query_gain, key_gain, *rest
):
    *parts, w, gains, part_low, part_high, unit, query, key, value, raw, mixed, mixed_rel, inverse = rest
    own, length = index[0], index[1]
    if len(parts) > 2:
        rows = w.shape[0] // len(parts)
        for at, part in enumerate(parts):
            to = pl.multiple_of((index[2] ^ at) * rows, rows)
            w[pl.ds(to, rows), :] = part[:rows, :]
            gains[:, pl.ds(to, rows)] = part[rows : rows + 16, :rows].astype(F32)[:8]
    else:
        w[...] = parts[0][...]
        gains[...] = parts[1][...]
    gain = gains[0:1, :]
    pair = h0.shape[0]
    block = pair // 2
    low = lanes((pair, 2 * HD)) < HD
    for at, h in enumerate((h0, h1, h2, h3)):
        kk, xx = divmod(at, 2)
        here = slice(at * pair, (at + 1) * pair)
        x = h[...].astype(F32)
        r = lax.rsqrt(jnp.mean(x * x, axis=-1, keepdims=True) + epsilon)
        u = (x * r * gain).astype(BF16)
        unit[here, :] = u
        lin = nn(u, w[:, : 4 * HD])
        raw[here, :] = lin
        q, kv = lin[:, : 2 * HD], lin[:, 2 * HD :]
        one, two = half_sums(q * q, low)
        r = jnp.where(low, lax.rsqrt(one / HD + epsilon), lax.rsqrt(two / HD + epsilon))
        y = q * r * query_gain[...]
        c, s = cosine[here, :], sine[here, :]
        q = (y * c + turned(y) * s).astype(BF16).astype(F32) * HD**-0.5
        one, _ = half_sums(kv * kv, low)
        y = kv * lax.rsqrt(one / HD + epsilon) * key_gain[...]
        kv = jnp.where(low, y * c + turned(y) * s, kv)
        other = pltpu.roll(kv, HD, 1)
        k, v = jnp.where(low, kv, other), jnp.where(low, other, kv)
        for yy in range(2):
            to = rows_of(own, kk, xx, yy, block)
            some = slice(yy * block, (yy + 1) * block)
            query[pl.ds(to, block), :] = q[some].astype(BF16)
            key[pl.ds(to, block), :] = k[some].astype(BF16)
            value[pl.ds(to, block), :] = v[some].astype(BF16)
    for at in range(4):
        here = slice(at * pair, (at + 1) * pair)
        n = (at + 1) * pair
        q = query[here, :]
        q = jnp.concatenate([jnp.where(low, q, jnp.zeros_like(q)), jnp.where(low, jnp.zeros_like(q), q)])
        e = masked_exp(q, key, at, pair, length)
        total = 1.0 / jnp.sum(e, axis=-1, keepdims=True)
        o = nn((e * total).astype(BF16), value[:n, :])
        mixed[here, :] = jnp.where(low, o[:pair], o[pair:])
        inverse[here, :] = jnp.where(low, total[:pair], total[pair:])
    for at in range(4):
        kk, xx = divmod(at, 2)
        pieces = [mixed[pl.ds(rows_of(own, kk, xx, yy, block), block), :] for yy in range(2)]
        m = jnp.concatenate(pieces).astype(BF16)
        mixed_rel[at * pair : (at + 1) * pair, :] = m
        part = nt(m, w[:, 4 * HD :]).astype(BF16)
        to = part_high if kk else part_low
        to[xx * pair : (xx + 1) * pair, :] = part


def masked_exp(query, key, at, pair, length):
    parts = []
    for past in range(at + 1):
        scores = nt(query, key[past * pair : (past + 1) * pair, :])
        columns = lax.broadcasted_iota(jnp.int32, scores.shape, 1)
        here = columns < length - past * pair
        if past == at:
            here = here & (columns <= lax.broadcasted_iota(jnp.int32, scores.shape, 0) % pair)
        parts.append(jnp.where(here, jnp.exp(scores), 0.0))
    return jnp.concatenate(parts, 1)


def attention_backward(
    index, a_low, a_high, w, query, key, value, raw, mixed, inverse, cosine, sine, query_gain, key_gain,
    first_low, first_high, back, gains, down, dq, dk, dv,
):
    own, length = index[0], index[1]
    pair = a_low.shape[0] // 2
    block = pair // 2
    low = lanes((pair, 2 * HD)) < HD
    for at in range(4):
        kk, xx = divmod(at, 2)
        a = a_high if kk else a_low
        m = nn(a[xx * pair : (xx + 1) * pair, :], w[:, 4 * HD :]).astype(BF16)
        for yy in range(2):
            down[pl.ds(rows_of(own, kk, xx, yy, block), block), :] = m[yy * block : (yy + 1) * block]
    dk[...] = jnp.zeros_like(dk)
    dv[...] = jnp.zeros_like(dv)
    for at in range(4):
        here = slice(at * pair, (at + 1) * pair)
        n = (at + 1) * pair
        q, m = query[here, :], down[here, :]
        zero = jnp.zeros_like(q)
        q = jnp.concatenate([jnp.where(low, q, zero), jnp.where(low, zero, q)])
        one, two = half_sums(m.astype(F32) * mixed[here, :], low)
        drop = jnp.concatenate([one, two])
        m = jnp.concatenate([jnp.where(low, m, zero), jnp.where(low, zero, m)])
        total = jnp.concatenate([inverse[here, 0:1], inverse[here, HD : HD + 1]])
        p = masked_exp(q, key, at, pair, length) * total
        g = (p * (nt(m, value[:n, :]) - drop)).astype(BF16)
        dv[:n, :] += tn(p.astype(BF16), m)
        dk[:n, :] += tn(g, q)
        o = nn(g, key[:n, :])
        dq[here, :] = jnp.where(low, o[:pair], o[pair:]) * HD**-0.5
    query_sum = jnp.zeros((1, 2 * HD), F32)
    key_sum = jnp.zeros((1, 2 * HD), F32)
    for at in range(4):
        kk, xx = divmod(at, 2)
        here = slice(at * pair, (at + 1) * pair)
        spots = [pl.ds(rows_of(own, kk, xx, yy, block), block) for yy in range(2)]
        c, s = cosine[here, :], sine[here, :]
        x, kv = raw[here, : 2 * HD], raw[here, 2 * HD :]
        one, two = half_sums(x * x, low)
        r = jnp.where(low, lax.rsqrt(one / HD + epsilon), lax.rsqrt(two / HD + epsilon))
        z = x * r
        y = jnp.concatenate([dq[spot, :] for spot in spots])
        y = y * c - turned(y) * s
        query_sum += jnp.sum(y * z, axis=0, keepdims=True)
        y = y * query_gain[...]
        one, two = half_sums(y * z, low)
        x = r * (y - z * jnp.where(low, one / HD, two / HD))
        one, _ = half_sums(kv * kv, low)
        r = lax.rsqrt(one / HD + epsilon)
        z = kv * r
        y = jnp.concatenate([dk[spot, :] for spot in spots])
        y = y + pltpu.roll(y, HD, 1)
        y = y * c - turned(y) * s
        key_sum += jnp.sum(y * z, axis=0, keepdims=True)
        y = y * key_gain[...]
        one, _ = half_sums(y * z, low)
        v = jnp.concatenate([dv[spot, :] for spot in spots])
        kv = jnp.where(low, r * (y - z * (one / HD)), v + pltpu.roll(v, HD, 1))
        lin = jnp.concatenate([x, kv], axis=1).astype(BF16)
        back[here, :] = lin
        part = nt(lin, w[:, : 4 * HD]).astype(BF16)
        to = first_high if kk else first_low
        to[xx * pair : (xx + 1) * pair, :] = part
    gains[0:1, :] = query_sum
    gains[1:2, :] = key_sum


def activated_gradient(index, b0, b1, b2, b3, *rest):
    *parts, down_w, back = rest
    own, length = index[0], index[1]
    count, rows = len(parts), parts[0].shape[0]
    for at, part in enumerate(parts):
        to = pl.multiple_of((index[2] + count - at) % count * rows, rows)
        down_w[pl.ds(to, rows), :] = part[...]
    pair = b0.shape[0]
    block = pair // 2
    row = lax.broadcasted_iota(jnp.int32, (pair, 1), 0)
    for at, b in enumerate((b0, b1, b2, b3)):
        kk, xx = divmod(at, 2)
        ok = (own ^ (kk + 4 * xx + jnp.where(row >= block, 2, 0))) * block + row % block < length
        back[at * pair : (at + 1) * pair, :] = jnp.where(ok, nn(b[...], down_w[...]), 0.0)


def feed_forward(index, x_low, x_high, b0, b1, b2, b3, back_all, gu_w, second_low, second_high, grad, activated, gate_up):
    own, length = index[0], index[1]
    width = x_low.shape[1]
    pair = b0.shape[0]
    block, four = pair // 2, 2 * pair
    main = gate_up.shape[1] // 2 // 128 * 128
    both = 2 * main
    wide = both + 128
    low = lanes((four, 128)) < HD
    row = lax.broadcasted_iota(jnp.int32, (four, 1), 0)
    bs = (b0, b1, b2, b3)
    for kk, (x, to) in enumerate(((x_low, second_low), (x_high, second_high))):
        here = slice(kk * four, (kk + 1) * four)
        start = own ^ (kk + jnp.where(row >= pair, 4, 0) + jnp.where(row % pair >= block, 2, 0))
        ok = start * block + row % block < length
        gu = nn(x[...], gu_w[...])
        back = back_all[here, :]
        tail = gu[:, both:]
        gate = jnp.concatenate([gu[:, :main], tail], 1)
        upper = jnp.concatenate([gu[:, main:both], pltpu.roll(tail, HD, 1)], 1)
        sigmoid = 1.0 / (1.0 + jnp.exp(-gate))
        silu = gate * sigmoid
        act = jnp.where(ok, silu * upper, 0.0)
        gate_back = back * upper * (sigmoid + silu * (1.0 - sigmoid))
        upper_back = back * silu
        activated[here, :main] = act[:, :main].astype(BF16)
        activated[here, main:] = jnp.where(low, act[:, main:], 0.0).astype(BF16)
        mix = jnp.where(low, gate_back[:, main:], pltpu.roll(upper_back[:, main:], HD, 1))
        gate_up[here, :main] = gate_back[:, :main].astype(BF16)
        gate_up[here, main:both] = upper_back[:, :main].astype(BF16)
        gate_up[here, both:] = mix.astype(BF16)
        to[...] = nt(gate_up[here, :], gu_w[...]).astype(BF16)
    step = 256

    @pl.loop(0, width // step)
    def _(at):
        here = pl.ds(pl.multiple_of(at * step, step), step)
        out = tn(x_low[:, here], gate_up[:four, :]) + tn(x_high[:, here], gate_up[four:, :])
        grad[here, :wide] = out.astype(BF16)
        out = tn(b0[:, here], activated[:pair, :])
        for piece in range(1, 4):
            out += tn(bs[piece][:, here], activated[piece * pair : (piece + 1) * pair, :])
        grad[here, wide:] = out.astype(BF16)


def down_product(index, activated, down_w, branch_low, branch_high):
    four = branch_low.shape[0]
    for at, branch in ((0, branch_low), (four, branch_high)):

        @pl.loop(0, 2)
        def _(xx, at=at, branch=branch):
            here = pl.ds(pl.multiple_of(at + xx * (four // 2), four // 2), four // 2)
            some = pl.ds(pl.multiple_of(xx * (four // 2), four // 2), four // 2)
            branch[some, :] = nt(activated[here, :], down_w[...]).astype(BF16)


def split_sum(near, far, left_low, right_low, left, right):
    rows, width = left.shape
    block = rows // 2
    for xx in range(2):
        for yy in range(2):
            here = slice((2 * xx + yy) * block, (2 * xx + yy + 1) * block)
            total = near[here, :].astype(F32) + far[here, :].astype(F32)
            for to, part, sent, at in (
                ((left_low if xx else left), total[:, :width], xx, yy),
                ((right_low if yy else right), total[:, width:], yy, xx),
            ):
                to[at * block : (at + 1) * block, :] = part.astype(BF16) if sent else part


def split_again(left, from_x, right, from_y, left_out, left_low, right_out, right_low):
    block = left_out.shape[0]
    for part, other, out, low in ((left, from_x, left_out, left_low), (right, from_y, right_out, right_low)):
        total = part[...] + other[...].astype(F32)
        out[...] = total[:block]
        low[...] = total[block:].astype(BF16)


def joined(left, from_y, right, from_x):
    left = left[...] + from_y[...].astype(F32)
    return jnp.concatenate([left, right[...] + from_x[...].astype(F32)], 1)


def inverse_of(values):
    return lax.rsqrt(jnp.mean(values * values, axis=-1, keepdims=True) + epsilon)


def validity(index, block):
    row = lax.broadcasted_iota(jnp.int32, (block, 1), 0)
    return (index[0] * block + row < index[1]).astype(F32)


def halves_of(values, left, right):
    width = left.shape[1]
    left[...] = values[:, :width].astype(BF16)
    right[...] = values[:, width:].astype(BF16)


def to_middle(left, from_y, right, from_x, hidden, gains, middle, inverse, out_left, out_right):
    block = middle.shape[0]
    m = hidden[:block, :].astype(F32) + joined(left, from_y, right, from_x)
    r = inverse_of(m)
    middle[...] = m
    inverse[...] = jnp.broadcast_to(r, inverse.shape)
    halves_of(m * r * gains[1:2, :], out_left, out_right)


def to_middle_grad(
    index, left, from_y, right, from_x, middle, inverse, cotangent, gains, second, middle_grad, out_left, out_right
):
    block = middle.shape[0]
    total = joined(left, from_y, right, from_x)
    second[...] = total
    r = inverse[:, 0:1]
    u, c = middle[...] * r, total * gains[1:2, :]
    upstream = cotangent[:block, :].astype(F32) * validity(index, block)
    grad = upstream + r * (c - u * jnp.mean(c * u, axis=-1, keepdims=True))
    middle_grad[...] = grad
    halves_of(grad, out_left, out_right)


def to_output(index, left, from_y, right, from_x, middle, branch, output):
    total = joined(left, from_y, right, from_x)
    branch[...] = total
    output[...] = ((middle[...] + total) * validity(index, middle.shape[0])).astype(BF16)


def to_input_grad(left, from_y, right, from_x, middle_grad, hidden, gains, out):
    block = out.shape[0]
    x = hidden[:block, :].astype(F32)
    r = inverse_of(x)
    u = x * r
    c = joined(left, from_y, right, from_x) * gains[0:1, :]
    out[...] = (middle_grad[...] + r * (c - u * jnp.mean(c * u, axis=-1, keepdims=True))).astype(BF16)


def small_sums(index, hidden, middle, branch, second, inverse, attention_sums, head_sums, out):
    block, width = middle.shape
    valid = validity(index, block)
    x, m = hidden[:block, :].astype(F32), middle[...]
    feedforward_sums = jnp.sum(second[...] * (m * inverse[:, 0:1]), axis=0, keepdims=True)
    for at in range(width // 128):
        here = slice(at * 128, (at + 1) * 128)
        out[at : at + 1, :] = feedforward_sums[:, here]
        out[width // 128 + at : width // 128 + at + 1, :] = attention_sums[0:1, here]
    lane = lanes((1, 128))
    q = head_sums[0:1, :] + pltpu.roll(head_sums[0:1, :], HD, 1)
    out[16:17, :] = jnp.where(lane < HD, q, pltpu.roll(head_sums[1:2, :], HD, 1))
    line = jnp.where(lane == 4, jnp.sum(valid), 0.0)
    for at, item in enumerate((x, m - x, m, branch[...])):
        line = jnp.where(lane == at, jnp.sum(item * item * valid), line)
    out[17:18, :] = line
    out[18:, :] = jnp.zeros((out.shape[0] - 18, 128), F32)


def attention_weights(index, unit, back, a_low, a_high, mixed_rel, w, gains, out, gain_out):
    wide = back.shape[1]
    half = a_low.shape[0]
    step = 256
    for row in range(0, out.shape[0], step):
        here = slice(row, row + step)
        grad = tn(unit[:, here], back[...])
        out[here, :wide] = grad.astype(BF16)
        grad = jnp.sum(grad * w[here, :wide].astype(F32), axis=1, keepdims=True)
        gain_out[:, here] = jnp.broadcast_to(grad, (step, 128)).T[:8] / gains[0:1, here]
        o = tn(a_low[:, here], mixed_rel[:half, :]) + tn(a_high[:, here], mixed_rel[half:, :])
        out[here, wide:] = o.astype(BF16)


def fetch(sources, targets, sems):
    copies = [pltpu.make_async_copy(one, two, sems.at[at]) for at, (one, two) in enumerate(zip(sources, targets))]
    for copy in copies:
        copy.start()
    return copies


def halves(own, source, targets, sems, base):
    block = targets[0].shape[0] // 2
    copies = []
    for kk, target in enumerate(targets):
        for yy in range(2):
            start = pl.multiple_of(((own ^ (2 * yy + kk)) & 3) * block, block)
            to = target.at[pl.ds(yy * block, block)]
            copies.append(pltpu.make_async_copy(source.at[0, pl.ds(start, block)], to, sems.at[base + len(copies)]))
    for copy in copies:
        copy.start()
    return copies


def prelude(
    index, query_from, key_from, value_from, output_from, one_from, two_from, hidden,
    out, hidden_near, hidden_far,
    query, key, value, output, one_gain, two_gain, sems,
):
    copies = fetch(
        (query_from, key_from, value_from, output_from, one_from, two_from),
        (query, key, value, output, one_gain, two_gain),
        sems,
    )
    late = halves(index[0], hidden, (hidden_near, hidden_far), sems, len(copies))
    for copy in copies:
        copy.wait()
    rows = query.shape[0]
    wide = query.shape[1] // 2
    for half in range(2):

        @pl.when(index[3] == half)
        def _():
            out[:rows, :wide] = query[:, half * wide : (half + 1) * wide]
            low = lanes((rows, 2 * HD)) < HD
            k, v = key[...].astype(F32), value[...].astype(F32)
            if half:
                kv = jnp.where(low, pltpu.roll(k, HD, 1), v)
            else:
                kv = jnp.where(low, k, pltpu.roll(v, HD, 1))
            out[:rows, wide : wide + 2 * HD] = kv.astype(BF16)
            out[:rows, wide + 2 * HD :] = output[half * wide : (half + 1) * wide, :].astype(F32).T.astype(BF16)

    one, two = one_gain[...].astype(F32)[None], two_gain[...].astype(F32)[None]
    first = lax.broadcasted_iota(jnp.int32, (16, rows), 0) == 0
    out[rows:, :rows] = jnp.where(first, one, two).astype(BF16)
    out[rows:, rows:] = jnp.zeros((16, out.shape[1] - rows), BF16)
    for copy in late:
        copy.wait()


def pack_feed_forward(index, *rest):
    cotangent, out, down_out, cotangent_near, cotangent_far, gate, upper, down, sems = rest[3:]
    copies = fetch(rest[:3], (gate, upper, down), sems)
    late = halves(index[0], cotangent, (cotangent_near, cotangent_far), sems, len(copies))
    for copy in copies:
        copy.wait()
    rows, hidden = gate.shape[0], gate.shape[1] // 2
    main = hidden // 128 * 128
    both, wide = 2 * main, 2 * hidden
    low = lanes((rows, 128)) < HD
    for half in range(2):

        @pl.when(index[3] == half)
        def _():
            tails = []
            for at, part in enumerate((gate, upper)):
                if half:
                    part = pltpu.roll(part[:, main:].astype(F32), main + HD, 1)
                else:
                    part = part[:, : main + 128].astype(F32)
                out[:, at * main : (at + 1) * main] = part[:, :main].astype(BF16)
                tails.append(part[:, main:])
            out[:, both:wide] = jnp.where(low, tails[0], pltpu.roll(tails[1], HD, 1)).astype(BF16)
            turned = down[half * hidden : (half + 1) * hidden, :].astype(F32)
            turned = jnp.concatenate([turned, jnp.zeros((HD, rows), F32)]).T
            down_out[...] = turned.astype(BF16)
    for copy in late:
        copy.wait()


def unpack_attention(index, mine, other, query, key, value, output):
    wide = query.shape[1] // 2
    low = lanes((mine.shape[0], 2 * HD)) < HD
    for half in range(2):

        @pl.when(index[3] == half)
        def _():
            first, second = (other, mine) if half else (mine, other)
            for at, part in enumerate((first, second)):
                query[:, at * wide : (at + 1) * wide] = part[:, :wide].astype(F32)
                output[at * wide : (at + 1) * wide, :] = part[:, wide + 2 * HD :].astype(F32).T
            one = first[:, wide : wide + 2 * HD].astype(F32)
            two = second[:, wide : wide + 2 * HD].astype(F32)
            key[...] = jnp.where(low, one, pltpu.roll(two, HD, 1))
            value[...] = jnp.where(low, pltpu.roll(one, HD, 1), two)


def unpack_feed_forward(index, mine, other, gate, upper, down):
    rows, hidden = mine.shape[0], gate.shape[1] // 2
    main = hidden // 128 * 128
    both, wide = 2 * main, 2 * hidden
    low = lanes((rows, 128)) < HD
    for half in range(2):

        @pl.when(index[3] == half)
        def _():
            first, second = (other, mine) if half else (mine, other)
            for at, to in enumerate((gate, upper)):
                to[:, :main] = first[:, at * main : (at + 1) * main].astype(F32)
                one = first[:, both : both + 128].astype(F32)
                two = second[:, both : both + 128].astype(F32)
                if at:
                    one = pltpu.roll(one, HD, 1)
                else:
                    two = pltpu.roll(two, HD, 1)
                end = second[:, at * main : (at + 1) * main].astype(F32)
                end = pltpu.roll(jnp.concatenate([end, jnp.zeros((rows, 128), F32)], 1), HD, 1)
                to[:, main : main + 128] = jnp.where(low, one, end[:, :128])
                to[:, main + 128 : 2 * main] = end[:, 128:main]
                to[:, 2 * main :] = jnp.where(low, end[:, main:], two)
            for at, part in enumerate((first, second)):
                turned = part[:, wide:].astype(F32).T
                down[at * hidden : (at + 1) * hidden, :] = turned[:hidden]


def small_results(index, small, feedforward_gain, attention_gain, query_gain, key_gain, stats):
    for at, to in enumerate((feedforward_gain, attention_gain)):
        line = jnp.concatenate([small[8 * at + row : 8 * at + row + 1, :] for row in range(8)], 1)
        shift = (line.shape[1] - index[2] * to.shape[0]) % line.shape[1]
        to[...] = pltpu.roll(line, shift, 1)[0, : to.shape[0]]
    query_gain[...] = small[16:17, :][0, :HD]
    key_gain[...] = pltpu.roll(small[16:17, :], HD, 1)[0, :HD]
    line = small[17:18, :]
    count = jnp.sum(jnp.where(lanes((1, 128)) == 4, line, 0.0))
    stats[...] = jnp.sqrt(line / (count * index[4].astype(F32)))[0, :4]


def unpack_rows(index, own, from_y, from_core, from_both, rows):
    block = own.shape[0]
    for at, part in enumerate((own, from_y, from_core, from_both)):
        to = pl.multiple_of(((index[0] ^ (2 * (at % 2) + at // 2)) & 3) * block, block)
        rows[pl.ds(to, block), :] = part[...].astype(rows.dtype)


def call(kernel, outs, args, scratch=(), limit=48, fetched=0, cost=0):
    vmem, hbm = pl.BlockSpec(memory_space=pltpu.VMEM), pl.BlockSpec(memory_space=pl.ANY)
    kinds = [
        pl.BlockSpec(memory_space=pltpu.SMEM)
        if arg.dtype == jnp.int32
        else hbm
        if fetched
        else vmem
        for arg in args
    ]
    scratch = [pltpu.VMEM(shape, kind) for shape, kind in scratch]
    if fetched:
        scratch += [pltpu.VMEM(arg.shape, arg.dtype) for arg in args[1 : 1 + fetched]]
        scratch += [pltpu.SemaphoreType.DMA((fetched + 4,))]
    return pl.pallas_call(
        kernel,
        out_shape=[jax.ShapeDtypeStruct(shape, kind) for shape, kind in outs],
        in_specs=kinds,
        out_specs=[vmem] * len(outs),
        scratch_shapes=scratch,
        compiler_params=pltpu.CompilerParams(vmem_limit_bytes=limit * 2**20),
        cost_estimate=pl.CostEstimate(flops=1000 + cost * 10**9, bytes_accessed=1000, transcendentals=0),
    )(*args)


def shards(
    hidden_in,
    lengths,
    positions,
    query_weight,
    key_weight,
    value_weight,
    output_weight,
    gate_weight,
    up_weight,
    down_weight,
    attention_gain,
    feedforward_gain,
    query_gain,
    key_gain,
    cotangent,
):
    ctx, why, core = lax.axis_index("ctx"), lax.axis_index("y"), lax.axis_index("core")
    local, width = hidden_in.shape[1:]
    block = local // 4
    every = 2 * local
    length = lengths[0]

    heads = query_weight.shape[1] // 2 // HD
    groups = key_weight.shape[1] // 2 // HD
    lane = 2 * HD
    wide = (heads + 2 * groups) * HD
    rows = query_weight.shape[0]
    hidden = gate_weight.shape[1] // 2
    main = hidden // 128 * 128
    assert hidden - main == HD and heads * HD == lane and groups == 1
    pack = 2 * hidden + main + lane
    own = ctx * 4 + why * 2 + core
    shard = lax.axis_index("fsdp")
    size = lax.axis_size("fsdp")
    index = jnp.stack([own, length, shard, ctx, jnp.int32(width)]).astype(jnp.int32)
    flag = length > 0

    attn_own, hidden_near, hidden_far = call(
        prelude,
        [((rows + 16, wide + lane), BF16)] + [((local // 2, width), BF16)] * 2,
        (
            index,
            query_weight,
            key_weight,
            value_weight,
            output_weight,
            attention_gain,
            feedforward_gain,
            hidden_in,
        ),
        limit=60,
        fetched=6,
    )
    if near_shards():
        attn_parts = direct([attn_own] * size)
    else:
        attn_parts = lax.all_gather(attn_own, "fsdp")
        gains = attn_parts[:, rows : rows + 8, :rows].astype(F32).transpose(1, 0, 2).reshape(8, -1)
        attn_parts = [attn_parts[:, :rows].reshape(-1, wide + lane), gains]

    def prepare(hidden_near, positions, gate_weight, up_weight, down_weight, cotangent):
        hidden_other = swap(hidden_near, "ctx")
        gu_own, down_own, *cotangent_rel = call(
            pack_feed_forward,
            [((rows, 2 * hidden), BF16), ((rows, main + lane), BF16)] + [((local // 2, width), BF16)] * 2,
            (index, gate_weight, up_weight, down_weight, cotangent),
            limit=60,
            fetched=3,
        )
        pieces = [
            lax.dynamic_slice_in_dim(positions[0], (2 * (why ^ yy) + (core ^ kk)) * block, block)
            for kk in range(2)
            for yy in range(2)
        ]
        places = jnp.concatenate(pieces).reshape(2, -1)
        places = jnp.stack([places, swap(places, "ctx")], 1).reshape(-1)
        freqs = rope_base ** (-2.0 * jnp.arange(HD // 2, dtype=F32) / HD)
        angles = places.astype(F32)[:, None] * jnp.tile(freqs, 4)[None, :]
        cosine = jnp.cos(angles)
        sine = jnp.sin(angles) * jnp.where(jnp.arange(lane) % HD < HD // 2, -1.0, 1.0)[None, :]
        hidden_other, gu_own, cosine, sine = together(hidden_other, gu_own, cosine, sine)
        return hidden_other, gu_own, down_own, cosine, sine, *cotangent_rel

    hidden_other, gu_own, down_own, cosine, sine, cotangent_near, cotangent_far = region(
        flag, prepare, hidden_near, positions, gate_weight, up_weight, down_weight, cotangent
    )
    attn_parts, gu_own, cotangent_near = together(attn_parts, gu_own, cotangent_near)
    gu_full = lax.all_gather(gu_own, "fsdp", axis=0, tiled=True)
    down_parts = [down_own]
    if near_shards():
        down_parts.append(onward(down_own))
    else:
        down_parts = [lax.all_gather(down_own, "fsdp", axis=0, tiled=True)]
    hidden_rel = (hidden_near, hidden_other, hidden_far, swap(hidden_other, "core"))
    cotangent_other = swap(cotangent_near, "ctx")
    query_row = jnp.tile(query_gain.astype(F32), 2)[None]
    key_row = jnp.concatenate([key_gain.astype(F32), jnp.ones((HD,), F32)])[None]

    def attend(hidden_rel, cosine, sine, query_row, key_row, attn_parts):
        attn_full, gains, near, far, unit, query, key, value, raw, mixed, mixed_rel, total = call(
            attention_forward,
            [((width, wide + lane), BF16), ((8, width), F32)]
            + [((every // 2, width), BF16)] * 2
            + [((every, width), BF16)]
            + [((every, lane), BF16)] * 3
            + [((every, 2 * lane), F32), ((every, lane), F32), ((every, lane), BF16), ((every, lane), F32)],
            (index, *hidden_rel, cosine, sine, query_row, key_row, *attn_parts),
            cost=8,
        )
        return near, far, gains, unit, mixed_rel, (attn_full, query, key, value, raw, mixed, total)

    near, far, gains, unit, mixed_rel, kept = region(
        flag, attend, hidden_rel, cosine, sine, query_row, key_row, attn_parts
    )
    kept = kept + (cosine, sine, query_row, key_row)
    near, down_parts = together(near, down_parts)
    if near_shards():
        down_parts.append(onward(down_parts[1]))
    quarter, whole = ((block, width // 2), BF16), ((block, width), F32)

    def add_attention(near, far, hidden_near, gains):
        return call(
            to_middle,
            [whole, ((block, lane), F32), quarter, quarter],
            (*sum_scatter(near, far), hidden_near, gains),
        )

    middle, inverse_two, *spread = region(flag, add_attention, near, far, hidden_near, gains)
    spread, cotangent_other, down_parts = together(spread, cotangent_other, down_parts)
    if near_shards():
        down_parts.append(onward(down_parts[2]))
    *unit_two, cotangent_last = region(flag, gather_plane, *spread, cotangent_other)
    if near_shards():
        unit_two, down_parts = together(unit_two, down_parts)

    cotangent_rel = (cotangent_near, cotangent_other, cotangent_far, cotangent_last)
    down_full, back = call(
        activated_gradient,
        [((width, main + lane), BF16), ((every, main + lane), F32)],
        (index, *cotangent_rel, *down_parts),
    )
    gu_full, back = together(gu_full, back)
    near, far, ff_grad, activated = call(
        feed_forward,
        [((every // 2, width), BF16)] * 2 + [((width, pack), BF16), ((every, main + lane), BF16)],
        (index, *unit_two, *cotangent_rel, back, gu_full),
        [((every, 2 * hidden), BF16)],
    )
    ff_grad, near = together(ff_grad, near)
    ff_share = lax.psum_scatter(ff_grad, "fsdp", scatter_dimension=0, tiled=True)

    def turn(near, far, middle, inverse_two, cotangent_near, gains, activated, down_full, unit, mixed_rel, kept):
        terms, branch_parts = together(
            scatter_start(near, swap(far, "core")),
            call(down_product, [((every // 2, width), BF16)] * 2, (index, activated, down_full)),
        )
        branch_far = swap(branch_parts[1], "core")
        second, middle_grad, left, right = call(
            to_middle_grad,
            [whole, whole, quarter, quarter],
            (index, *scatter_next(*terms), middle, inverse_two, cotangent_near, gains),
        )
        attention_grad = gather_end(left, swap(left, "ctx"), right, swap(right, "y"))
        attention_grad, branch_far = together(attention_grad, branch_far)
        branch = scatter_start(branch_parts[0], branch_far)
        near, far, back, head_sums = call(
            attention_backward,
            [((every // 2, width), BF16)] * 2 + [((every, 2 * lane), BF16), ((8, lane), F32)],
            (index, *attention_grad, *kept),
            [((every, lane), BF16)] + [((every, lane), F32)] * 3,
        )
        back, branch = together(back, branch)
        rows_of_branch = scatter_halves(*branch)
        back, rows_of_branch = together(back, rows_of_branch)
        branch = scatter_swap(*rows_of_branch)
        attn_grad, attention_sums = call(
            attention_weights,
            [((width, wide + lane), BF16), ((8, width), F32)],
            (index, unit, back, *attention_grad, mixed_rel, kept[0], gains),
        )
        attn_grad, branch = together(attn_grad, branch)
        return near, far, attn_grad, attention_sums, head_sums, branch, second, middle_grad

    near, far, attn_grad, attention_sums, head_sums, branch, second, middle_grad = region(
        flag,
        turn,
        near,
        far,
        middle,
        inverse_two,
        cotangent_near,
        gains,
        activated,
        down_full,
        unit,
        mixed_rel,
        kept,
    )
    attn_share = lax.psum_scatter(attn_grad, "fsdp", scatter_dimension=0, tiled=True)

    def sum_first(near, far, branch, middle, hidden_near, second, inverse, attention_sums, head_sums):
        terms = scatter_start(near, swap(far, "core"))
        branch, output = call(to_output, [whole, ((block, width), BF16)], (index, *branch, middle))
        (small,) = call(
            small_sums,
            [((24, lane), F32)],
            (index, hidden_near, middle, branch, second, inverse, attention_sums, head_sums),
        )
        small = small + hop(small, "core")
        terms, small = together(terms, small)
        terms, more = together(scatter_next(*terms), hop(small, "ctx"))
        return terms, small + more, output

    pieces, small, output = region(
        flag,
        sum_first,
        near,
        far,
        branch,
        middle,
        hidden_near,
        second,
        inverse_two,
        attention_sums,
        head_sums,
    )
    pieces, ff_share = together(pieces, ff_share)
    ff_other = swap(ff_share, "ctx")

    def finish(pieces, middle_grad, hidden_near, gains, output, small):
        (own_rows,) = call(
            to_input_grad, [((block, width), BF16)], (*pieces, middle_grad, hidden_near, gains)
        )
        own_rows, small = together(own_rows, small + hop(small, "y"))
        rows_y, rows_core = swap(own_rows, "y"), swap(own_rows, "core")
        output_y = swap(output, "y")
        rows_y, rows_core, output_y, small = together(rows_y, rows_core, output_y, small + hop(small, "fsdp"))
        (input_rows,) = call(
            unpack_rows, [((local, width), F32)], (index, own_rows, rows_y, rows_core, swap(rows_y, "core"))
        )
        step = 2
        while step < size:
            small = small + hop(small, "fsdp", step)
            step *= 2
        return together(input_rows, output_y, small)

    input_rows, output_y, small = region(flag, finish, pieces, middle_grad, hidden_near, gains, output, small)
    output_y, attn_share, ff_other = together(output_y, attn_share, ff_other)
    attn_other = swap(attn_share, "ctx")

    def unpack(index, output, output_y, ff_share, ff_other, small):
        output_core, last = swap(output, "core"), swap(output_y, "core")
        ff_grads = call(
            unpack_feed_forward,
            [((rows, 2 * hidden), F32)] * 2 + [((2 * hidden, rows), F32)],
            (index, ff_share, ff_other),
        )
        results = call(
            small_results, [((rows,), F32)] * 2 + [((HD,), F32)] * 2 + [((4,), F32)], (index, small)
        )
        output_core, last, ff_grads, results = together(output_core, last, ff_grads, results)
        (block_rows,) = call(
            unpack_rows, [((local, width), BF16)], (index, output, output_y, output_core, last)
        )
        return block_rows, ff_grads, results

    block_rows, ff_grads, results = region(flag, unpack, index, output, output_y, ff_share, ff_other, small)
    attn_other, block_rows = together(attn_other, block_rows)
    attn_grads = call(
        unpack_attention,
        [((rows, 2 * lane), F32)] + [((rows, lane), F32)] * 2 + [((2 * lane, rows), F32)],
        (index, attn_share, attn_other),
    )
    grads = (*attn_grads, *ff_grads)
    feedforward_share, attention_share, query_share, key_share, stats = results
    return (
        block_rows[None],
        input_rows[None],
        *grads,
        attention_share,
        feedforward_share,
        query_share,
        key_share,
        stats,
    )


def solution(mesh):
    fsdp, ctx, tp = (mesh.shape[axis] for axis in ("fsdp", "ctx", "tp"))
    assert ctx == 2 and tp == 4
    plane = Mesh(mesh.devices.reshape(fsdp, 2, 2, 2), ("fsdp", "ctx", "y", "core"))
    tp = ("y", "core")
    in_specs = (
        P("fsdp", "ctx", None),
        P("fsdp"),
        P("fsdp", "ctx"),
        P("fsdp", tp),
        P("fsdp", tp),
        P("fsdp", tp),
        P(tp, "fsdp"),
        P("fsdp", tp),
        P("fsdp", tp),
        P(tp, "fsdp"),
        P("fsdp"),
        P("fsdp"),
        P(),
        P(),
        P("fsdp", "ctx", None),
    )
    out_specs = (
        P("fsdp", "ctx", None),
        P("fsdp", "ctx", None),
        P("fsdp", tp),
        P("fsdp", tp),
        P("fsdp", tp),
        P(tp, "fsdp"),
        P("fsdp", tp),
        P("fsdp", tp),
        P(tp, "fsdp"),
        P("fsdp"),
        P("fsdp"),
        P(),
        P(),
        P(),
    )
    return jax.shard_map(shards, mesh=plane, in_specs=in_specs, out_specs=out_specs, check_vma=False)
```

```python
import jax
import jax.numpy as jnp
from jax import lax
from jax.experimental import pallas as pl
from jax.experimental.pallas import tpu as pltpu
from jax.sharding import Mesh, PartitionSpec as P

HD = 64
epsilon = 1e-05
rope_base = 1000000.0
F32 = jnp.float32
BF16 = jnp.bfloat16
PLANE = ("ctx", "y", "core")


def swap(value, axis):
    return lax.ppermute(value, axis, [(0, 1), (1, 0)])


def hop(value, axis, step=1):
    size = lax.axis_size(axis)
    return lax.ppermute(value, axis, [(i, i ^ step) for i in range(size)])


def scatter_start(near, far):
    rows, width = near.shape[0] // 2, near.shape[1] // 2
    low, keep = ((rows, width), BF16), ((rows, width), F32)
    left_low, right_low, left, right = call(split_sum, [low, low, keep, keep], (near, far))
    return left, swap(left_low, "ctx"), right, swap(right_low, "y")


def scatter_halves(left, from_x, right, from_y):
    rows, width = left.shape[0] // 2, left.shape[1]
    low, keep = ((rows, width), BF16), ((rows, width), F32)
    return call(split_again, [keep, low, keep, low], (left, from_x, right, from_y))


def scatter_swap(left, left_low, right, right_low):
    return left, swap(left_low, "y"), right, swap(right_low, "ctx")


def scatter_next(left, from_x, right, from_y):
    return scatter_swap(*scatter_halves(left, from_x, right, from_y))


def sum_scatter(near, far):
    return scatter_next(*scatter_start(near, swap(far, "core")))


def gather_end(left, left_x, right, right_y):
    width = left.shape[1]
    left = jnp.stack([left, left_x])
    right = jnp.stack([right, right_y])
    left = jnp.stack([left, swap(left, "y")], 1)
    right = jnp.stack([right, swap(right, "ctx")], 0)
    near = jnp.concatenate([left, right], -1).reshape(-1, 2 * width)
    return near, swap(near, "core")


def gather_plane(left, right, beside):
    beside, left_x, right_y = together(swap(beside, "core"), swap(left, "ctx"), swap(right, "y"))
    return *gather_end(left, left_x, right, right_y), beside


def near_shards():
    return lax.axis_size("fsdp") <= 4


def direct(pieces):
    size = lax.axis_size("fsdp")
    return [
        piece if step == 0 else lax.ppermute(piece, "fsdp", [(i, i ^ step) for i in range(size)])
        for step, piece in enumerate(pieces)
    ]


def onward(value):
    size = lax.axis_size("fsdp")
    return lax.ppermute(value, "fsdp", [(i, (i + 1) % size) for i in range(size)])


def together(*values):
    return lax.optimization_barrier(values)


def region(flag, work, *args):
    leaves, tree = jax.tree.flatten(jax.eval_shape(work, *args))

    def otherwise(*_):
        hbm = pl.BlockSpec(memory_space=pl.ANY)
        outs = pl.pallas_call(
            lambda *refs: None,
            out_shape=[jax.ShapeDtypeStruct(leaf.shape, leaf.dtype) for leaf in leaves],
            out_specs=[hbm] * len(leaves),
        )()
        return jax.tree.unflatten(tree, outs)

    return lax.cond(flag, work, otherwise, *args)


def lanes(shape):
    return lax.broadcasted_iota(jnp.int32, shape, len(shape) - 1)


def nt(left, right):
    return lax.dot_general(left, right, (((1,), (1,)), ((), ())), preferred_element_type=F32)


def tn(left, right):
    return lax.dot_general(left, right, (((0,), (0,)), ((), ())), preferred_element_type=F32)


def nn(left, right):
    return lax.dot_general(left, right, (((1,), (0,)), ((), ())), preferred_element_type=F32)


def half_sums(values, low):
    first = jnp.sum(jnp.where(low, values, 0.0), axis=-1, keepdims=True)
    second = jnp.sum(jnp.where(low, 0.0, values), axis=-1, keepdims=True)
    return first, second


def turned(values):
    return jnp.where(lanes(values.shape) % HD < HD // 2, pltpu.roll(values, 96, 1), pltpu.roll(values, 32, 1))


def rows_of(own, kk, xx, yy, block):
    return pl.multiple_of((own ^ (xx * 4 + yy * 2 + kk)) * block, block)


def attention_forward(
    index, h0, h1, h2, h3, cosine, sine, query_gain, key_gain, *rest
):
    *parts, w, gains, part_low, part_high, unit, query, key, value, raw, mixed, mixed_rel, inverse = rest
    own, length = index[0], index[1]
    if len(parts) > 2:
        rows = w.shape[0] // len(parts)
        for at, part in enumerate(parts):
            to = pl.multiple_of((index[2] ^ at) * rows, rows)
            w[pl.ds(to, rows), :] = part[:rows, :]
            gains[:, pl.ds(to, rows)] = part[rows : rows + 16, :rows].astype(F32)[:8]
    else:
        w[...] = parts[0][...]
        gains[...] = parts[1][...]
    gain = gains[0:1, :]
    pair = h0.shape[0]
    block = pair // 2
    low = lanes((pair, 2 * HD)) < HD
    for at, h in enumerate((h0, h1, h2, h3)):
        kk, xx = divmod(at, 2)
        here = slice(at * pair, (at + 1) * pair)
        x = h[...].astype(F32)
        r = lax.rsqrt(jnp.mean(x * x, axis=-1, keepdims=True) + epsilon)
        u = (x * r * gain).astype(BF16)
        unit[here, :] = u
        lin = nn(u, w[:, : 4 * HD])
        raw[here, :] = lin
        q, kv = lin[:, : 2 * HD], lin[:, 2 * HD :]
        one, two = half_sums(q * q, low)
        r = jnp.where(low, lax.rsqrt(one / HD + epsilon), lax.rsqrt(two / HD + epsilon))
        y = q * r * query_gain[...]
        c, s = cosine[here, :], sine[here, :]
        q = (y * c + turned(y) * s).astype(BF16).astype(F32) * HD**-0.5
        one, _ = half_sums(kv * kv, low)
        y = kv * lax.rsqrt(one / HD + epsilon) * key_gain[...]
        kv = jnp.where(low, y * c + turned(y) * s, kv)
        other = pltpu.roll(kv, HD, 1)
        k, v = jnp.where(low, kv, other), jnp.where(low, other, kv)
        for yy in range(2):
            to = rows_of(own, kk, xx, yy, block)
            some = slice(yy * block, (yy + 1) * block)
            query[pl.ds(to, block), :] = q[some].astype(BF16)
            key[pl.ds(to, block), :] = k[some].astype(BF16)
            value[pl.ds(to, block), :] = v[some].astype(BF16)
    for at in range(4):
        here = slice(at * pair, (at + 1) * pair)
        n = (at + 1) * pair
        q = query[here, :]
        q = jnp.concatenate([jnp.where(low, q, jnp.zeros_like(q)), jnp.where(low, jnp.zeros_like(q), q)])
        e = masked_exp(q, key, at, pair, length)
        total = 1.0 / jnp.sum(e, axis=-1, keepdims=True)
        o = nn((e * total).astype(BF16), value[:n, :])
        mixed[here, :] = jnp.where(low, o[:pair], o[pair:])
        inverse[here, :] = jnp.where(low, total[:pair], total[pair:])
    for at in range(4):
        kk, xx = divmod(at, 2)
        pieces = [mixed[pl.ds(rows_of(own, kk, xx, yy, block), block), :] for yy in range(2)]
        m = jnp.concatenate(pieces).astype(BF16)
        mixed_rel[at * pair : (at + 1) * pair, :] = m
        part = nt(m, w[:, 4 * HD :]).astype(BF16)
        to = part_high if kk else part_low
        to[xx * pair : (xx + 1) * pair, :] = part


def masked_exp(query, key, at, pair, length):
    parts = []
    for past in range(at + 1):
        scores = nt(query, key[past * pair : (past + 1) * pair, :])
        columns = lax.broadcasted_iota(jnp.int32, scores.shape, 1)
        here = columns < length - past * pair
        if past == at:
            here = here & (columns <= lax.broadcasted_iota(jnp.int32, scores.shape, 0) % pair)
        parts.append(jnp.where(here, jnp.exp(scores), 0.0))
    return jnp.concatenate(parts, 1)


def attention_backward(
    index, a_low, a_high, w, query, key, value, raw, mixed, inverse, cosine, sine, query_gain, key_gain,
    first_low, first_high, back, gains, down, dq, dk, dv,
):
    own, length = index[0], index[1]
    pair = a_low.shape[0] // 2
    block = pair // 2
    low = lanes((pair, 2 * HD)) < HD
    for at in range(4):
        kk, xx = divmod(at, 2)
        a = a_high if kk else a_low
        m = nn(a[xx * pair : (xx + 1) * pair, :], w[:, 4 * HD :]).astype(BF16)
        for yy in range(2):
            down[pl.ds(rows_of(own, kk, xx, yy, block), block), :] = m[yy * block : (yy + 1) * block]
    dk[...] = jnp.zeros_like(dk)
    dv[...] = jnp.zeros_like(dv)
    for at in range(4):
        here = slice(at * pair, (at + 1) * pair)
        n = (at + 1) * pair
        q, m = query[here, :], down[here, :]
        zero = jnp.zeros_like(q)
        q = jnp.concatenate([jnp.where(low, q, zero), jnp.where(low, zero, q)])
        one, two = half_sums(m.astype(F32) * mixed[here, :], low)
        drop = jnp.concatenate([one, two])
        m = jnp.concatenate([jnp.where(low, m, zero), jnp.where(low, zero, m)])
        total = jnp.concatenate([inverse[here, 0:1], inverse[here, HD : HD + 1]])
        p = masked_exp(q, key, at, pair, length) * total
        g = (p * (nt(m, value[:n, :]) - drop)).astype(BF16)
        dv[:n, :] += tn(p.astype(BF16), m)
        dk[:n, :] += tn(g, q)
        o = nn(g, key[:n, :])
        dq[here, :] = jnp.where(low, o[:pair], o[pair:]) * HD**-0.5
    query_sum = jnp.zeros((1, 2 * HD), F32)
    key_sum = jnp.zeros((1, 2 * HD), F32)
    for at in range(4):
        kk, xx = divmod(at, 2)
        here = slice(at * pair, (at + 1) * pair)
        spots = [pl.ds(rows_of(own, kk, xx, yy, block), block) for yy in range(2)]
        c, s = cosine[here, :], sine[here, :]
        x, kv = raw[here, : 2 * HD], raw[here, 2 * HD :]
        one, two = half_sums(x * x, low)
        r = jnp.where(low, lax.rsqrt(one / HD + epsilon), lax.rsqrt(two / HD + epsilon))
        z = x * r
        y = jnp.concatenate([dq[spot, :] for spot in spots])
        y = y * c - turned(y) * s
        query_sum += jnp.sum(y * z, axis=0, keepdims=True)
        y = y * query_gain[...]
        one, two = half_sums(y * z, low)
        x = r * (y - z * jnp.where(low, one / HD, two / HD))
        one, _ = half_sums(kv * kv, low)
        r = lax.rsqrt(one / HD + epsilon)
        z = kv * r
        y = jnp.concatenate([dk[spot, :] for spot in spots])
        y = y + pltpu.roll(y, HD, 1)
        y = y * c - turned(y) * s
        key_sum += jnp.sum(y * z, axis=0, keepdims=True)
        y = y * key_gain[...]
        one, _ = half_sums(y * z, low)
        v = jnp.concatenate([dv[spot, :] for spot in spots])
        kv = jnp.where(low, r * (y - z * (one / HD)), v + pltpu.roll(v, HD, 1))
        lin = jnp.concatenate([x, kv], axis=1).astype(BF16)
        back[here, :] = lin
        part = nt(lin, w[:, : 4 * HD]).astype(BF16)
        to = first_high if kk else first_low
        to[xx * pair : (xx + 1) * pair, :] = part
    gains[0:1, :] = query_sum
    gains[1:2, :] = key_sum


def activated_gradient(index, b0, b1, b2, b3, *rest):
    *parts, down_w, back = rest
    own, length = index[0], index[1]
    count, rows = len(parts), parts[0].shape[0]
    for at, part in enumerate(parts):
        to = pl.multiple_of((index[2] + count - at) % count * rows, rows)
        down_w[pl.ds(to, rows), :] = part[...]
    pair = b0.shape[0]
    block = pair // 2
    row = lax.broadcasted_iota(jnp.int32, (pair, 1), 0)
    for at, b in enumerate((b0, b1, b2, b3)):
        kk, xx = divmod(at, 2)
        ok = (own ^ (kk + 4 * xx + jnp.where(row >= block, 2, 0))) * block + row % block < length
        back[at * pair : (at + 1) * pair, :] = jnp.where(ok, nn(b[...], down_w[...]), 0.0)


def feed_forward(index, x_low, x_high, b0, b1, b2, b3, back_all, gu_w, second_low, second_high, grad, activated, gate_up):
    own, length = index[0], index[1]
    width = x_low.shape[1]
    pair = b0.shape[0]
    block, four = pair // 2, 2 * pair
    main = gate_up.shape[1] // 2 // 128 * 128
    both = 2 * main
    wide = both + 128
    low = lanes((four, 128)) < HD
    row = lax.broadcasted_iota(jnp.int32, (four, 1), 0)
    bs = (b0, b1, b2, b3)
    for kk, (x, to) in enumerate(((x_low, second_low), (x_high, second_high))):
        here = slice(kk * four, (kk + 1) * four)
        start = own ^ (kk + jnp.where(row >= pair, 4, 0) + jnp.where(row % pair >= block, 2, 0))
        ok = start * block + row % block < length
        gu = nn(x[...], gu_w[...])
        back = back_all[here, :]
        tail = gu[:, both:]
        gate = jnp.concatenate([gu[:, :main], tail], 1)
        upper = jnp.concatenate([gu[:, main:both], pltpu.roll(tail, HD, 1)], 1)
        sigmoid = 1.0 / (1.0 + jnp.exp(-gate))
        silu = gate * sigmoid
        act = jnp.where(ok, silu * upper, 0.0)
        gate_back = back * upper * (sigmoid + silu * (1.0 - sigmoid))
        upper_back = back * silu
        activated[here, :main] = act[:, :main].astype(BF16)
        activated[here, main:] = jnp.where(low, act[:, main:], 0.0).astype(BF16)
        mix = jnp.where(low, gate_back[:, main:], pltpu.roll(upper_back[:, main:], HD, 1))
        gate_up[here, :main] = gate_back[:, :main].astype(BF16)
        gate_up[here, main:both] = upper_back[:, :main].astype(BF16)
        gate_up[here, both:] = mix.astype(BF16)
        to[...] = nt(gate_up[here, :], gu_w[...]).astype(BF16)
    step = 256

    @pl.loop(0, width // step)
    def _(at):
        here = pl.ds(pl.multiple_of(at * step, step), step)
        out = tn(x_low[:, here], gate_up[:four, :]) + tn(x_high[:, here], gate_up[four:, :])
        grad[here, :wide] = out.astype(BF16)
        out = tn(b0[:, here], activated[:pair, :])
        for piece in range(1, 4):
            out += tn(bs[piece][:, here], activated[piece * pair : (piece + 1) * pair, :])
        grad[here, wide:] = out.astype(BF16)


def down_product(index, activated, down_w, branch_low, branch_high):
    four = branch_low.shape[0]
    for at, branch in ((0, branch_low), (four, branch_high)):

        @pl.loop(0, 2)
        def _(xx, at=at, branch=branch):
            here = pl.ds(pl.multiple_of(at + xx * (four // 2), four // 2), four // 2)
            some = pl.ds(pl.multiple_of(xx * (four // 2), four // 2), four // 2)
            branch[some, :] = nt(activated[here, :], down_w[...]).astype(BF16)


def split_sum(near, far, left_low, right_low, left, right):
    rows, width = left.shape
    block = rows // 2
    for xx in range(2):
        for yy in range(2):
            here = slice((2 * xx + yy) * block, (2 * xx + yy + 1) * block)
            total = near[here, :].astype(F32) + far[here, :].astype(F32)
            for to, part, sent, at in (
                ((left_low if xx else left), total[:, :width], xx, yy),
                ((right_low if yy else right), total[:, width:], yy, xx),
            ):
                to[at * block : (at + 1) * block, :] = part.astype(BF16) if sent else part


def split_again(left, from_x, right, from_y, left_out, left_low, right_out, right_low):
    block = left_out.shape[0]
    for part, other, out, low in ((left, from_x, left_out, left_low), (right, from_y, right_out, right_low)):
        total = part[...] + other[...].astype(F32)
        out[...] = total[:block]
        low[...] = total[block:].astype(BF16)


def joined(left, from_y, right, from_x):
    left = left[...] + from_y[...].astype(F32)
    return jnp.concatenate([left, right[...] + from_x[...].astype(F32)], 1)


def inverse_of(values):
    return lax.rsqrt(jnp.mean(values * values, axis=-1, keepdims=True) + epsilon)


def validity(index, block):
    row = lax.broadcasted_iota(jnp.int32, (block, 1), 0)
    return (index[0] * block + row < index[1]).astype(F32)


def halves_of(values, left, right):
    width = left.shape[1]
    left[...] = values[:, :width].astype(BF16)
    right[...] = values[:, width:].astype(BF16)


def to_middle(left, from_y, right, from_x, hidden, gains, middle, inverse, out_left, out_right):
    block = middle.shape[0]
    m = hidden[:block, :].astype(F32) + joined(left, from_y, right, from_x)
    r = inverse_of(m)
    middle[...] = m
    inverse[...] = jnp.broadcast_to(r, inverse.shape)
    halves_of(m * r * gains[1:2, :], out_left, out_right)


def to_middle_grad(
    index, left, from_y, right, from_x, middle, inverse, cotangent, gains, second, middle_grad, out_left, out_right
):
    block = middle.shape[0]
    total = joined(left, from_y, right, from_x)
    second[...] = total
    r = inverse[:, 0:1]
    u, c = middle[...] * r, total * gains[1:2, :]
    upstream = cotangent[:block, :].astype(F32) * validity(index, block)
    grad = upstream + r * (c - u * jnp.mean(c * u, axis=-1, keepdims=True))
    middle_grad[...] = grad
    halves_of(grad, out_left, out_right)


def to_output(index, left, from_y, right, from_x, middle, branch, output):
    total = joined(left, from_y, right, from_x)
    branch[...] = total
    output[...] = ((middle[...] + total) * validity(index, middle.shape[0])).astype(BF16)


def to_input_grad(left, from_y, right, from_x, middle_grad, hidden, gains, out):
    block = out.shape[0]
    x = hidden[:block, :].astype(F32)
    r = inverse_of(x)
    u = x * r
    c = joined(left, from_y, right, from_x) * gains[0:1, :]
    out[...] = (middle_grad[...] + r * (c - u * jnp.mean(c * u, axis=-1, keepdims=True))).astype(BF16)


def small_sums(index, hidden, middle, branch, second, inverse, attention_sums, head_sums, out):
    block, width = middle.shape
    valid = validity(index, block)
    x, m = hidden[:block, :].astype(F32), middle[...]
    feedforward_sums = jnp.sum(second[...] * (m * inverse[:, 0:1]), axis=0, keepdims=True)
    for at in range(width // 128):
        here = slice(at * 128, (at + 1) * 128)
        out[at : at + 1, :] = feedforward_sums[:, here]
        out[width // 128 + at : width // 128 + at + 1, :] = attention_sums[0:1, here]
    lane = lanes((1, 128))
    q = head_sums[0:1, :] + pltpu.roll(head_sums[0:1, :], HD, 1)
    out[16:17, :] = jnp.where(lane < HD, q, pltpu.roll(head_sums[1:2, :], HD, 1))
    line = jnp.where(lane == 4, jnp.sum(valid), 0.0)
    for at, item in enumerate((x, m - x, m, branch[...])):
        line = jnp.where(lane == at, jnp.sum(item * item * valid), line)
    out[17:18, :] = line
    out[18:, :] = jnp.zeros((out.shape[0] - 18, 128), F32)


def attention_weights(index, unit, back, a_low, a_high, mixed_rel, w, gains, out, gain_out):
    wide = back.shape[1]
    half = a_low.shape[0]
    step = 256
    for row in range(0, out.shape[0], step):
        here = slice(row, row + step)
        grad = tn(unit[:, here], back[...])
        out[here, :wide] = grad.astype(BF16)
        grad = jnp.sum(grad * w[here, :wide].astype(F32), axis=1, keepdims=True)
        gain_out[:, here] = jnp.broadcast_to(grad, (step, 128)).T[:8] / gains[0:1, here]
        o = tn(a_low[:, here], mixed_rel[:half, :]) + tn(a_high[:, here], mixed_rel[half:, :])
        out[here, wide:] = o.astype(BF16)


def fetch(sources, targets, sems):
    copies = [pltpu.make_async_copy(one, two, sems.at[at]) for at, (one, two) in enumerate(zip(sources, targets))]
    for copy in copies:
        copy.start()
    return copies


def halves(own, source, targets, sems, base):
    block = targets[0].shape[0] // 2
    copies = []
    for kk, target in enumerate(targets):
        for yy in range(2):
            start = pl.multiple_of(((own ^ (2 * yy + kk)) & 3) * block, block)
            to = target.at[pl.ds(yy * block, block)]
            copies.append(pltpu.make_async_copy(source.at[0, pl.ds(start, block)], to, sems.at[base + len(copies)]))
    for copy in copies:
        copy.start()
    return copies


def prelude(
    index, query_from, key_from, value_from, output_from, one_from, two_from, hidden,
    out, hidden_near, hidden_far,
    query, key, value, output, one_gain, two_gain, sems,
):
    copies = fetch(
        (query_from, key_from, value_from, output_from, one_from, two_from),
        (query, key, value, output, one_gain, two_gain),
        sems,
    )
    late = halves(index[0], hidden, (hidden_near, hidden_far), sems, len(copies))
    for copy in copies:
        copy.wait()
    rows = query.shape[0]
    wide = query.shape[1] // 2
    for half in range(2):

        @pl.when(index[3] == half)
        def _():
            out[:rows, :wide] = query[:, half * wide : (half + 1) * wide]
            low = lanes((rows, 2 * HD)) < HD
            k, v = key[...].astype(F32), value[...].astype(F32)
            if half:
                kv = jnp.where(low, pltpu.roll(k, HD, 1), v)
            else:
                kv = jnp.where(low, k, pltpu.roll(v, HD, 1))
            out[:rows, wide : wide + 2 * HD] = kv.astype(BF16)
            out[:rows, wide + 2 * HD :] = output[half * wide : (half + 1) * wide, :].astype(F32).T.astype(BF16)

    one, two = one_gain[...].astype(F32)[None], two_gain[...].astype(F32)[None]
    first = lax.broadcasted_iota(jnp.int32, (16, rows), 0) == 0
    out[rows:, :rows] = jnp.where(first, one, two).astype(BF16)
    out[rows:, rows:] = jnp.zeros((16, out.shape[1] - rows), BF16)
    for copy in late:
        copy.wait()


def pack_feed_forward(index, *rest):
    cotangent, out, down_out, cotangent_near, cotangent_far, gate, upper, down, sems = rest[3:]
    copies = fetch(rest[:3], (gate, upper, down), sems)
    late = halves(index[0], cotangent, (cotangent_near, cotangent_far), sems, len(copies))
    for copy in copies:
        copy.wait()
    rows, hidden = gate.shape[0], gate.shape[1] // 2
    main = hidden // 128 * 128
    both, wide = 2 * main, 2 * hidden
    low = lanes((rows, 128)) < HD
    for half in range(2):

        @pl.when(index[3] == half)
        def _():
            tails = []
            for at, part in enumerate((gate, upper)):
                if half:
                    part = pltpu.roll(part[:, main:].astype(F32), main + HD, 1)
                else:
                    part = part[:, : main + 128].astype(F32)
                out[:, at * main : (at + 1) * main] = part[:, :main].astype(BF16)
                tails.append(part[:, main:])
            out[:, both:wide] = jnp.where(low, tails[0], pltpu.roll(tails[1], HD, 1)).astype(BF16)
            turned = down[half * hidden : (half + 1) * hidden, :].astype(F32)
            turned = jnp.concatenate([turned, jnp.zeros((HD, rows), F32)]).T
            down_out[...] = turned.astype(BF16)
    for copy in late:
        copy.wait()


def unpack_attention(index, mine, other, query, key, value, output):
    wide = query.shape[1] // 2
    low = lanes((mine.shape[0], 2 * HD)) < HD
    for half in range(2):

        @pl.when(index[3] == half)
        def _():
            first, second = (other, mine) if half else (mine, other)
            for at, part in enumerate((first, second)):
                query[:, at * wide : (at + 1) * wide] = part[:, :wide].astype(F32)
                output[at * wide : (at + 1) * wide, :] = part[:, wide + 2 * HD :].astype(F32).T
            one = first[:, wide : wide + 2 * HD].astype(F32)
            two = second[:, wide : wide + 2 * HD].astype(F32)
            key[...] = jnp.where(low, one, pltpu.roll(two, HD, 1))
            value[...] = jnp.where(low, pltpu.roll(one, HD, 1), two)


def unpack_feed_forward(index, mine, other, gate, upper, down):
    rows, hidden = mine.shape[0], gate.shape[1] // 2
    main = hidden // 128 * 128
    both, wide = 2 * main, 2 * hidden
    low = lanes((rows, 128)) < HD
    for half in range(2):

        @pl.when(index[3] == half)
        def _():
            first, second = (other, mine) if half else (mine, other)
            for at, to in enumerate((gate, upper)):
                to[:, :main] = first[:, at * main : (at + 1) * main].astype(F32)
                one = first[:, both : both + 128].astype(F32)
                two = second[:, both : both + 128].astype(F32)
                if at:
                    one = pltpu.roll(one, HD, 1)
                else:
                    two = pltpu.roll(two, HD, 1)
                end = second[:, at * main : (at + 1) * main].astype(F32)
                end = pltpu.roll(jnp.concatenate([end, jnp.zeros((rows, 128), F32)], 1), HD, 1)
                to[:, main : main + 128] = jnp.where(low, one, end[:, :128])
                to[:, main + 128 : 2 * main] = end[:, 128:main]
                to[:, 2 * main :] = jnp.where(low, end[:, main:], two)
            for at, part in enumerate((first, second)):
                turned = part[:, wide:].astype(F32).T
                down[at * hidden : (at + 1) * hidden, :] = turned[:hidden]


def small_results(index, small, feedforward_gain, attention_gain, query_gain, key_gain, stats):
    for at, to in enumerate((feedforward_gain, attention_gain)):
        line = jnp.concatenate([small[8 * at + row : 8 * at + row + 1, :] for row in range(8)], 1)
        shift = (line.shape[1] - index[2] * to.shape[0]) % line.shape[1]
        to[...] = pltpu.roll(line, shift, 1)[0, : to.shape[0]]
    query_gain[...] = small[16:17, :][0, :HD]
    key_gain[...] = pltpu.roll(small[16:17, :], HD, 1)[0, :HD]
    line = small[17:18, :]
    count = jnp.sum(jnp.where(lanes((1, 128)) == 4, line, 0.0))
    stats[...] = jnp.sqrt(line / (count * index[4].astype(F32)))[0, :4]


def unpack_rows(index, own, from_y, from_core, from_both, rows):
    block = own.shape[0]
    for at, part in enumerate((own, from_y, from_core, from_both)):
        to = pl.multiple_of(((index[0] ^ (2 * (at % 2) + at // 2)) & 3) * block, block)
        rows[pl.ds(to, block), :] = part[...].astype(rows.dtype)


def call(kernel, outs, args, scratch=(), limit=48, fetched=0, cost=0):
    vmem, hbm = pl.BlockSpec(memory_space=pltpu.VMEM), pl.BlockSpec(memory_space=pl.ANY)
    kinds = [
        pl.BlockSpec(memory_space=pltpu.SMEM)
        if arg.dtype == jnp.int32
        else hbm
        if fetched
        else vmem
        for arg in args
    ]
    scratch = [pltpu.VMEM(shape, kind) for shape, kind in scratch]
    if fetched:
        scratch += [pltpu.VMEM(arg.shape, arg.dtype) for arg in args[1 : 1 + fetched]]
        scratch += [pltpu.SemaphoreType.DMA((fetched + 4,))]
    return pl.pallas_call(
        kernel,
        out_shape=[jax.ShapeDtypeStruct(shape, kind) for shape, kind in outs],
        in_specs=kinds,
        out_specs=[vmem] * len(outs),
        scratch_shapes=scratch,
        compiler_params=pltpu.CompilerParams(vmem_limit_bytes=limit * 2**20),
        cost_estimate=pl.CostEstimate(flops=1000 + cost * 10**9, bytes_accessed=1000, transcendentals=0),
    )(*args)


def shards(
    hidden_in,
    lengths,
    positions,
    query_weight,
    key_weight,
    value_weight,
    output_weight,
    gate_weight,
    up_weight,
    down_weight,
    attention_gain,
    feedforward_gain,
    query_gain,
    key_gain,
    cotangent,
):
    ctx, why, core = lax.axis_index("ctx"), lax.axis_index("y"), lax.axis_index("core")
    local, width = hidden_in.shape[1:]
    block = local // 4
    every = 2 * local
    length = lengths[0]

    heads = query_weight.shape[1] // 2 // HD
    groups = key_weight.shape[1] // 2 // HD
    lane = 2 * HD
    wide = (heads + 2 * groups) * HD
    rows = query_weight.shape[0]
    hidden = gate_weight.shape[1] // 2
    main = hidden // 128 * 128
    assert hidden - main == HD and heads * HD == lane and groups == 1
    pack = 2 * hidden + main + lane
    own = ctx * 4 + why * 2 + core
    shard = lax.axis_index("fsdp")
    size = lax.axis_size("fsdp")
    index = jnp.stack([own, length, shard, ctx, jnp.int32(width)]).astype(jnp.int32)
    flag = length > 0

    attn_own, hidden_near, hidden_far = call(
        prelude,
        [((rows + 16, wide + lane), BF16)] + [((local // 2, width), BF16)] * 2,
        (
            index,
            query_weight,
            key_weight,
            value_weight,
            output_weight,
            attention_gain,
            feedforward_gain,
            hidden_in,
        ),
        limit=60,
        fetched=6,
    )
    if near_shards():
        attn_parts = direct([attn_own] * size)
    else:
        attn_parts = lax.all_gather(attn_own, "fsdp")
        gains = attn_parts[:, rows : rows + 8, :rows].astype(F32).transpose(1, 0, 2).reshape(8, -1)
        attn_parts = [attn_parts[:, :rows].reshape(-1, wide + lane), gains]

    def prepare(hidden_near, positions, gate_weight, up_weight, down_weight, cotangent):
        hidden_other = swap(hidden_near, "ctx")
        gu_own, down_own, *cotangent_rel = call(
            pack_feed_forward,
            [((rows, 2 * hidden), BF16), ((rows, main + lane), BF16)] + [((local // 2, width), BF16)] * 2,
            (index, gate_weight, up_weight, down_weight, cotangent),
            limit=60,
            fetched=3,
        )
        pieces = [
            lax.dynamic_slice_in_dim(positions[0], (2 * (why ^ yy) + (core ^ kk)) * block, block)
            for kk in range(2)
            for yy in range(2)
        ]
        places = jnp.concatenate(pieces).reshape(2, -1)
        places = jnp.stack([places, swap(places, "ctx")], 1).reshape(-1)
        freqs = rope_base ** (-2.0 * jnp.arange(HD // 2, dtype=F32) / HD)
        angles = places.astype(F32)[:, None] * jnp.tile(freqs, 4)[None, :]
        cosine = jnp.cos(angles)
        sine = jnp.sin(angles) * jnp.where(jnp.arange(lane) % HD < HD // 2, -1.0, 1.0)[None, :]
        hidden_other, gu_own, cosine, sine = together(hidden_other, gu_own, cosine, sine)
        return hidden_other, gu_own, down_own, cosine, sine, *cotangent_rel

    hidden_other, gu_own, down_own, cosine, sine, cotangent_near, cotangent_far = region(
        flag, prepare, hidden_near, positions, gate_weight, up_weight, down_weight, cotangent
    )
    attn_parts, gu_own, cotangent_near = together(attn_parts, gu_own, cotangent_near)
    gu_full = lax.all_gather(gu_own, "fsdp", axis=0, tiled=True)
    down_parts = [down_own]
    if near_shards():
        down_parts.append(onward(down_own))
    else:
        down_parts = [lax.all_gather(down_own, "fsdp", axis=0, tiled=True)]
    hidden_rel = (hidden_near, hidden_other, hidden_far, swap(hidden_other, "core"))
    cotangent_other = swap(cotangent_near, "ctx")
    query_row = jnp.tile(query_gain.astype(F32), 2)[None]
    key_row = jnp.concatenate([key_gain.astype(F32), jnp.ones((HD,), F32)])[None]

    def attend(hidden_rel, cosine, sine, query_row, key_row, attn_parts):
        attn_full, gains, near, far, unit, query, key, value, raw, mixed, mixed_rel, total = call(
            attention_forward,
            [((width, wide + lane), BF16), ((8, width), F32)]
            + [((every // 2, width), BF16)] * 2
            + [((every, width), BF16)]
            + [((every, lane), BF16)] * 3
            + [((every, 2 * lane), F32), ((every, lane), F32), ((every, lane), BF16), ((every, lane), F32)],
            (index, *hidden_rel, cosine, sine, query_row, key_row, *attn_parts),
            cost=8,
        )
        return near, far, gains, unit, mixed_rel, (attn_full, query, key, value, raw, mixed, total)

    near, far, gains, unit, mixed_rel, kept = region(
        flag, attend, hidden_rel, cosine, sine, query_row, key_row, attn_parts
    )
    kept = kept + (cosine, sine, query_row, key_row)
    near, down_parts = together(near, down_parts)
    if near_shards():
        down_parts.append(onward(down_parts[1]))
    quarter, whole = ((block, width // 2), BF16), ((block, width), F32)

    def add_attention(near, far, hidden_near, gains):
        return call(
            to_middle,
            [whole, ((block, lane), F32), quarter, quarter],
            (*sum_scatter(near, far), hidden_near, gains),
        )

    middle, inverse_two, *spread = region(flag, add_attention, near, far, hidden_near, gains)
    spread, cotangent_other, down_parts = together(spread, cotangent_other, down_parts)
    if near_shards():
        down_parts.append(onward(down_parts[2]))
    *unit_two, cotangent_last = region(flag, gather_plane, *spread, cotangent_other)
    if near_shards():
        unit_two, down_parts = together(unit_two, down_parts)

    cotangent_rel = (cotangent_near, cotangent_other, cotangent_far, cotangent_last)
    down_full, back = call(
        activated_gradient,
        [((width, main + lane), BF16), ((every, main + lane), F32)],
        (index, *cotangent_rel, *down_parts),
    )
    gu_full, back = together(gu_full, back)
    near, far, ff_grad, activated = call(
        feed_forward,
        [((every // 2, width), BF16)] * 2 + [((width, pack), BF16), ((every, main + lane), BF16)],
        (index, *unit_two, *cotangent_rel, back, gu_full),
        [((every, 2 * hidden), BF16)],
    )
    ff_grad, near = together(ff_grad, near)
    ff_share = lax.psum_scatter(ff_grad, "fsdp", scatter_dimension=0, tiled=True)

    def turn(near, far, middle, inverse_two, cotangent_near, gains, activated, down_full, unit, mixed_rel, kept):
        terms, branch_parts = together(
            scatter_start(near, swap(far, "core")),
            call(down_product, [((every // 2, width), BF16)] * 2, (index, activated, down_full)),
        )
        branch_far = swap(branch_parts[1], "core")
        second, middle_grad, left, right = call(
            to_middle_grad,
            [whole, whole, quarter, quarter],
            (index, *scatter_next(*terms), middle, inverse_two, cotangent_near, gains),
        )
        attention_grad = gather_end(left, swap(left, "ctx"), right, swap(right, "y"))
        attention_grad, branch_far = together(attention_grad, branch_far)
        branch = scatter_start(branch_parts[0], branch_far)
        near, far, back, head_sums = call(
            attention_backward,
            [((every // 2, width), BF16)] * 2 + [((every, 2 * lane), BF16), ((8, lane), F32)],
            (index, *attention_grad, *kept),
            [((every, lane), BF16)] + [((every, lane), F32)] * 3,
        )
        back, branch = together(back, branch)
        rows_of_branch = scatter_halves(*branch)
        back, rows_of_branch = together(back, rows_of_branch)
        branch = scatter_swap(*rows_of_branch)
        attn_grad, attention_sums = call(
            attention_weights,
            [((width, wide + lane), BF16), ((8, width), F32)],
            (index, unit, back, *attention_grad, mixed_rel, kept[0], gains),
        )
        attn_grad, branch = together(attn_grad, branch)
        return near, far, attn_grad, attention_sums, head_sums, branch, second, middle_grad

    near, far, attn_grad, attention_sums, head_sums, branch, second, middle_grad = region(
        flag,
        turn,
        near,
        far,
        middle,
        inverse_two,
        cotangent_near,
        gains,
        activated,
        down_full,
        unit,
        mixed_rel,
        kept,
    )
    attn_share = lax.psum_scatter(attn_grad, "fsdp", scatter_dimension=0, tiled=True)

    def sum_first(near, far, branch, middle, hidden_near, second, inverse, attention_sums, head_sums):
        terms = scatter_start(near, swap(far, "core"))
        branch, output = call(to_output, [whole, ((block, width), BF16)], (index, *branch, middle))
        (small,) = call(
            small_sums,
            [((24, lane), F32)],
            (index, hidden_near, middle, branch, second, inverse, attention_sums, head_sums),
        )
        small = small + hop(small, "core")
        terms, small = together(terms, small)
        terms, more = together(scatter_next(*terms), hop(small, "ctx"))
        return terms, small + more, output

    pieces, small, output = region(
        flag,
        sum_first,
        near,
        far,
        branch,
        middle,
        hidden_near,
        second,
        inverse_two,
        attention_sums,
        head_sums,
    )
    pieces, ff_share = together(pieces, ff_share)
    ff_other = swap(ff_share, "ctx")

    def finish(pieces, middle_grad, hidden_near, gains, output, small):
        (own_rows,) = call(
            to_input_grad, [((block, width), BF16)], (*pieces, middle_grad, hidden_near, gains)
        )
        own_rows, small = together(own_rows, small + hop(small, "y"))
        rows_y, rows_core = swap(own_rows, "y"), swap(own_rows, "core")
        output_y = swap(output, "y")
        step = 1
        while step < size:
            small = small + hop(small, "fsdp", step)
            step *= 2
        rows_y, rows_core, output_y, small = together(rows_y, rows_core, output_y, small)
        results = call(
            small_results, [((rows,), F32)] * 2 + [((HD,), F32)] * 2 + [((4,), F32)], (index, small)
        )
        last, results = together(swap(rows_y, "core"), results)
        (input_rows,) = call(unpack_rows, [((local, width), F32)], (index, own_rows, rows_y, rows_core, last))
        return input_rows, output_y, results

    input_rows, output_y, results = region(flag, finish, pieces, middle_grad, hidden_near, gains, output, small)
    output_y, attn_share, ff_other = together(output_y, attn_share, ff_other)
    attn_other = swap(attn_share, "ctx")

    def unpack(index, output, output_y, ff_share, ff_other):
        output_core, last = swap(output, "core"), swap(output_y, "core")
        ff_grads = call(
            unpack_feed_forward,
            [((rows, 2 * hidden), F32)] * 2 + [((2 * hidden, rows), F32)],
            (index, ff_share, ff_other),
        )
        output_core, last, ff_grads = together(output_core, last, ff_grads)
        (block_rows,) = call(
            unpack_rows, [((local, width), BF16)], (index, output, output_y, output_core, last)
        )
        return block_rows, ff_grads

    block_rows, ff_grads = region(flag, unpack, index, output, output_y, ff_share, ff_other)
    attn_other, block_rows = together(attn_other, block_rows)
    attn_grads = call(
        unpack_attention,
        [((rows, 2 * lane), F32)] + [((rows, lane), F32)] * 2 + [((2 * lane, rows), F32)],
        (index, attn_share, attn_other),
    )
    grads = (*attn_grads, *ff_grads)
    feedforward_share, attention_share, query_share, key_share, stats = results
    return (
        block_rows[None],
        input_rows[None],
        *grads,
        attention_share,
        feedforward_share,
        query_share,
        key_share,
        stats,
    )


def solution(mesh):
    fsdp, ctx, tp = (mesh.shape[axis] for axis in ("fsdp", "ctx", "tp"))
    assert ctx == 2 and tp == 4
    plane = Mesh(mesh.devices.reshape(fsdp, 2, 2, 2), ("fsdp", "ctx", "y", "core"))
    tp = ("y", "core")
    in_specs = (
        P("fsdp", "ctx", None),
        P("fsdp"),
        P("fsdp", "ctx"),
        P("fsdp", tp),
        P("fsdp", tp),
        P("fsdp", tp),
        P(tp, "fsdp"),
        P("fsdp", tp),
        P("fsdp", tp),
        P(tp, "fsdp"),
        P("fsdp"),
        P("fsdp"),
        P(),
        P(),
        P("fsdp", "ctx", None),
    )
    out_specs = (
        P("fsdp", "ctx", None),
        P("fsdp", "ctx", None),
        P("fsdp", tp),
        P("fsdp", tp),
        P("fsdp", tp),
        P(tp, "fsdp"),
        P("fsdp", tp),
        P("fsdp", tp),
        P(tp, "fsdp"),
        P("fsdp"),
        P("fsdp"),
        P(),
        P(),
        P(),
    )
    return jax.shard_map(shards, mesh=plane, in_specs=in_specs, out_specs=out_specs, check_vma=False)
```
